32 devices in a mesh: lon: 8 (over z, y), lat: 4 (over x, core).
Axes of the slice: x: 2, y: 2, z: 4, core: 2. Of those that a mesh axis runs over, the one named last changes fastest.
Arguments:
- tokens: bfloat16 [2, 48, 192, 192], P(None, 'lat', 'lon'), may hold values from -6 to 6
- mask_ids: int32 [2, 48, 192], P(None, 'lat', 'lon'), may hold values from 0 to 1
- fine_qkv: bfloat16 [192, 576], replicated, may hold values from -0.4375 to 0.4375
- fine_proj: bfloat16 [192, 192], replicated, may hold values from -0.4375 to 0.4375
- fine_up: bfloat16 [192, 768], replicated, may hold values from -0.4375 to 0.4375
- fine_down: bfloat16 [768, 192], replicated, may hold values from -0.21875 to 0.21875
- fine_bias: float32 [8, 6, 3312], P('lat'), may hold values from -10 to 260
- reduce_weight: bfloat16 [768, 384], replicated, may hold values from -0.21875 to 0.21875
- coarse_qkv: bfloat16 [384, 1152], replicated, may hold values from -0.3125 to 0.3125
- coarse_proj: bfloat16 [384, 384], replicated, may hold values from -0.3125 to 0.3125
- coarse_up: bfloat16 [384, 1536], replicated, may hold values from -0.3125 to 0.3125
- coarse_down: bfloat16 [1536, 384], replicated, may hold values from -0.15625 to 0.15625
- coarse_bias: float32 [4, 12, 3312], P('lat'), may hold values from -10 to 260
- out_grad: bfloat16 [2, 24, 96, 384], P(None, 'lat', 'lon'), may hold values from -6 to 6
Outputs:
- coarse_result: bfloat16 [2, 24, 96, 384], P(None, 'lat', 'lon')
- d_tokens: bfloat16 [2, 48, 192, 192], P(None, 'lat', 'lon')
- fine_bias_grad: float32 [8, 6, 3312], P('lat')
- coarse_bias_grad: float32 [4, 12, 3312], P('lat')
The draws below stay inside these ranges and needn't reach their ends.
All inputs are finite; a program needn't handle non-finite values.
Results may differ from the reference program's by a relative error of at most 0.024.
Values may be sent and summed in bfloat16 or wider, within the bound.
No kernel may reach another device: no remote copies, remote signals or barrier semaphores. Data moves between devices by JAX's collectives and lax.ppermute only.
A program may use at most 128 MiB of HBM per device.

```python
import jax
import jax.numpy as jnp
from jax import lax

D = 192
HEADS_F = 6
FF = 768
D2 = 384
HEADS_C = 12
FF2 = 1536
ZL = 2
WLAT = 6
WLON = 12
NLAT = 48
NLON = 192
WT = 144


def table_values(key, table_shape):
    noise_part = jnp.clip(jax.random.normal(jax.random.fold_in(key, 1), table_shape, jnp.float32), -9.0, 9.0)
    whole = noise_part
    return whole.reshape(table_shape[0], table_shape[1], table_shape[2] * table_shape[3])


def draw_fine_bias(key, part):
    key = jax.random.fold_in(key, 11)
    table_shape = (NLAT // WLAT, HEADS_F, ZL * WLAT, ZL * WLAT * (2 * WLON - 1))
    return table_values(key, table_shape)


def draw_coarse_bias(key, part):
    key = jax.random.fold_in(key, 12)
    table_shape = (NLAT // (2 * WLAT), HEADS_C, ZL * WLAT, ZL * WLAT * (2 * WLON - 1))
    return table_values(key, table_shape)


def touch_ends(drawn, own_key, smallest, top_value):
    extent = drawn.shape
    index_at = [jax.random.randint(jax.random.fold_in(own_key, axis), (), 0, extent[axis]) for axis in range(len(extent))]
    drawn = drawn.at[tuple(index_at)].set(smallest)
    longest = extent.index(max(extent))
    index_at[longest] = (index_at[longest] + 1) % extent[longest]
    return drawn.at[tuple(index_at)].set(top_value)


def level_of(rng, extent, cuts, least, high):
    loudness = 1.0
    for position, blocks in cuts:
        heights = jax.random.uniform(jax.random.fold_in(jax.random.fold_in(rng, 6), position), (blocks,), jnp.float32, least / len(cuts), high / len(cuts))
        loudness = loudness * jnp.repeat(jnp.exp(heights), extent[position] // blocks).reshape((-1,) + (1,) * (len(extent) - 1 - position))
    return loudness


def noise(rng, extent, width, reach, cuts=(), kind=jnp.bfloat16):
    gain = level_of(rng, extent, cuts, -0.22, 0.18) if cuts else 1.0
    values = jax.random.normal(rng, extent, jnp.float32) * width * gain
    return jnp.minimum(jnp.maximum(values, -reach), reach).astype(kind)


def setup_inputs(seed: int = 0) -> dict:
    splits = jax.random.split(jax.random.key(seed), 15)
    tokens = noise(splits[0], (ZL, NLAT, NLON, D), 1.0, 6.0, ((1, 4), (2, 8)))
    mask_ids = touch_ends(jax.random.randint(splits[1], (ZL, NLAT, NLON), 0, 2), jax.random.fold_in(splits[1], 1), 0, 1).astype(jnp.int32)
    fine_qkv = noise(splits[2], (D, 3 * D), D ** -0.5, 0.4375)
    fine_proj = noise(splits[3], (D, D), D ** -0.5, 0.4375)
    fine_up = noise(splits[4], (D, FF), D ** -0.5, 0.4375)
    fine_down = noise(splits[5], (FF, D), FF ** -0.5, 0.21875)
    fine_bias = draw_fine_bias(jax.random.fold_in(splits[14], 71), 0)
    reduce_weight = noise(splits[7], (4 * D, D2), (4 * D) ** -0.5, 0.21875)
    coarse_qkv = noise(splits[8], (D2, 3 * D2), D2 ** -0.5, 0.3125)
    coarse_proj = noise(splits[9], (D2, D2), D2 ** -0.5, 0.3125)
    coarse_up = noise(splits[10], (D2, FF2), D2 ** -0.5, 0.3125)
    coarse_down = noise(splits[11], (FF2, D2), FF2 ** -0.5, 0.15625)
    coarse_bias = draw_coarse_bias(jax.random.fold_in(splits[14], 71), 0)
    out_grad = noise(splits[13], (ZL, NLAT // 2, NLON // 2, D2), 1.0, 6.0, ((1, 4), (2, 8)))
    return dict(tokens=tokens, mask_ids=mask_ids, fine_qkv=fine_qkv, fine_proj=fine_proj, fine_up=fine_up, fine_down=fine_down, fine_bias=fine_bias, reduce_weight=reduce_weight, coarse_qkv=coarse_qkv, coarse_proj=coarse_proj, coarse_up=coarse_up, coarse_down=coarse_down, coarse_bias=coarse_bias, out_grad=out_grad)


norm_eps = 1e-05
masked_score = -1e+30

def layer_norm(values):
    average = lax.optimization_barrier(jnp.mean(values, axis=-1, keepdims=True))
    centred = values - average
    variance = lax.optimization_barrier(jnp.mean(centred * centred, axis=-1, keepdims=True))
    return centred * lax.rsqrt(variance + norm_eps)

def to_windows(values):
    levels, lat_rows, lon_cols, channels = values.shape
    pieces = values.reshape(levels, lat_rows // WLAT, WLAT, lon_cols // WLON, WLON, channels)
    return pieces.transpose(1, 3, 0, 2, 4, 5).reshape(lat_rows // WLAT, lon_cols // WLON, levels * WLAT * WLON, channels)

def from_windows(blocks, levels):
    band_count, across, window_len, channels = blocks.shape
    pieces = blocks.reshape(band_count, across, levels, WLAT, WLON, channels)
    return pieces.transpose(2, 0, 3, 1, 4, 5).reshape(levels, band_count * WLAT, across * WLON, channels)

def allowed_mask(labels, row_start):
    row_index = lax.broadcasted_iota(jnp.int32, labels.shape, 1) + row_start
    pole_side = jnp.where(row_index < WLAT // 2, 1, 0).astype(jnp.int32)
    marked = (labels * 2 + pole_side)[..., None]
    windowed = to_windows(marked)[..., 0]
    return windowed[..., :, None] == windowed[..., None, :]

def expand_bias(table):
    band_count, head_count, entries = table.shape
    span = 2 * WLON - 1
    grid = table.reshape(band_count, head_count, ZL, WLAT, ZL, WLAT, span)
    offset = lax.broadcasted_iota(jnp.int32, (span, WLON, WLON), 1) - lax.broadcasted_iota(jnp.int32, (span, WLON, WLON), 2) + (WLON - 1)
    picker = jnp.where(offset == lax.broadcasted_iota(jnp.int32, (span, WLON, WLON), 0), 1.0, 0.0).astype(jnp.float32)
    full = jnp.einsum('bhaicjr,rxy->bhaixcjy', grid, picker, precision=lax.Precision.HIGHEST)
    return full.reshape(band_count, head_count, WT, WT)

def band_attention(packed, head_count):
    triple, bias_band, allowed_band = packed
    across = triple.shape[0]
    window_len = triple.shape[1]
    channels = triple.shape[2] // 3
    head_size = channels // head_count
    parts = triple.astype(jnp.float32).reshape(across, window_len, 3, head_count, head_size)
    queries = parts[:, :, 0]
    key_part = parts[:, :, 1]
    value_part = parts[:, :, 2]
    scores = jnp.einsum('aqhd,akhd->ahqk', queries, key_part) * head_size ** (-0.5) + bias_band[None]
    scores = jnp.where(allowed_band[:, None], scores, masked_score)
    highest = lax.optimization_barrier(jnp.max(scores, axis=-1, keepdims=True))
    raised = jnp.exp(scores - highest)
    probs = (raised / lax.optimization_barrier(jnp.sum(raised, axis=-1, keepdims=True))).astype(jnp.bfloat16)
    mixture = jnp.einsum('ahqk,akhd->aqhd', probs.astype(jnp.float32), value_part)
    return mixture.astype(jnp.bfloat16).reshape(across, window_len, channels)

def earth_block(base, w_qkv, w_proj, w_up, w_down, bias_flat, allowed, head_count):
    levels, lat_rows, lon_cols, channels = base.shape
    bias_table = expand_bias(bias_flat)
    widened = base.astype(jnp.float32).reshape(-1, channels)
    normed = layer_norm(widened).astype(jnp.bfloat16)
    triple = jnp.dot(normed, w_qkv, preferred_element_type=jnp.float32).astype(jnp.bfloat16)
    blocks = to_windows(triple.reshape(levels, lat_rows, lon_cols, 3 * channels))
    mixture = lax.map(lambda packed: band_attention(packed, head_count), (blocks, bias_table, allowed))
    gathered = from_windows(mixture, levels).reshape(-1, channels)
    first = widened + jnp.dot(gathered, w_proj, preferred_element_type=jnp.float32)
    renormed = layer_norm(first).astype(jnp.bfloat16)
    inner = jnp.dot(renormed, w_up, preferred_element_type=jnp.float32)
    active = jax.nn.gelu(inner, approximate=False).astype(jnp.bfloat16)
    result = first + jnp.dot(active, w_down, preferred_element_type=jnp.float32)
    return result.astype(jnp.bfloat16).reshape(base.shape)

def merge_cells(values, reduce_weight):
    levels, lat_rows, lon_cols, channels = values.shape
    pieces = values.reshape(levels, lat_rows // 2, 2, lon_cols // 2, 2, channels)
    joined = pieces.transpose(0, 1, 3, 4, 2, 5).reshape(-1, 4 * channels)
    normed = layer_norm(joined.astype(jnp.float32)).astype(jnp.bfloat16)
    reduced = jnp.dot(normed, reduce_weight, preferred_element_type=jnp.float32).astype(jnp.bfloat16)
    return reduced.reshape(levels, lat_rows // 2, lon_cols // 2, reduce_weight.shape[1])

def reference(tokens, mask_ids, fine_qkv, fine_proj, fine_up, fine_down, fine_bias, reduce_weight, coarse_qkv, coarse_proj, coarse_up, coarse_down, coarse_bias, out_grad):
    levels, lat_rows, lon_cols, channels = tokens.shape
    fine_allowed = allowed_mask(mask_ids, 0)
    coarse_labels = jnp.zeros((levels, lat_rows // 2, lon_cols // 2), jnp.int32)
    coarse_allowed = allowed_mask(coarse_labels, 0)
    lat_shift = WLAT // 2
    lon_shift = WLON // 2

    def forward(values, fine_table, coarse_table):
        rolled = jnp.roll(values, (lat_shift, lon_shift), axis=(1, 2))
        fine_result = earth_block(rolled, fine_qkv, fine_proj, fine_up, fine_down, fine_table, fine_allowed, HEADS_F)
        twice = jnp.roll(fine_result, (lat_shift, lon_shift), axis=(1, 2))
        coarse_in = merge_cells(twice, reduce_weight)
        coarse_block = earth_block(coarse_in, coarse_qkv, coarse_proj, coarse_up, coarse_down, coarse_table, coarse_allowed, HEADS_C)
        return jnp.roll(coarse_block, (-lat_shift, -lon_shift), axis=(1, 2))
    coarse_result, backward = jax.vjp(forward, tokens, fine_bias, coarse_bias)
    d_tokens, fine_bias_grad, coarse_bias_grad = backward(out_grad)
    return (coarse_result, d_tokens, fine_bias_grad, coarse_bias_grad)
```

```python
import math

import jax
import jax.numpy as jnp
import numpy as np
from jax import lax
from jax.experimental import pallas as pl
from jax.experimental.pallas import tpu as pltpu
from jax.sharding import PartitionSpec as P

HEADS_F = 6
HEADS_C = 12
HEAD = 32
WIN = 144
QUAD = 36
SPAN = 23
ENTRIES = 276
LOG2E = math.log2(math.e)
VMEM = 32 * 1024 * 1024
f32 = jnp.float32
bf16 = jnp.bfloat16


def spot(z, i, j):
    quadrant = (i % 6) // 3 * 2 + (j % 12) // 6
    return quadrant * QUAD + z * 18 + i % 3 * 6 + j % 6


def fine_spot(z, i, j):
    return (i // 6 * 2 + j // 12) * WIN + spot(z, i, j)


def in_quad(z, i, j):
    return z * 18 + i % 3 * 6 + j % 6


def index_maps():
    arrive = np.zeros(576, np.int32)
    merge = np.zeros(576, np.int32)
    split = np.full(608, -1, np.int32)
    back = np.zeros(576, np.int32)
    leave = np.zeros(576, np.int32)
    for z in range(2):
        for i in range(12):
            for j in range(24):
                here = fine_spot(z, i, j)
                if i >= 3 and j >= 6:
                    arrive[here] = z * 288 + (i - 3) * 24 + j - 6
                    came = fine_spot(z, i - 3, j - 6)
                elif i >= 3:
                    arrive[here] = 576 + z * 72 + (i - 3) * 8 + 2 + j
                    came = 576 + (i - 3) // 3 * QUAD + in_quad(z, i, j)
                elif j >= 6:
                    arrive[here] = 720 + z * 72 + i * 24 + j - 6
                    came = 688 + (j - 6) // 6 * QUAD + in_quad(z, i, j)
                else:
                    arrive[here] = 864 + z * 24 + i * 8 + 2 + j
                    came = 800 + in_quad(z, i, j)
                part = (i % 2 + j % 2 * 2) * WIN + spot(z, i // 2, j // 2)
                merge[part] = came
                if i >= 3 and j >= 6:
                    slot = 272 + z * 162 + (i - 3) * 18 + j - 6
                    back[fine_spot(z, i - 3, j - 6)] = slot
                elif i >= 3:
                    slot = z * 54 + (i - 3) * 6 + j
                    back[fine_spot(z, i - 3, j + 18)] = slot
                elif j >= 6:
                    slot = 112 + z * 54 + i * 18 + j - 6
                    back[fine_spot(z, i + 9, j - 6)] = slot
                else:
                    slot = 224 + z * 18 + i * 6 + j
                    back[fine_spot(z, i + 9, j + 18)] = slot
                split[slot] = part
                natural = z * 288 + i * 24 + j
                if i < 9 and j < 18:
                    leave[natural] = fine_spot(z, i + 3, j + 6)
                elif i < 9:
                    leave[natural] = 576 + i // 3 * QUAD + in_quad(z, i, j)
                elif j < 18:
                    leave[natural] = 688 + j // 6 * QUAD + in_quad(z, i, j)
                else:
                    leave[natural] = 800 + in_quad(z, i, j)
    result = np.zeros(WIN, np.int32)
    base = np.zeros(WIN, np.int32)
    row_slot = np.zeros(WIN, np.int32)
    for z in range(2):
        for i in range(6):
            for j in range(12):
                result[z * 72 + i * 12 + j] = (i // 3 * 2 + j // 6) * 48 + in_quad(z, i, j)
                here = spot(z, i, j)
                base[here] = (z * 6 + i) * SPAN + 11 - j
                row_slot[here] = j * 16 + z * 6 + i
    return arrive, merge, split, back, leave, result, base, row_slot


ARRIVE, MERGE, SPLIT, BACK, LEAVE, RESULT, BASE, ROW_SLOT = index_maps()


def one_hot(column, width):
    spots = lax.broadcasted_iota(jnp.int32, (column.shape[0], width), 1)
    return jnp.where(spots == column, 1.0, 0.0).astype(bf16)


def mm(left, right):
    return jnp.dot(left, right, preferred_element_type=f32)


def mm_nt(left, right):
    return lax.dot_general(left, right, (((1,), (1,)), ((), ())), preferred_element_type=f32)


def mm_tn(left, right):
    return lax.dot_general(left, right, (((0,), (0,)), ((), ())), preferred_element_type=f32)


def norm(values):
    centred = values - jnp.mean(values, axis=-1, keepdims=True)
    scale = lax.rsqrt(jnp.mean(centred * centred, axis=-1, keepdims=True) + 1e-5)
    return centred * scale, scale


def norm_back(grad, normed, scale):
    along = jnp.mean(grad * normed, axis=-1, keepdims=True)
    return (grad - jnp.mean(grad, axis=-1, keepdims=True) - normed * along) * scale


def gelu_pair(x):
    u = jnp.abs(x) * math.sqrt(0.5)
    t = 1.0 / (1.0 + 0.3275911 * u)
    e = jnp.exp(-u * u)
    poly = 1.421413741 + t * (-1.453152027 + t * 1.061405429)
    tail = 0.5 * (t * (0.254829592 + t * (-0.284496736 + t * poly))) * e
    below = jnp.where(x >= 0, 1.0 - tail, tail)
    return x * below, below + x * (e * (1.0 / math.sqrt(2 * math.pi)))


def groups(channels):
    return [(start, min(start + 128, channels)) for start in range(0, channels, 128)]


def head_lanes(rows, width):
    return lax.broadcasted_iota(jnp.int32, (rows, width), 1) // HEAD


def stack_heads(part):
    lanes = head_lanes(part.shape[0], part.shape[1])
    count = part.shape[1] // HEAD
    zero = jnp.zeros_like(part)
    return jnp.concatenate([jnp.where(lanes == h, part, zero) for h in range(count)], axis=0)


def pick_heads(stacked):
    width = stacked.shape[1]
    lanes = head_lanes(WIN, width)
    total = stacked[:WIN]
    for h in range(1, width // HEAD):
        total = jnp.where(lanes == h, stacked[h * WIN : (h + 1) * WIN], total)
    return total


def attend(queries, keys, values, bias_ref, bias_row, mask, probs_ref, probs_row):
    mixed = []
    for start, stop in groups(queries.shape[1]):
        count = (stop - start) // HEAD
        scores = mm_nt(stack_heads(queries[:, start:stop]), keys[:, start:stop])
        row = start // HEAD * WIN
        for h in range(count):
            here = row + h * WIN
            logits = (
                scores[h * WIN : (h + 1) * WIN] * (HEAD**-0.5 * LOG2E)
                + bias_ref[pl.ds(bias_row + here, WIN), :]
                + mask
            )
            raised = jnp.exp2(logits - jnp.max(logits, axis=-1, keepdims=True))
            probs = raised * (1.0 / jnp.sum(raised, axis=-1, keepdims=True))
            probs_ref[pl.ds(probs_row + here, WIN), :] = probs.astype(bf16)
        stacked = mm(probs_ref[pl.ds(probs_row + row, count * WIN), :], values[:, start:stop])
        mixed.append(pick_heads(stacked))
    return jnp.concatenate(mixed, axis=1)


def attend_back(queries, keys, values, mix_grad, probs_ref, probs_row, score_ref, add):
    query_grad, key_grad, value_grad = [], [], []
    for start, stop in groups(queries.shape[1]):
        count = (stop - start) // HEAD
        row = start // HEAD * WIN
        probs_all = probs_ref[pl.ds(probs_row + row, count * WIN), :]
        grads = stack_heads(mix_grad[:, start:stop])
        value_grad.append(mm_tn(probs_all, grads))
        probs_grad = mm_nt(grads, values[:, start:stop])
        pieces = []
        for h in range(count):
            probs = probs_all[h * WIN : (h + 1) * WIN].astype(f32)
            grad = probs_grad[h * WIN : (h + 1) * WIN]
            weighted = grad * probs
            score_grad = weighted - probs * jnp.sum(weighted, axis=-1, keepdims=True)
            place = pl.ds(row + h * WIN, WIN)
            if add:
                score_ref[place, :] += score_grad
            else:
                score_ref[place, :] = score_grad
            pieces.append(score_grad.astype(bf16))
        score_all = jnp.concatenate(pieces, axis=0)
        query_grad.append(pick_heads(mm(score_all, keys[:, start:stop])))
        key_grad.append(mm_tn(score_all, stack_heads(queries[:, start:stop])))
    scale = HEAD**-0.5
    return (
        jnp.concatenate(query_grad, axis=1) * scale,
        jnp.concatenate(key_grad, axis=1) * scale,
        jnp.concatenate(value_grad, axis=1),
    )


def table_grad(score_ref, base_ref, slot_ref, rows_ref):
    regroup = jnp.where(
        lax.broadcasted_iota(jnp.int32, (192, WIN), 0) == slot_ref[...], 1.0, 0.0
    ).astype(bf16)
    for h in range(12):
        moved = mm(regroup, score_ref[pl.ds(h * WIN, WIN), :].astype(bf16)).astype(bf16)
        rows_ref[:, pl.ds(h * 16, 16), :] = moved.reshape(12, 16, WIN)
    total = jnp.zeros((192, ENTRIES), f32)
    for column in range(12):
        total += mm(rows_ref[column], one_hot(base_ref[...] + column, ENTRIES))
    return total


def pack(pieces, rows):
    count = sum(piece.shape[0] for piece in pieces)
    if rows > count:
        pieces = pieces + [jnp.zeros((rows - count, pieces[0].shape[1]), f32)]
    return jnp.concatenate(pieces, axis=0).astype(bf16)


def quadrant(windows, qi, qj):
    part = (qi % 2 * 2 + qj % 2) * QUAD
    return windows[qi // 2 * 2 + qj // 2][part : part + QUAD]


def bias_kernel(table_ref, base_ref, slot_ref, grad_ref, fine_ref, coarse_ref, g0, g1, g2, g3, held):
    table = table_ref[...]
    high = table.astype(bf16)
    low = (table - high.astype(f32)).astype(bf16)
    entry = lax.broadcasted_iota(jnp.int32, (ENTRIES, WIN), 0)
    for column in range(12):
        picker = jnp.where(entry == base_ref[...] + column, 1.0, 0.0).astype(bf16)
        held[:, 0, column] = mm(high, picker).astype(bf16).reshape(24, 16, WIN)
        held[:, 1, column] = mm(low, picker).astype(bf16).reshape(24, 16, WIN)
    once = one_hot(slot_ref[...], 192)
    for h in range(24):
        place = pl.ds(h % 12 * WIN, WIN)
        target = fine_ref if h < 12 else coarse_ref
        target[place, :] = (
            mm(once, held[h, 0].reshape(192, WIN)) + mm(once, held[h, 1].reshape(192, WIN))
        ) * LOG2E
    for index, out in enumerate((g0, g1, g2, g3)):
        hi, hj = index // 2, index % 2
        pieces = [
            grad_ref[z, hi * 3 + row].astype(f32)[hj * 6 : hj * 6 + 6]
            for z in range(2)
            for row in range(3)
        ]
        out[...] = pack(pieces, 48)


def fine_kernel(
    tokens_ref, lon_ref, lat_ref, diag_ref, arrive_ref, bias_ref, mask_ref,
    qkv_ref, proj_ref, up_ref, down_ref,
    res_ref, slon_ref, slat_ref, sdiag_ref,
    q_ref, k_ref, v_ref, probs_ref, n1_ref, r1_ref, n2_ref, r2_ref, slope_ref,
    source,
):
    source[0:576] = tokens_ref[...]
    source[576:720] = lon_ref[...]
    source[720:864] = lat_ref[...]
    source[864:912] = diag_ref[...]
    everything = source[...]
    w_qkv = qkv_ref[...]
    bases = []
    for w in range(4):
        rows = pl.ds(w * WIN, WIN)
        base = mm(one_hot(arrive_ref[rows, :], 912), everything)
        normed, scale = norm(base)
        normed = normed.astype(bf16)
        n1_ref[rows, :] = normed
        r1_ref[rows, :] = scale
        q_ref[rows, :] = mm(normed, w_qkv[:, 0:192]).astype(bf16)
        k_ref[rows, :] = mm(normed, w_qkv[:, 192:384]).astype(bf16)
        v_ref[rows, :] = mm(normed, w_qkv[:, 384:576]).astype(bf16)
        bases.append(base)
    windows = []
    for w in range(4):
        rows = pl.ds(w * WIN, WIN)
        mixture = attend(
            q_ref[rows, :], k_ref[rows, :], v_ref[rows, :],
            bias_ref, w // 2 * 6 * WIN, mask_ref[w], probs_ref, w * 6 * WIN,
        ).astype(bf16)
        first = bases[w] + mm(mixture, proj_ref[...])
        renormed, scale = norm(first)
        renormed = renormed.astype(bf16)
        n2_ref[rows, :] = renormed
        r2_ref[rows, :] = scale
        active, slope = gelu_pair(mm(renormed, up_ref[...]))
        slope_ref[rows, :] = slope.astype(bf16)
        result = first + mm(active.astype(bf16), down_ref[...])
        res_ref[rows, :] = result.astype(bf16)
        windows.append(result)
    slon_ref[...] = pack([quadrant(windows, q, 3) for q in range(3)], 112)
    slat_ref[...] = pack([quadrant(windows, 3, q) for q in range(3)], 112)
    sdiag_ref[...] = pack([quadrant(windows, 3, 3)], 48)


def coarse_kernel(
    res_ref, lon_ref, lat_ref, diag_ref, merge_ref, split_ref, bias_ref, mask_ref,
    gloc_ref, glon_ref, glat_ref, gdiag_ref,
    reduce_ref, qkv_ref, proj_ref, up_ref, down_ref, base_ref, slot_ref,
    c0, c1, c2, c3, dlon_ref, dlat_ref, ddiag_ref, dloc_ref, table_ref,
    source, probs_ref, score_ref, rows_ref, parts_ref,
):
    source[0:576] = res_ref[...]
    source[576:688] = lon_ref[...]
    source[688:800] = lat_ref[...]
    source[800:848] = diag_ref[...]
    everything = source[...]
    parts = [mm(one_hot(merge_ref[pl.ds(k * WIN, WIN), :], 848), everything) for k in range(4)]
    mean = sum(jnp.sum(part, axis=-1, keepdims=True) for part in parts) * (1.0 / 768)
    parts = [part - mean for part in parts]
    square = sum(jnp.sum(part * part, axis=-1, keepdims=True) for part in parts)
    merge_scale = lax.rsqrt(square * (1.0 / 768) + 1e-5)
    parts = [(part * merge_scale).astype(bf16) for part in parts]
    base = sum(mm(parts[k], reduce_ref[k * 192 : (k + 1) * 192]) for k in range(4))
    base = base.astype(bf16).astype(f32)
    normed, scale1 = norm(base)
    normed = normed.astype(bf16)
    queries = mm(normed, qkv_ref[:, 0:384]).astype(bf16)
    keys = mm(normed, qkv_ref[:, 384:768]).astype(bf16)
    values = mm(normed, qkv_ref[:, 768:1152]).astype(bf16)
    mixture = attend(queries, keys, values, bias_ref, 0, mask_ref[...], probs_ref, 0).astype(bf16)
    first = base + mm(mixture, proj_ref[...])
    renormed, scale2 = norm(first)
    renormed = renormed.astype(bf16)
    active, slope = gelu_pair(mm(renormed, up_ref[...]))
    result = first + mm(active.astype(bf16), down_ref[...])
    for index, out in enumerate((c0, c1, c2, c3)):
        out[...] = pack([result[index * QUAD : (index + 1) * QUAD]], 48)

    grad = jnp.concatenate(
        [ref[...].astype(f32)[:QUAD] for ref in (gdiag_ref, glat_ref, glon_ref, gloc_ref)], axis=0
    )
    inner = mm_nt(grad.astype(bf16), down_ref[...]) * slope
    grad = grad + norm_back(mm_nt(inner.astype(bf16), up_ref[...]), renormed.astype(f32), scale2)
    mix_grad = mm_nt(grad.astype(bf16), proj_ref[...]).astype(bf16)
    dq, dk, dv = attend_back(queries, keys, values, mix_grad, probs_ref, 0, score_ref, False)
    normed_grad = (
        mm_nt(dq.astype(bf16), qkv_ref[:, 0:384])
        + mm_nt(dk.astype(bf16), qkv_ref[:, 384:768])
        + mm_nt(dv.astype(bf16), qkv_ref[:, 768:1152])
    )
    grad = grad + norm_back(normed_grad, normed.astype(f32), scale1)
    grad = grad.astype(bf16)
    grads = [mm_nt(grad, reduce_ref[k * 192 : (k + 1) * 192]) for k in range(4)]
    mean = sum(jnp.sum(g, axis=-1, keepdims=True) for g in grads) * (1.0 / 768)
    along = sum(
        jnp.sum(g * p.astype(f32), axis=-1, keepdims=True) for g, p in zip(grads, parts)
    ) * (1.0 / 768)
    for k in range(4):
        part = (grads[k] - mean - parts[k].astype(f32) * along) * merge_scale
        parts_ref[pl.ds(k * WIN, WIN), :] = part.astype(bf16)
    everything = parts_ref[...]
    moved = mm(one_hot(split_ref[...], 576), everything).astype(bf16)
    dlon_ref[...] = moved[0:112]
    dlat_ref[...] = moved[112:224]
    ddiag_ref[...] = moved[224:272]
    dloc_ref[...] = moved[272:608]
    table_ref[...] = table_grad(score_ref, base_ref, slot_ref, rows_ref).astype(bf16)


def fine_back_kernel(
    dlon_ref, dlat_ref, ddiag_ref, dloc_ref, back_ref,
    q_ref, k_ref, v_ref, probs_ref, n1_ref, r1_ref, n2_ref, r2_ref, slope_ref,
    qkv_ref, proj_ref, up_ref, down_ref, base_ref, slot_ref,
    res_ref, slon_ref, slat_ref, sdiag_ref, table_ref,
    source, score_ref, rows_ref,
):
    source[0:112] = dlon_ref[...]
    source[112:224] = dlat_ref[...]
    source[224:272] = ddiag_ref[...]
    source[272:608] = dloc_ref[...]
    everything = source[...]
    w_qkv = qkv_ref[...]
    windows = []
    for w in range(4):
        rows = pl.ds(w * WIN, WIN)
        grad = mm(one_hot(back_ref[rows, :], 608), everything)
        inner = mm_nt(grad.astype(bf16), down_ref[...]) * slope_ref[rows, :].astype(f32)
        grad = grad + norm_back(
            mm_nt(inner.astype(bf16), up_ref[...]), n2_ref[rows, :].astype(f32), r2_ref[rows, :]
        )
        mix_grad = mm_nt(grad.astype(bf16), proj_ref[...]).astype(bf16)
        dq, dk, dv = attend_back(
            q_ref[rows, :], k_ref[rows, :], v_ref[rows, :], mix_grad,
            probs_ref, w * 6 * WIN,
            score_ref.at[pl.ds(w // 2 * 6 * WIN, 6 * WIN)], w % 2 == 1,
        )
        normed_grad = (
            mm_nt(dq.astype(bf16), w_qkv[:, 0:192])
            + mm_nt(dk.astype(bf16), w_qkv[:, 192:384])
            + mm_nt(dv.astype(bf16), w_qkv[:, 384:576])
        )
        result = grad + norm_back(normed_grad, n1_ref[rows, :].astype(f32), r1_ref[rows, :])
        res_ref[rows, :] = result.astype(bf16)
        windows.append(result)
    slon_ref[...] = pack([quadrant(windows, q, 0) for q in range(1, 4)], 112)
    slat_ref[...] = pack([quadrant(windows, 0, q) for q in range(1, 4)], 112)
    sdiag_ref[...] = pack([quadrant(windows, 0, 0)], 48)
    table_ref[...] = table_grad(score_ref, base_ref, slot_ref, rows_ref).astype(bf16)


def last_kernel(
    res_ref, lon_ref, lat_ref, diag_ref, leave_ref, cloc, clon, clat, cdiag, result_ref,
    tokens_ref, coarse_ref, source, coarse_source,
):
    source[0:576] = res_ref[...]
    source[576:688] = lon_ref[...]
    source[688:800] = lat_ref[...]
    source[800:848] = diag_ref[...]
    everything = source[...]
    for w in range(4):
        rows = pl.ds(w * WIN, WIN)
        tokens_ref[rows, :] = mm(one_hot(leave_ref[rows, :], 848), everything).astype(bf16)
    coarse_source[0:48] = cloc[...]
    coarse_source[48:96] = clon[...]
    coarse_source[96:144] = clat[...]
    coarse_source[144:192] = cdiag[...]
    moved = mm(one_hot(result_ref[...], 192), coarse_source[...])
    for z in range(2):
        for row in range(6):
            start = z * 72 + row * 12
            coarse_ref[z, row] = moved[start : start + 12].astype(bf16)


def run(kernel, outs, scratch, flops, inputs):
    shapes = [jax.ShapeDtypeStruct(shape, kind) for shape, kind in outs]
    size = sum(math.prod(s.shape) * s.dtype.itemsize for s in shapes)
    size += sum(x.size * x.dtype.itemsize for x in inputs)
    return pl.pallas_call(
        kernel,
        out_shape=shapes,
        scratch_shapes=[pltpu.VMEM(shape, kind) for shape, kind in scratch],
        compiler_params=pltpu.CompilerParams(vmem_limit_bytes=VMEM),
        cost_estimate=pl.CostEstimate(flops=flops, bytes_accessed=size, transcendentals=0),
    )(*inputs)


def move(value, lon_steps, lat_steps):
    lon, lat = lax.axis_size("lon"), lax.axis_size("lat")
    if lat_steps == 0:
        pairs = [(s, (s + lon_steps) % lon) for s in range(lon)]
        return lax.ppermute(value, "lon", pairs)
    if lon_steps == 0:
        pairs = [(s, (s + lat_steps) % lat) for s in range(lat)]
        return lax.ppermute(value, "lat", pairs)
    pairs = [
        (b * lat + a, (b + lon_steps) % lon * lat + (a + lat_steps) % lat)
        for b in range(lon)
        for a in range(lat)
    ]
    return lax.ppermute(value, ("lon", "lat"), pairs)


def send(pieces, steps):
    on_lon, on_lat, on_both = pieces
    return move(on_lon, steps, 0), move(on_lat, 0, steps), move(on_both, steps, steps)


def lon_total(value):
    count = lax.axis_size("lon")
    if count & (count - 1):
        return lax.psum(value, "lon").astype(f32)
    step = 1
    total = value
    while step < count:
        kept = total.astype(bf16)
        other = lax.ppermute(kept, "lon", [(s, s ^ step) for s in range(count)])
        total = kept.astype(f32) + other.astype(f32)
        step *= 2
    return total.astype(f32)


def to_table(grad, bands, heads):
    return grad.reshape(12, 16, ENTRIES)[:, :12].reshape(bands, heads, 12 * ENTRIES)


def body(
    tokens, mask_ids, fine_qkv, fine_proj, fine_up, fine_down, fine_bias, reduce_weight,
    coarse_qkv, coarse_proj, coarse_up, coarse_down, coarse_bias, out_grad,
):
    lat_index = lax.axis_index("lat")
    flat = tokens.reshape(576, 192)
    arrived = send(
        (
            tokens[:, 0:9, 16:24].reshape(144, 192),
            tokens[:, 9:12].reshape(144, 192),
            tokens[:, 9:12, 16:24].reshape(48, 192),
        ),
        1,
    )
    column = lambda index: jnp.asarray(index).reshape(-1, 1)
    line = lambda index: jnp.asarray(index).reshape(1, -1)

    tables = jnp.concatenate(
        [fine_bias.reshape(12, 12, ENTRIES), coarse_bias.reshape(12, 12, ENTRIES)], axis=0
    )
    tables = jnp.pad(tables, ((0, 0), (0, 4), (0, 0))).reshape(384, ENTRIES)
    expanded = run(
        bias_kernel,
        [((12 * WIN, WIN), f32)] * 2 + [((48, 384), bf16)] * 4,
        [((24, 2, 12, 16, WIN), bf16)],
        4_000_000_000,
        (tables, line(BASE), column(ROW_SLOT), out_grad),
    )
    fine_table, coarse_table, g00, g01, g10, g11 = expanded
    grads = (g00, *send((g01, g10, g11), 1))

    labels = mask_ids.reshape(2, 2, 2, 3, 2, 2, 6)
    top = jnp.zeros((2, 2, 1, 1, 1, 1), jnp.int32).at[0, 0].set(1)[None]
    labels = labels * 2 + jnp.where(lat_index == 0, top, 0)
    labels = labels.transpose(1, 4, 2, 5, 0, 3, 6).reshape(4, WIN)
    fine_mask = jnp.where(labels[:, :, None] == labels[:, None, :], 0.0, -1e30).astype(f32)
    low_half = jnp.arange(WIN) < WIN // 2
    coarse_mask = jnp.where(
        (low_half[:, None] == low_half[None, :]) | (lat_index != 0), 0.0, -1e30
    ).astype(f32)

    tok = ((576, 192), bf16)
    edges = [((112, 192), bf16), ((112, 192), bf16), ((48, 192), bf16)]
    fine = run(
        fine_kernel,
        [tok] + edges
        + [tok] * 3
        + [((24 * WIN, WIN), bf16), tok, ((576, 1), f32), tok, ((576, 1), f32), ((576, 768), bf16)],
        [((912, 192), bf16)],
        2_000_000_000,
        (flat, *arrived, column(ARRIVE), fine_table, fine_mask, fine_qkv, fine_proj, fine_up, fine_down),
    )
    saved = fine[4:]
    arrived = send(fine[1:4], 1)
    coarse = run(
        coarse_kernel,
        [((48, 384), bf16)] * 4 + edges + [((336, 192), bf16), ((192, ENTRIES), bf16)],
        [
            ((848, 192), bf16),
            ((12 * WIN, WIN), bf16),
            ((12 * WIN, WIN), f32),
            ((12, 192, WIN), bf16),
            ((576, 192), bf16),
        ],
        3_000_000_000,
        (
            fine[0], *arrived, column(MERGE), column(SPLIT), coarse_table, coarse_mask, *grads,
            reduce_weight, coarse_qkv, coarse_proj, coarse_up, coarse_down,
            column(BASE), line(ROW_SLOT),
        ),
    )
    c00, c01, c10, c11 = coarse[:4]
    arrived = send(coarse[4:7], -1)
    results = (c11, *send((c10, c01, c00), -1))
    coarse_total = lon_total(coarse[8])
    fine_back = run(
        fine_back_kernel,
        [tok] + edges + [((192, ENTRIES), bf16)],
        [((608, 192), bf16), ((12 * WIN, WIN), f32), ((12, 192, WIN), bf16)],
        3_000_000_000,
        (
            *arrived, coarse[7], column(BACK), *saved,
            fine_qkv, fine_proj, fine_up, fine_down, column(BASE), line(ROW_SLOT),
        ),
    )
    arrived = send(fine_back[1:4], -1)
    fine_total = lon_total(fine_back[4])
    d_tokens, coarse_result = run(
        last_kernel,
        [tok, ((2, 6, 12, 384), bf16)],
        [((848, 192), bf16), ((192, 384), bf16)],
        300_000_000,
        (fine_back[0], *arrived, column(LEAVE), *results, column(RESULT)),
    )
    return (
        coarse_result,
        d_tokens.reshape(tokens.shape),
        to_table(fine_total, 2, HEADS_F),
        to_table(coarse_total, 1, HEADS_C),
    )


def solution(mesh):
    grid = P(None, "lat", "lon", None)
    bands = P("lat", None, None)
    in_specs = (
        grid, P(None, "lat", "lon"), P(), P(), P(), P(), bands,
        P(), P(), P(), P(), P(), bands, grid,
    )
    out_specs = (grid, grid, bands, bands)
    return jax.shard_map(body, mesh=mesh, in_specs=in_specs, out_specs=out_specs, check_vma=False)
```

```python
import math

import jax
import jax.numpy as jnp
import numpy as np
from jax import lax
from jax.experimental import pallas as pl
from jax.experimental.pallas import tpu as pltpu
from jax.sharding import PartitionSpec as P

HEADS_F = 6
HEADS_C = 12
HEAD = 32
WIN = 144
QUAD = 36
SPAN = 23
ENTRIES = 276
LOG2E = math.log2(math.e)
VMEM = 20 * 1024 * 1024
f32 = jnp.float32
bf16 = jnp.bfloat16


def spot(z, i, j):
    quadrant = (i % 6) // 3 * 2 + (j % 12) // 6
    return quadrant * QUAD + z * 18 + i % 3 * 6 + j % 6


def fine_spot(z, i, j):
    return (i // 6 * 2 + j // 12) * WIN + spot(z, i, j)


def in_quad(z, i, j):
    return z * 18 + i % 3 * 6 + j % 6


def index_maps():
    arrive = np.zeros(576, np.int32)
    edge = np.full(272, -1, np.int32)
    merge = np.zeros(576, np.int32)
    split = np.full(608, -1, np.int32)
    back = np.zeros(576, np.int32)
    leave = np.zeros(576, np.int32)
    for z in range(2):
        for i in range(12):
            for j in range(24):
                here = fine_spot(z, i, j)
                if i >= 3 and j >= 6:
                    arrive[here] = z * 288 + (i - 3) * 24 + j - 6
                    came = fine_spot(z, i - 3, j - 6)
                elif i >= 3:
                    came = 576 + (i - 3) // 3 * QUAD + in_quad(z, i, j)
                    edge[came - 576] = z * 288 + (i - 3) * 24 + 18 + j
                elif j >= 6:
                    came = 688 + (j - 6) // 6 * QUAD + in_quad(z, i, j)
                    edge[came - 576] = z * 288 + (i + 9) * 24 + j - 6
                else:
                    came = 800 + in_quad(z, i, j)
                    edge[came - 576] = z * 288 + (i + 9) * 24 + 18 + j
                if came >= 576:
                    arrive[here] = came
                part = (i % 2 + j % 2 * 2) * WIN + spot(z, i // 2, j // 2)
                merge[part] = came
                if i >= 3 and j >= 6:
                    slot = 272 + z * 162 + (i - 3) * 18 + j - 6
                    back[fine_spot(z, i - 3, j - 6)] = slot
                elif i >= 3:
                    slot = z * 54 + (i - 3) * 6 + j
                    back[fine_spot(z, i - 3, j + 18)] = slot
                elif j >= 6:
                    slot = 112 + z * 54 + i * 18 + j - 6
                    back[fine_spot(z, i + 9, j - 6)] = slot
                else:
                    slot = 224 + z * 18 + i * 6 + j
                    back[fine_spot(z, i + 9, j + 18)] = slot
                split[slot] = part
                natural = z * 288 + i * 24 + j
                if i < 9 and j < 18:
                    leave[natural] = fine_spot(z, i + 3, j + 6)
                elif i < 9:
                    leave[natural] = 576 + i // 3 * QUAD + in_quad(z, i, j)
                elif j < 18:
                    leave[natural] = 688 + j // 6 * QUAD + in_quad(z, i, j)
                else:
                    leave[natural] = 800 + in_quad(z, i, j)
    result = np.zeros(WIN, np.int32)
    base = np.zeros(WIN, np.int32)
    row_slot = np.zeros(WIN, np.int32)
    for z in range(2):
        for i in range(6):
            for j in range(12):
                result[z * 72 + i * 12 + j] = (i // 3 * 2 + j // 6) * 48 + in_quad(z, i, j)
                here = spot(z, i, j)
                base[here] = (z * 6 + i) * SPAN + 11 - j
                row_slot[here] = j * 16 + z * 6 + i
    return arrive, edge, merge, split, back, leave, result, base, row_slot


ARRIVE, EDGE, MERGE, SPLIT, BACK, LEAVE, RESULT, BASE, ROW_SLOT = index_maps()


def one_hot(column, width):
    spots = lax.broadcasted_iota(jnp.int32, (column.shape[0], width), 1)
    return jnp.where(spots == column, 1.0, 0.0).astype(bf16)


def mm(left, right):
    return jnp.dot(left, right, preferred_element_type=f32)


def mm_nt(left, right):
    return lax.dot_general(left, right, (((1,), (1,)), ((), ())), preferred_element_type=f32)


def mm_tn(left, right):
    return lax.dot_general(left, right, (((0,), (0,)), ((), ())), preferred_element_type=f32)


def norm(values):
    centred = values - jnp.mean(values, axis=-1, keepdims=True)
    scale = lax.rsqrt(jnp.mean(centred * centred, axis=-1, keepdims=True) + 1e-5)
    return centred * scale, scale


def norm_back(grad, normed, scale):
    along = jnp.mean(grad * normed, axis=-1, keepdims=True)
    return (grad - jnp.mean(grad, axis=-1, keepdims=True) - normed * along) * scale


def gelu_pair(x):
    u = jnp.abs(x) * math.sqrt(0.5)
    t = 1.0 / (1.0 + 0.3275911 * u)
    e = jnp.exp(-u * u)
    poly = 1.421413741 + t * (-1.453152027 + t * 1.061405429)
    tail = 0.5 * (t * (0.254829592 + t * (-0.284496736 + t * poly))) * e
    below = jnp.where(x >= 0, 1.0 - tail, tail)
    return x * below, below + x * (e * (1.0 / math.sqrt(2 * math.pi)))


def groups(channels):
    return [(start, min(start + 128, channels)) for start in range(0, channels, 128)]


def head_lanes(rows, width):
    return lax.broadcasted_iota(jnp.int32, (rows, width), 1) // HEAD


def stack_heads(part):
    lanes = head_lanes(part.shape[0], part.shape[1])
    count = part.shape[1] // HEAD
    zero = jnp.zeros_like(part)
    return jnp.concatenate([jnp.where(lanes == h, part, zero) for h in range(count)], axis=0)


def pick_heads(stacked):
    width = stacked.shape[1]
    lanes = head_lanes(WIN, width)
    total = stacked[:WIN]
    for h in range(1, width // HEAD):
        total = jnp.where(lanes == h, stacked[h * WIN : (h + 1) * WIN], total)
    return total


def attend(queries, keys, values, bias_ref, bias_row, mask, probs_ref, probs_row):
    mixed = []
    for start, stop in groups(queries.shape[1]):
        count = (stop - start) // HEAD
        scores = mm_nt(stack_heads(queries[:, start:stop]), keys[:, start:stop])
        row = start // HEAD * WIN
        for h in range(count):
            here = row + h * WIN
            logits = (
                scores[h * WIN : (h + 1) * WIN] * (HEAD**-0.5 * LOG2E)
                + bias_ref[pl.ds(bias_row + here, WIN), :]
                + mask
            )
            raised = jnp.exp2(logits - jnp.max(logits, axis=-1, keepdims=True))
            probs = raised * (1.0 / jnp.sum(raised, axis=-1, keepdims=True))
            probs_ref[pl.ds(probs_row + here, WIN), :] = probs.astype(bf16)
        stacked = mm(probs_ref[pl.ds(probs_row + row, count * WIN), :], values[:, start:stop])
        mixed.append(pick_heads(stacked))
    return jnp.concatenate(mixed, axis=1)


def attend_back(queries, keys, values, mix_grad, probs_ref, probs_row, score_ref, add):
    query_grad, key_grad, value_grad = [], [], []
    for start, stop in groups(queries.shape[1]):
        count = (stop - start) // HEAD
        row = start // HEAD * WIN
        probs_all = probs_ref[pl.ds(probs_row + row, count * WIN), :]
        grads = stack_heads(mix_grad[:, start:stop])
        value_grad.append(mm_tn(probs_all, grads))
        probs_grad = mm_nt(grads, values[:, start:stop])
        pieces = []
        for h in range(count):
            probs = probs_all[h * WIN : (h + 1) * WIN].astype(f32)
            grad = probs_grad[h * WIN : (h + 1) * WIN]
            weighted = grad * probs
            score_grad = weighted - probs * jnp.sum(weighted, axis=-1, keepdims=True)
            place = pl.ds(row + h * WIN, WIN)
            if add:
                score_ref[place, :] += score_grad
            else:
                score_ref[place, :] = score_grad
            pieces.append(score_grad.astype(bf16))
        score_all = jnp.concatenate(pieces, axis=0)
        query_grad.append(pick_heads(mm(score_all, keys[:, start:stop])))
        key_grad.append(mm_tn(score_all, stack_heads(queries[:, start:stop])))
    scale = HEAD**-0.5
    return (
        jnp.concatenate(query_grad, axis=1) * scale,
        jnp.concatenate(key_grad, axis=1) * scale,
        jnp.concatenate(value_grad, axis=1),
    )


def swap_rows():
    row = lax.broadcasted_iota(jnp.int32, (192, 192), 0)
    return jnp.where(
        lax.broadcasted_iota(jnp.int32, (192, 192), 1) == row % 16 * 16 + row // 16, 1.0, 0.0
    ).astype(bf16)


def table_grad(score_ref, base_ref, slot_ref, rows_ref):
    regroup = jnp.where(
        lax.broadcasted_iota(jnp.int32, (192, WIN), 0) == slot_ref[...], 1.0, 0.0
    ).astype(bf16)
    for h in range(12):
        moved = mm(regroup, score_ref[pl.ds(h * WIN, WIN), :].astype(bf16)).astype(bf16)
        rows_ref[:, pl.ds(h * 16, 16), :] = moved.reshape(12, 16, WIN)
    total = jnp.zeros((192, ENTRIES), f32)
    for column in range(12):
        total += mm(rows_ref[column], one_hot(base_ref[...] + column, ENTRIES))
    swapped = mm(swap_rows(), total.astype(bf16))
    halves = [
        jnp.concatenate([swapped[a * 16 : a * 16 + 12] for a in range(start, start + 6)], axis=1)
        for start in (0, 6)
    ]
    return jnp.concatenate(halves, axis=0).astype(bf16)


def pack(pieces, rows):
    count = sum(piece.shape[0] for piece in pieces)
    if rows > count:
        pieces = pieces + [jnp.zeros((rows - count, pieces[0].shape[1]), f32)]
    return jnp.concatenate(pieces, axis=0).astype(bf16)


def quadrant(windows, qi, qj):
    part = (qi % 2 * 2 + qj % 2) * QUAD
    return windows[qi // 2 * 2 + qj // 2][part : part + QUAD]


def edge_kernel(tokens_ref, edge_ref, slon_ref, slat_ref, sdiag_ref):
    moved = mm(one_hot(edge_ref[...], 576), tokens_ref[...]).astype(bf16)
    slon_ref[...] = moved[0:112]
    slat_ref[...] = moved[112:224]
    sdiag_ref[...] = moved[224:272]


def expand(table_ref, base_ref, slot_ref, out_ref, held):
    table = jnp.concatenate([table_ref[:, b, :] for b in range(table_ref.shape[1])], axis=0)
    filler = jnp.zeros((4, ENTRIES), f32)
    pieces = []
    for a in range(12):
        pieces += [table[:, a * ENTRIES : (a + 1) * ENTRIES], filler]
    table = jnp.concatenate(pieces, axis=0)
    high = table.astype(bf16)
    low = (table - high.astype(f32)).astype(bf16)
    swap = swap_rows()
    high, low = mm(swap, high).astype(bf16), mm(swap, low).astype(bf16)
    entry = lax.broadcasted_iota(jnp.int32, (ENTRIES, WIN), 0)
    for column in range(12):
        picker = jnp.where(entry == base_ref[...] + column, 1.0, 0.0).astype(bf16)
        held[:, 0, column] = mm(high, picker).astype(bf16).reshape(12, 16, WIN)
        held[:, 1, column] = mm(low, picker).astype(bf16).reshape(12, 16, WIN)
    once = one_hot(slot_ref[...], 192)
    for h in range(12):
        out_ref[pl.ds(h * WIN, WIN), :] = (
            mm(once, held[h, 0].reshape(192, WIN)) + mm(once, held[h, 1].reshape(192, WIN))
        ) * LOG2E


def fine_bias_kernel(table_ref, base_ref, slot_ref, grad_ref, out_ref, g0, g1, g2, g3, held):
    for index, out in enumerate((g0, g1, g2, g3)):
        hi, hj = index // 2, index % 2
        pieces = [
            grad_ref[z, hi * 3 + row].astype(f32)[hj * 6 : hj * 6 + 6]
            for z in range(2)
            for row in range(3)
        ]
        out[...] = pack(pieces, 48)
    expand(table_ref, base_ref, slot_ref, out_ref, held)


def coarse_bias_kernel(table_ref, base_ref, slot_ref, out_ref, held):
    expand(table_ref, base_ref, slot_ref, out_ref, held)


def coarse_table_kernel(score_ref, base_ref, slot_ref, table_ref, rows_ref):
    table_ref[...] = table_grad(score_ref, base_ref, slot_ref, rows_ref)


def table_sum_kernel(kept_ref, other_ref, out_ref):
    total = kept_ref[...].astype(f32) + other_ref[...].astype(f32)
    total = jnp.concatenate([total[0:12], total[12:24]], axis=1)
    heads = out_ref.shape[0]
    for b in range(out_ref.shape[1]):
        out_ref[:, b, :] = total[b * heads : (b + 1) * heads]


def fine_kernel(
    tokens_ref, lon_ref, lat_ref, diag_ref, arrive_ref, bias_ref, mask_ref,
    qkv_ref, proj_ref, up_ref, down_ref,
    res_ref, slon_ref, slat_ref, sdiag_ref,
    q_ref, k_ref, v_ref, probs_ref, n1_ref, r1_ref, n2_ref, r2_ref, slope_ref,
    source,
):
    source[0:576] = tokens_ref[...]
    source[576:688] = lon_ref[...]
    source[688:800] = lat_ref[...]
    source[800:848] = diag_ref[...]
    everything = source[...]
    w_qkv = qkv_ref[...]
    bases = []
    for w in range(4):
        rows = pl.ds(w * WIN, WIN)
        base = mm(one_hot(arrive_ref[rows, :], 848), everything)
        normed, scale = norm(base)
        normed = normed.astype(bf16)
        n1_ref[rows, :] = normed
        r1_ref[rows, :] = scale
        q_ref[rows, :] = mm(normed, w_qkv[:, 0:192]).astype(bf16)
        k_ref[rows, :] = mm(normed, w_qkv[:, 192:384]).astype(bf16)
        v_ref[rows, :] = mm(normed, w_qkv[:, 384:576]).astype(bf16)
        bases.append(base)
    windows = []
    for w in range(4):
        rows = pl.ds(w * WIN, WIN)
        mixture = attend(
            q_ref[rows, :], k_ref[rows, :], v_ref[rows, :],
            bias_ref, w // 2 * 6 * WIN, mask_ref[w], probs_ref, w * 6 * WIN,
        ).astype(bf16)
        first = bases[w] + mm(mixture, proj_ref[...])
        renormed, scale = norm(first)
        renormed = renormed.astype(bf16)
        n2_ref[rows, :] = renormed
        r2_ref[rows, :] = scale
        active, slope = gelu_pair(mm(renormed, up_ref[...]))
        slope_ref[rows, :] = slope.astype(bf16)
        result = first + mm(active.astype(bf16), down_ref[...])
        res_ref[rows, :] = result.astype(bf16)
        windows.append(result)
    slon_ref[...] = pack([quadrant(windows, q, 3) for q in range(3)], 112)
    slat_ref[...] = pack([quadrant(windows, 3, q) for q in range(3)], 112)
    sdiag_ref[...] = pack([quadrant(windows, 3, 3)], 48)


def coarse_kernel(
    res_ref, lon_ref, lat_ref, diag_ref, merge_ref, split_ref, bias_ref, mask_ref,
    gloc_ref, glon_ref, glat_ref, gdiag_ref,
    reduce_ref, qkv_ref, proj_ref, up_ref, down_ref,
    c0, c1, c2, c3, dlon_ref, dlat_ref, ddiag_ref, dloc_ref, score_ref,
    source, probs_ref, parts_ref,
):
    source[0:576] = res_ref[...]
    source[576:688] = lon_ref[...]
    source[688:800] = lat_ref[...]
    source[800:848] = diag_ref[...]
    everything = source[...]
    parts = [mm(one_hot(merge_ref[pl.ds(k * WIN, WIN), :], 848), everything) for k in range(4)]
    mean = sum(jnp.sum(part, axis=-1, keepdims=True) for part in parts) * (1.0 / 768)
    parts = [part - mean for part in parts]
    square = sum(jnp.sum(part * part, axis=-1, keepdims=True) for part in parts)
    merge_scale = lax.rsqrt(square * (1.0 / 768) + 1e-5)
    parts = [(part * merge_scale).astype(bf16) for part in parts]
    base = sum(mm(parts[k], reduce_ref[k * 192 : (k + 1) * 192]) for k in range(4))
    base = base.astype(bf16).astype(f32)
    normed, scale1 = norm(base)
    normed = normed.astype(bf16)
    queries = mm(normed, qkv_ref[:, 0:384]).astype(bf16)
    keys = mm(normed, qkv_ref[:, 384:768]).astype(bf16)
    values = mm(normed, qkv_ref[:, 768:1152]).astype(bf16)
    mixture = attend(queries, keys, values, bias_ref, 0, mask_ref[...], probs_ref, 0).astype(bf16)
    first = base + mm(mixture, proj_ref[...])
    renormed, scale2 = norm(first)
    renormed = renormed.astype(bf16)
    active, slope = gelu_pair(mm(renormed, up_ref[...]))
    result = first + mm(active.astype(bf16), down_ref[...])
    for index, out in enumerate((c0, c1, c2, c3)):
        out[...] = pack([result[index * QUAD : (index + 1) * QUAD]], 48)

    grad = jnp.concatenate(
        [ref[...].astype(f32)[:QUAD] for ref in (gdiag_ref, glat_ref, glon_ref, gloc_ref)], axis=0
    )
    inner = mm_nt(grad.astype(bf16), down_ref[...]) * slope
    grad = grad + norm_back(mm_nt(inner.astype(bf16), up_ref[...]), renormed.astype(f32), scale2)
    mix_grad = mm_nt(grad.astype(bf16), proj_ref[...]).astype(bf16)
    dq, dk, dv = attend_back(queries, keys, values, mix_grad, probs_ref, 0, score_ref, False)
    normed_grad = (
        mm_nt(dq.astype(bf16), qkv_ref[:, 0:384])
        + mm_nt(dk.astype(bf16), qkv_ref[:, 384:768])
        + mm_nt(dv.astype(bf16), qkv_ref[:, 768:1152])
    )
    grad = grad + norm_back(normed_grad, normed.astype(f32), scale1)
    grad = grad.astype(bf16)
    grads = [mm_nt(grad, reduce_ref[k * 192 : (k + 1) * 192]) for k in range(4)]
    mean = sum(jnp.sum(g, axis=-1, keepdims=True) for g in grads) * (1.0 / 768)
    along = sum(
        jnp.sum(g * p.astype(f32), axis=-1, keepdims=True) for g, p in zip(grads, parts)
    ) * (1.0 / 768)
    for k in range(4):
        part = (grads[k] - mean - parts[k].astype(f32) * along) * merge_scale
        parts_ref[pl.ds(k * WIN, WIN), :] = part.astype(bf16)
    everything = parts_ref[...]
    moved = mm(one_hot(split_ref[...], 576), everything).astype(bf16)
    dlon_ref[...] = moved[0:112]
    dlat_ref[...] = moved[112:224]
    ddiag_ref[...] = moved[224:272]
    dloc_ref[...] = moved[272:608]


def fine_back_kernel(
    dlon_ref, dlat_ref, ddiag_ref, dloc_ref, back_ref,
    q_ref, k_ref, v_ref, probs_ref, n2_ref, r2_ref, slope_ref,
    proj_ref, up_ref, down_ref, base_ref, slot_ref,
    grad_ref, dq_ref, dk_ref, dv_ref, table_ref,
    source, score_ref, rows_ref,
):
    source[0:112] = dlon_ref[...]
    source[112:224] = dlat_ref[...]
    source[224:272] = ddiag_ref[...]
    source[272:608] = dloc_ref[...]
    everything = source[...]
    for w in range(4):
        rows = pl.ds(w * WIN, WIN)
        grad = mm(one_hot(back_ref[rows, :], 608), everything)
        inner = mm_nt(grad.astype(bf16), down_ref[...]) * slope_ref[rows, :].astype(f32)
        grad = grad + norm_back(
            mm_nt(inner.astype(bf16), up_ref[...]), n2_ref[rows, :].astype(f32), r2_ref[rows, :]
        )
        grad_ref[rows, :] = grad
        mix_grad = mm_nt(grad.astype(bf16), proj_ref[...]).astype(bf16)
        dq, dk, dv = attend_back(
            q_ref[rows, :], k_ref[rows, :], v_ref[rows, :], mix_grad,
            probs_ref, w * 6 * WIN,
            score_ref.at[pl.ds(w // 2 * 6 * WIN, 6 * WIN)], w % 2 == 1,
        )
        dq_ref[rows, :] = dq.astype(bf16)
        dk_ref[rows, :] = dk.astype(bf16)
        dv_ref[rows, :] = dv.astype(bf16)
    table_ref[...] = table_grad(score_ref, base_ref, slot_ref, rows_ref)


def qkv_back_kernel(
    grad_ref, dq_ref, dk_ref, dv_ref, n1_ref, r1_ref, qkv_ref,
    res_ref, slon_ref, slat_ref, sdiag_ref,
):
    w_qkv = qkv_ref[...]
    windows = []
    for w in range(4):
        rows = pl.ds(w * WIN, WIN)
        normed_grad = (
            mm_nt(dq_ref[rows, :], w_qkv[:, 0:192])
            + mm_nt(dk_ref[rows, :], w_qkv[:, 192:384])
            + mm_nt(dv_ref[rows, :], w_qkv[:, 384:576])
        )
        result = grad_ref[rows, :] + norm_back(
            normed_grad, n1_ref[rows, :].astype(f32), r1_ref[rows, :]
        )
        res_ref[rows, :] = result.astype(bf16)
        windows.append(result)
    slon_ref[...] = pack([quadrant(windows, q, 0) for q in range(1, 4)], 112)
    slat_ref[...] = pack([quadrant(windows, 0, q) for q in range(1, 4)], 112)
    sdiag_ref[...] = pack([quadrant(windows, 0, 0)], 48)


def last_kernel(
    res_ref, lon_ref, lat_ref, diag_ref, leave_ref, cloc, clon, clat, cdiag, result_ref,
    tokens_ref, coarse_ref, source, coarse_source,
):
    source[0:576] = res_ref[...]
    source[576:688] = lon_ref[...]
    source[688:800] = lat_ref[...]
    source[800:848] = diag_ref[...]
    everything = source[...]
    for w in range(4):
        rows = pl.ds(w * WIN, WIN)
        tokens_ref[rows, :] = mm(one_hot(leave_ref[rows, :], 848), everything).astype(bf16)
    coarse_source[0:48] = cloc[...]
    coarse_source[48:96] = clon[...]
    coarse_source[96:144] = clat[...]
    coarse_source[144:192] = cdiag[...]
    moved = mm(one_hot(result_ref[...], 192), coarse_source[...])
    for z in range(2):
        for row in range(6):
            start = z * 72 + row * 12
            coarse_ref[z, row] = moved[start : start + 12].astype(bf16)


def run(kernel, outs, scratch, weight, inputs):
    shapes = [jax.ShapeDtypeStruct(shape, kind) for shape, kind in outs]
    size = sum(math.prod(s.shape) * s.dtype.itemsize for s in shapes)
    size += sum(x.size * x.dtype.itemsize for x in inputs)
    return pl.pallas_call(
        kernel,
        out_shape=shapes,
        scratch_shapes=[pltpu.VMEM(shape, kind) for shape, kind in scratch],
        compiler_params=pltpu.CompilerParams(vmem_limit_bytes=VMEM),
        cost_estimate=pl.CostEstimate(
            flops=weight * 1_000_000_000, bytes_accessed=size, transcendentals=0
        ),
    )(*inputs)


def move(value, lon_steps, lat_steps):
    lon, lat = lax.axis_size("lon"), lax.axis_size("lat")
    if lat_steps == 0:
        pairs = [(s, (s + lon_steps) % lon) for s in range(lon)]
        return lax.ppermute(value, "lon", pairs)
    if lon_steps == 0:
        pairs = [(s, (s + lat_steps) % lat) for s in range(lat)]
        return lax.ppermute(value, "lat", pairs)
    pairs = [
        (b * lat + a, (b + lon_steps) % lon * lat + (a + lat_steps) % lat)
        for b in range(lon)
        for a in range(lat)
    ]
    return lax.ppermute(value, ("lon", "lat"), pairs)


def send(pieces, steps):
    on_lon, on_lat, on_both = pieces
    return move(on_lon, steps, 0), move(on_lat, 0, steps), move(on_both, steps, steps)


def lon_total(value):
    count = lax.axis_size("lon")
    step = 1
    total = value
    while step < count:
        kept = total.astype(bf16)
        other = lax.ppermute(kept, "lon", [(s, s ^ step) for s in range(count)])
        total = kept.astype(f32) + other.astype(f32)
        step *= 2
    return kept, other


def body(
    tokens, mask_ids, fine_qkv, fine_proj, fine_up, fine_down, fine_bias, reduce_weight,
    coarse_qkv, coarse_proj, coarse_up, coarse_down, coarse_bias, out_grad,
):
    lat_index = lax.axis_index("lat")
    flat = tokens.reshape(576, 192)
    column = lambda index: jnp.asarray(index).reshape(-1, 1)
    line = lambda index: jnp.asarray(index).reshape(1, -1)
    tok = ((576, 192), bf16)
    edges = [((112, 192), bf16), ((112, 192), bf16), ((48, 192), bf16)]
    scores = ((12 * WIN, WIN), f32)
    table = ((24, 6 * ENTRIES), bf16)
    table_rows = ((12, 192, WIN), bf16)

    arrived = send(run(edge_kernel, edges, [], 1, (flat, column(EDGE))), 1)
    held = ((12, 2, 12, 16, WIN), bf16)
    fine_table, g00, g01, g10, g11 = run(
        fine_bias_kernel,
        [scores] + [((48, 384), bf16)] * 4,
        [held],
        2,
        (fine_bias.transpose(1, 0, 2), line(BASE), column(ROW_SLOT), out_grad),
    )
    grads = (g00, *send((g01, g10, g11), 1))

    labels = mask_ids.reshape(2, 2, 2, 3, 2, 2, 6)
    top = jnp.zeros((2, 2, 1, 1, 1, 1), jnp.int32).at[0, 0].set(1)[None]
    labels = labels * 2 + jnp.where(lat_index == 0, top, 0)
    labels = labels.transpose(1, 4, 2, 5, 0, 3, 6).reshape(4, WIN)
    fine_mask = jnp.where(labels[:, :, None] == labels[:, None, :], 0.0, -1e30).astype(f32)
    low_half = jnp.arange(WIN) < WIN // 2
    coarse_mask = jnp.where(
        (low_half[:, None] == low_half[None, :]) | (lat_index != 0), 0.0, -1e30
    ).astype(f32)

    fine = run(
        fine_kernel,
        [tok] + edges
        + [tok] * 3
        + [((24 * WIN, WIN), bf16), tok, ((576, 1), f32), tok, ((576, 1), f32), ((576, 768), bf16)],
        [((848, 192), bf16)],
        8,
        (flat, *arrived, column(ARRIVE), fine_table, fine_mask, fine_qkv, fine_proj, fine_up, fine_down),
    )
    q, k, v, probs, n1, r1, n2, r2, slope = fine[4:]
    arrived = send(fine[1:4], 1)
    late_table, _ = lax.optimization_barrier((coarse_bias.transpose(1, 0, 2), fine[1]))
    (coarse_table,) = run(
        coarse_bias_kernel, [scores], [held], 2, (late_table, line(BASE), column(ROW_SLOT))
    )
    coarse = run(
        coarse_kernel,
        [((48, 384), bf16)] * 4 + edges + [((336, 192), bf16), scores],
        [((848, 192), bf16), ((12 * WIN, WIN), bf16), ((576, 192), bf16)],
        9,
        (
            fine[0], *arrived, column(MERGE), column(SPLIT), coarse_table, coarse_mask, *grads,
            reduce_weight, coarse_qkv, coarse_proj, coarse_up, coarse_down,
        ),
    )
    c00, c01, c10, c11 = coarse[:4]
    arrived = send(coarse[4:7], -1)
    (coarse_grad,) = run(
        coarse_table_kernel, [table], [table_rows], 2, (coarse[8], column(BASE), line(ROW_SLOT))
    )
    results = (c11, *send((c10, c01, c00), -1))
    coarse_total = lon_total(coarse_grad)
    *passed, fine_grad = run(
        fine_back_kernel,
        [((576, 192), f32)] + [tok] * 3 + [table],
        [((608, 192), bf16), scores, table_rows],
        7,
        (
            *arrived, coarse[7], column(BACK), q, k, v, probs, n2, r2, slope,
            fine_proj, fine_up, fine_down, column(BASE), line(ROW_SLOT),
        ),
    )
    fine_total = lon_total(fine_grad)
    fine_back = run(
        qkv_back_kernel, [tok] + edges, [], 2, (*passed, n1, r1, fine_qkv)
    )
    arrived = send(fine_back[1:4], -1)
    d_tokens, coarse_result = run(
        last_kernel,
        [tok, ((2, 6, 12, 384), bf16)],
        [((848, 192), bf16), ((192, 384), bf16)],
        1,
        (fine_back[0], *arrived, column(LEAVE), *results, column(RESULT)),
    )
    (coarse_out,) = run(
        table_sum_kernel, [((HEADS_C, 1, 12 * ENTRIES), f32)], [], 1, coarse_total
    )
    (fine_out,) = run(table_sum_kernel, [((HEADS_F, 2, 12 * ENTRIES), f32)], [], 1, fine_total)
    return (
        coarse_result,
        d_tokens.reshape(tokens.shape),
        fine_out.transpose(1, 0, 2),
        coarse_out.transpose(1, 0, 2),
    )


def solution(mesh):
    grid = P(None, "lat", "lon", None)
    bands = P("lat", None, None)
    in_specs = (
        grid, P(None, "lat", "lon"), P(), P(), P(), P(), bands,
        P(), P(), P(), P(), P(), bands, grid,
    )
    out_specs = (grid, grid, bands, bands)
    return jax.shard_map(body, mesh=mesh, in_specs=in_specs, out_specs=out_specs, check_vma=False)
```

```python
import math

import jax
import jax.numpy as jnp
import numpy as np
from jax import lax
from jax.experimental import pallas as pl
from jax.experimental.pallas import tpu as pltpu
from jax.sharding import PartitionSpec as P

HEADS_F = 6
HEADS_C = 12
HEAD = 32
WIN = 144
QUAD = 36
SPAN = 23
ENTRIES = 276
LOG2E = math.log2(math.e)
VMEM = 20 * 1024 * 1024
f32 = jnp.float32
bf16 = jnp.bfloat16


def spot(z, i, j):
    quadrant = (i % 6) // 3 * 2 + (j % 12) // 6
    return quadrant * QUAD + z * 18 + i % 3 * 6 + j % 6


def fine_spot(z, i, j):
    return (i // 6 * 2 + j // 12) * WIN + spot(z, i, j)


def in_quad(z, i, j):
    return z * 18 + i % 3 * 6 + j % 6


def index_maps():
    arrive = np.zeros(576, np.int32)
    merge = np.zeros(576, np.int32)
    split = np.full(608, -1, np.int32)
    back = np.zeros(576, np.int32)
    leave = np.zeros(576, np.int32)
    for z in range(2):
        for i in range(12):
            for j in range(24):
                here = fine_spot(z, i, j)
                if i >= 3 and j >= 6:
                    arrive[here] = z * 288 + (i - 3) * 24 + j - 6
                    came = fine_spot(z, i - 3, j - 6)
                elif i >= 3:
                    came = 576 + (i - 3) // 3 * QUAD + in_quad(z, i, j)
                elif j >= 6:
                    came = 688 + (j - 6) // 6 * QUAD + in_quad(z, i, j)
                else:
                    came = 800 + in_quad(z, i, j)
                if came >= 576:
                    arrive[here] = came
                part = (i % 2 + j % 2 * 2) * WIN + spot(z, i // 2, j // 2)
                merge[part] = came
                if i >= 3 and j >= 6:
                    slot = 272 + z * 162 + (i - 3) * 18 + j - 6
                    back[fine_spot(z, i - 3, j - 6)] = slot
                elif i >= 3:
                    slot = z * 54 + (i - 3) * 6 + j
                    back[fine_spot(z, i - 3, j + 18)] = slot
                elif j >= 6:
                    slot = 112 + z * 54 + i * 18 + j - 6
                    back[fine_spot(z, i + 9, j - 6)] = slot
                else:
                    slot = 224 + z * 18 + i * 6 + j
                    back[fine_spot(z, i + 9, j + 18)] = slot
                split[slot] = part
                natural = z * 288 + i * 24 + j
                if i < 9 and j < 18:
                    leave[natural] = fine_spot(z, i + 3, j + 6)
                elif i < 9:
                    leave[natural] = 576 + i // 3 * QUAD + in_quad(z, i, j)
                elif j < 18:
                    leave[natural] = 688 + j // 6 * QUAD + in_quad(z, i, j)
                else:
                    leave[natural] = 800 + in_quad(z, i, j)
    result = np.zeros(WIN, np.int32)
    base = np.zeros(WIN, np.int32)
    row_slot = np.zeros(WIN, np.int32)
    for z in range(2):
        for i in range(6):
            for j in range(12):
                result[z * 72 + i * 12 + j] = (i // 3 * 2 + j // 6) * 48 + in_quad(z, i, j)
                here = spot(z, i, j)
                base[here] = (z * 6 + i) * SPAN + 11 - j
                row_slot[here] = j * 16 + z * 6 + i
    return arrive, merge, split, back, leave, result, base, row_slot


ARRIVE, MERGE, SPLIT, BACK, LEAVE, RESULT, BASE, ROW_SLOT = index_maps()


def one_hot(column, width):
    spots = lax.broadcasted_iota(jnp.int32, (column.shape[0], width), 1)
    return jnp.where(spots == column, 1.0, 0.0).astype(bf16)


def mm(left, right):
    return jnp.dot(left, right, preferred_element_type=f32)


def mm_nt(left, right):
    return lax.dot_general(left, right, (((1,), (1,)), ((), ())), preferred_element_type=f32)


def mm_tn(left, right):
    return lax.dot_general(left, right, (((0,), (0,)), ((), ())), preferred_element_type=f32)


def norm(values):
    centred = values - jnp.mean(values, axis=-1, keepdims=True)
    scale = lax.rsqrt(jnp.mean(centred * centred, axis=-1, keepdims=True) + 1e-5)
    return centred * scale, scale


def norm_back(grad, normed, scale):
    along = jnp.mean(grad * normed, axis=-1, keepdims=True)
    return (grad - jnp.mean(grad, axis=-1, keepdims=True) - normed * along) * scale


def gelu_pair(x):
    u = jnp.abs(x) * math.sqrt(0.5)
    t = 1.0 / (1.0 + 0.3275911 * u)
    e = jnp.exp(-u * u)
    poly = 1.421413741 + t * (-1.453152027 + t * 1.061405429)
    tail = 0.5 * (t * (0.254829592 + t * (-0.284496736 + t * poly))) * e
    below = jnp.where(x >= 0, 1.0 - tail, tail)
    return x * below, below + x * (e * (1.0 / math.sqrt(2 * math.pi)))


def groups(channels):
    return [(start, min(start + 128, channels)) for start in range(0, channels, 128)]


def head_lanes(rows, width):
    return lax.broadcasted_iota(jnp.int32, (rows, width), 1) // HEAD


def stack_heads(part):
    lanes = head_lanes(part.shape[0], part.shape[1])
    count = part.shape[1] // HEAD
    zero = jnp.zeros_like(part)
    return jnp.concatenate([jnp.where(lanes == h, part, zero) for h in range(count)], axis=0)


def pick_heads(stacked):
    width = stacked.shape[1]
    lanes = head_lanes(WIN, width)
    total = stacked[:WIN]
    for h in range(1, width // HEAD):
        total = jnp.where(lanes == h, stacked[h * WIN : (h + 1) * WIN], total)
    return total


def attend(queries, keys, values, bias_ref, bias_row, mask, probs_ref, probs_row):
    mixed = []
    for start, stop in groups(queries.shape[1]):
        count = (stop - start) // HEAD
        scores = mm_nt(stack_heads(queries[:, start:stop]), keys[:, start:stop])
        row = start // HEAD * WIN
        for h in range(count):
            here = row + h * WIN
            logits = (
                scores[h * WIN : (h + 1) * WIN] * (HEAD**-0.5 * LOG2E)
                + bias_ref[pl.ds(bias_row + here, WIN), :]
                + mask
            )
            raised = jnp.exp2(logits - jnp.max(logits, axis=-1, keepdims=True))
            probs = raised * (1.0 / jnp.sum(raised, axis=-1, keepdims=True))
            probs_ref[pl.ds(probs_row + here, WIN), :] = probs.astype(bf16)
        stacked = mm(probs_ref[pl.ds(probs_row + row, count * WIN), :], values[:, start:stop])
        mixed.append(pick_heads(stacked))
    return jnp.concatenate(mixed, axis=1)


def attend_back(queries, keys, values, mix_grad, probs_ref, probs_row, score_ref, add):
    query_grad, key_grad, value_grad = [], [], []
    for start, stop in groups(queries.shape[1]):
        count = (stop - start) // HEAD
        row = start // HEAD * WIN
        probs_all = probs_ref[pl.ds(probs_row + row, count * WIN), :]
        grads = stack_heads(mix_grad[:, start:stop])
        value_grad.append(mm_tn(probs_all, grads))
        probs_grad = mm_nt(grads, values[:, start:stop])
        pieces = []
        for h in range(count):
            probs = probs_all[h * WIN : (h + 1) * WIN].astype(f32)
            grad = probs_grad[h * WIN : (h + 1) * WIN]
            weighted = grad * probs
            score_grad = weighted - probs * jnp.sum(weighted, axis=-1, keepdims=True)
            place = pl.ds(row + h * WIN, WIN)
            if add:
                score_ref[place, :] += score_grad
            else:
                score_ref[place, :] = score_grad
            pieces.append(score_grad.astype(bf16))
        score_all = jnp.concatenate(pieces, axis=0)
        query_grad.append(pick_heads(mm(score_all, keys[:, start:stop])))
        key_grad.append(mm_tn(score_all, stack_heads(queries[:, start:stop])))
    scale = HEAD**-0.5
    return (
        jnp.concatenate(query_grad, axis=1) * scale,
        jnp.concatenate(key_grad, axis=1) * scale,
        jnp.concatenate(value_grad, axis=1),
    )


def swap_rows():
    row = lax.broadcasted_iota(jnp.int32, (192, 192), 0)
    return jnp.where(
        lax.broadcasted_iota(jnp.int32, (192, 192), 1) == row % 16 * 16 + row // 16, 1.0, 0.0
    ).astype(bf16)


def table_grad(score_ref, base_ref, slot_ref, rows_ref):
    regroup = jnp.where(
        lax.broadcasted_iota(jnp.int32, (192, WIN), 0) == slot_ref[...], 1.0, 0.0
    ).astype(bf16)
    for h in range(12):
        moved = mm(regroup, score_ref[pl.ds(h * WIN, WIN), :].astype(bf16)).astype(bf16)
        rows_ref[:, pl.ds(h * 16, 16), :] = moved.reshape(12, 16, WIN)
    total = jnp.zeros((192, ENTRIES), f32)
    for column in range(12):
        total += mm(rows_ref[column], one_hot(base_ref[...] + column, ENTRIES))
    swapped = mm(swap_rows(), total.astype(bf16))
    halves = [
        jnp.concatenate([swapped[a * 16 : a * 16 + 12] for a in range(start, start + 6)], axis=1)
        for start in (0, 6)
    ]
    return jnp.concatenate(halves, axis=0).astype(bf16)


def pack(pieces, rows):
    count = sum(piece.shape[0] for piece in pieces)
    if rows > count:
        pieces = pieces + [jnp.zeros((rows - count, pieces[0].shape[1]), f32)]
    return jnp.concatenate(pieces, axis=0).astype(bf16)


def quadrant(windows, qi, qj):
    part = (qi % 2 * 2 + qj % 2) * QUAD
    return windows[qi // 2 * 2 + qj // 2][part : part + QUAD]


def halves(values):
    return [values[:, 0:192], values[:, 192:384]]


def edge_kernel(tokens_ref, grad_ref, slon_ref, slat_ref, sdiag_ref, gloc_ref):
    tokens = tokens_ref[...].astype(f32)

    def token_quadrant(row, start):
        pieces = []
        for z in range(2):
            for i in range(row, row + 3):
                place = (z * 12 + i) * 24 + start
                pieces.append(tokens[place : place + 6])
        return jnp.concatenate(pieces, axis=0)

    def grad_quadrant(hi, hj):
        pieces = [
            grad_ref[z, hi * 3 + row].astype(f32)[hj * 6 : hj * 6 + 6]
            for z in range(2)
            for row in range(3)
        ]
        return pack(pieces, 48)

    slon_ref[0:112] = pack([token_quadrant(q * 3, 18) for q in range(3)], 112)
    slat_ref[0:112] = pack([token_quadrant(9, q * 6) for q in range(3)], 112)
    sdiag_ref[0:48] = pack([token_quadrant(9, 18)], 48)
    gloc_ref[0:48], gloc_ref[48:96] = halves(grad_quadrant(0, 0))
    slon_ref[112:160], slon_ref[160:208] = halves(grad_quadrant(0, 1))
    slat_ref[112:160], slat_ref[160:208] = halves(grad_quadrant(1, 0))
    sdiag_ref[48:96], sdiag_ref[96:144] = halves(grad_quadrant(1, 1))


def expand(table_ref, base_ref, slot_ref, out_ref, held):
    table = jnp.concatenate([table_ref[:, b, :] for b in range(table_ref.shape[1])], axis=0)
    filler = jnp.zeros((4, ENTRIES), f32)
    pieces = []
    for a in range(12):
        pieces += [table[:, a * ENTRIES : (a + 1) * ENTRIES], filler]
    table = jnp.concatenate(pieces, axis=0)
    high = table.astype(bf16)
    low = (table - high.astype(f32)).astype(bf16)
    swap = swap_rows()
    high, low = mm(swap, high).astype(bf16), mm(swap, low).astype(bf16)
    entry = lax.broadcasted_iota(jnp.int32, (ENTRIES, WIN), 0)
    for column in range(12):
        picker = jnp.where(entry == base_ref[...] + column, 1.0, 0.0).astype(bf16)
        held[:, 0, column] = mm(high, picker).astype(bf16).reshape(12, 16, WIN)
        held[:, 1, column] = mm(low, picker).astype(bf16).reshape(12, 16, WIN)
    once = one_hot(slot_ref[...], 192)
    for h in range(12):
        out_ref[pl.ds(h * WIN, WIN), :] = (
            mm(once, held[h, 0].reshape(192, WIN)) + mm(once, held[h, 1].reshape(192, WIN))
        ) * LOG2E


def bias_kernel(table_ref, base_ref, slot_ref, out_ref, held):
    expand(table_ref, base_ref, slot_ref, out_ref, held)


def coarse_table_kernel(score_ref, base_ref, slot_ref, table_ref, rows_ref):
    table_ref[...] = table_grad(score_ref, base_ref, slot_ref, rows_ref)


def table_sum_kernel(sums_ref, fine_ref, coarse_ref):
    rows = jnp.concatenate([sums_ref[c].astype(f32) for c in range(sums_ref.shape[0])], axis=0)
    for start, out in ((0, fine_ref), (24, coarse_ref)):
        total = jnp.concatenate([rows[start : start + 12], rows[start + 12 : start + 24]], axis=1)
        heads = out.shape[0]
        for b in range(out.shape[1]):
            out[:, b, :] = total[b * heads : (b + 1) * heads]


def fine_kernel(
    tokens_ref, lon_ref, lat_ref, diag_ref, arrive_ref, bias_ref, mask_ref,
    qkv_ref, proj_ref, up_ref, down_ref,
    res_ref, slon_ref, slat_ref, sdiag_ref,
    q_ref, k_ref, v_ref, probs_ref, n1_ref, r1_ref, n2_ref, r2_ref, slope_ref,
    source,
):
    source[0:576] = tokens_ref[...]
    source[576:688] = lon_ref[0:112]
    source[688:800] = lat_ref[0:112]
    source[800:848] = diag_ref[0:48]
    everything = source[...]
    w_qkv = qkv_ref[...]
    bases = []
    for w in range(4):
        rows = pl.ds(w * WIN, WIN)
        base = mm(one_hot(arrive_ref[rows, :], 848), everything)
        normed, scale = norm(base)
        normed = normed.astype(bf16)
        n1_ref[rows, :] = normed
        r1_ref[rows, :] = scale
        q_ref[rows, :] = mm(normed, w_qkv[:, 0:192]).astype(bf16)
        k_ref[rows, :] = mm(normed, w_qkv[:, 192:384]).astype(bf16)
        v_ref[rows, :] = mm(normed, w_qkv[:, 384:576]).astype(bf16)
        bases.append(base)
    windows = []
    for w in range(4):
        rows = pl.ds(w * WIN, WIN)
        mixture = attend(
            q_ref[rows, :], k_ref[rows, :], v_ref[rows, :],
            bias_ref, w // 2 * 6 * WIN, mask_ref[w], probs_ref, w * 6 * WIN,
        ).astype(bf16)
        first = bases[w] + mm(mixture, proj_ref[...])
        renormed, scale = norm(first)
        renormed = renormed.astype(bf16)
        n2_ref[rows, :] = renormed
        r2_ref[rows, :] = scale
        active, slope = gelu_pair(mm(renormed, up_ref[...]))
        slope_ref[rows, :] = slope.astype(bf16)
        result = first + mm(active.astype(bf16), down_ref[...])
        res_ref[rows, :] = result.astype(bf16)
        windows.append(result)
    slon_ref[...] = pack([quadrant(windows, q, 3) for q in range(3)], 112)
    slat_ref[...] = pack([quadrant(windows, 3, q) for q in range(3)], 112)
    sdiag_ref[...] = pack([quadrant(windows, 3, 3)], 48)


def coarse_kernel(
    res_ref, lon_ref, lat_ref, diag_ref, merge_ref, split_ref, bias_ref, mask_ref,
    gloc_ref, glon_ref, glat_ref, gdiag_ref,
    reduce_ref, qkv_ref, proj_ref, up_ref, down_ref,
    c0, c1, c2, c3, dlon_ref, dlat_ref, ddiag_ref, dloc_ref, score_ref,
    source, probs_ref, parts_ref,
):
    source[0:576] = res_ref[...]
    source[576:688] = lon_ref[...]
    source[688:800] = lat_ref[...]
    source[800:848] = diag_ref[...]
    everything = source[...]
    parts = [mm(one_hot(merge_ref[pl.ds(k * WIN, WIN), :], 848), everything) for k in range(4)]
    mean = sum(jnp.sum(part, axis=-1, keepdims=True) for part in parts) * (1.0 / 768)
    parts = [part - mean for part in parts]
    square = sum(jnp.sum(part * part, axis=-1, keepdims=True) for part in parts)
    merge_scale = lax.rsqrt(square * (1.0 / 768) + 1e-5)
    parts = [(part * merge_scale).astype(bf16) for part in parts]
    base = sum(mm(parts[k], reduce_ref[k * 192 : (k + 1) * 192]) for k in range(4))
    base = base.astype(bf16).astype(f32)
    normed, scale1 = norm(base)
    normed = normed.astype(bf16)
    queries = mm(normed, qkv_ref[:, 0:384]).astype(bf16)
    keys = mm(normed, qkv_ref[:, 384:768]).astype(bf16)
    values = mm(normed, qkv_ref[:, 768:1152]).astype(bf16)
    mixture = attend(queries, keys, values, bias_ref, 0, mask_ref[...], probs_ref, 0).astype(bf16)
    first = base + mm(mixture, proj_ref[...])
    renormed, scale2 = norm(first)
    renormed = renormed.astype(bf16)
    active, slope = gelu_pair(mm(renormed, up_ref[...]))
    result = first + mm(active.astype(bf16), down_ref[...])
    for index, out in enumerate((c0, c1, c2, c3)):
        piece = pack([result[index * QUAD : (index + 1) * QUAD]], 48)
        out[0:48], out[48:96] = halves(piece)

    pieces = []
    for ref, start in ((gdiag_ref, 48), (glat_ref, 112), (glon_ref, 112), (gloc_ref, 0)):
        both = [ref[start : start + 48], ref[start + 48 : start + 96]]
        pieces.append(jnp.concatenate([half.astype(f32)[:QUAD] for half in both], axis=1))
    grad = jnp.concatenate(pieces, axis=0)
    inner = mm_nt(grad.astype(bf16), down_ref[...]) * slope
    grad = grad + norm_back(mm_nt(inner.astype(bf16), up_ref[...]), renormed.astype(f32), scale2)
    mix_grad = mm_nt(grad.astype(bf16), proj_ref[...]).astype(bf16)
    dq, dk, dv = attend_back(queries, keys, values, mix_grad, probs_ref, 0, score_ref, False)
    normed_grad = (
        mm_nt(dq.astype(bf16), qkv_ref[:, 0:384])
        + mm_nt(dk.astype(bf16), qkv_ref[:, 384:768])
        + mm_nt(dv.astype(bf16), qkv_ref[:, 768:1152])
    )
    grad = grad + norm_back(normed_grad, normed.astype(f32), scale1)
    grad = grad.astype(bf16)
    grads = [mm_nt(grad, reduce_ref[k * 192 : (k + 1) * 192]) for k in range(4)]
    mean = sum(jnp.sum(g, axis=-1, keepdims=True) for g in grads) * (1.0 / 768)
    along = sum(
        jnp.sum(g * p.astype(f32), axis=-1, keepdims=True) for g, p in zip(grads, parts)
    ) * (1.0 / 768)
    for k in range(4):
        part = (grads[k] - mean - parts[k].astype(f32) * along) * merge_scale
        parts_ref[pl.ds(k * WIN, WIN), :] = part.astype(bf16)
    everything = parts_ref[...]
    moved = mm(one_hot(split_ref[...], 576), everything).astype(bf16)
    dlon_ref[...] = moved[0:112]
    dlat_ref[...] = moved[112:224]
    ddiag_ref[...] = moved[224:272]
    dloc_ref[...] = moved[272:608]


def fine_back_kernel(
    dlon_ref, dlat_ref, ddiag_ref, dloc_ref, back_ref,
    q_ref, k_ref, v_ref, probs_ref, n2_ref, r2_ref, slope_ref,
    proj_ref, up_ref, down_ref, base_ref, slot_ref, coarse_table_ref,
    grad_ref, dq_ref, dk_ref, dv_ref, table_ref,
    source, score_ref, rows_ref,
):
    source[0:112] = dlon_ref[...]
    source[112:224] = dlat_ref[...]
    source[224:272] = ddiag_ref[...]
    source[272:608] = dloc_ref[...]
    everything = source[...]
    for w in range(4):
        rows = pl.ds(w * WIN, WIN)
        grad = mm(one_hot(back_ref[rows, :], 608), everything)
        inner = mm_nt(grad.astype(bf16), down_ref[...]) * slope_ref[rows, :].astype(f32)
        grad = grad + norm_back(
            mm_nt(inner.astype(bf16), up_ref[...]), n2_ref[rows, :].astype(f32), r2_ref[rows, :]
        )
        grad_ref[rows, :] = grad
        mix_grad = mm_nt(grad.astype(bf16), proj_ref[...]).astype(bf16)
        dq, dk, dv = attend_back(
            q_ref[rows, :], k_ref[rows, :], v_ref[rows, :], mix_grad,
            probs_ref, w * 6 * WIN,
            score_ref.at[pl.ds(w // 2 * 6 * WIN, 6 * WIN)], w % 2 == 1,
        )
        dq_ref[rows, :] = dq.astype(bf16)
        dk_ref[rows, :] = dk.astype(bf16)
        dv_ref[rows, :] = dv.astype(bf16)
    tables = [table_grad(score_ref, base_ref, slot_ref, rows_ref), coarse_table_ref[...]]
    rows = jnp.concatenate([part.astype(f32) for part in tables], axis=0)
    count = table_ref.shape[1]
    for chunk in range(table_ref.shape[0]):
        table_ref[chunk] = rows[chunk * count : (chunk + 1) * count].astype(bf16)


def qkv_back_kernel(
    grad_ref, dq_ref, dk_ref, dv_ref, n1_ref, r1_ref, qkv_ref, clon_ref, clat_ref, cdiag_ref,
    res_ref, slon_ref, slat_ref, sdiag_ref,
):
    w_qkv = qkv_ref[...]
    windows = []
    for w in range(4):
        rows = pl.ds(w * WIN, WIN)
        normed_grad = (
            mm_nt(dq_ref[rows, :], w_qkv[:, 0:192])
            + mm_nt(dk_ref[rows, :], w_qkv[:, 192:384])
            + mm_nt(dv_ref[rows, :], w_qkv[:, 384:576])
        )
        result = grad_ref[rows, :] + norm_back(
            normed_grad, n1_ref[rows, :].astype(f32), r1_ref[rows, :]
        )
        res_ref[rows, :] = result.astype(bf16)
        windows.append(result)
    slon_ref[0:112] = pack([quadrant(windows, q, 0) for q in range(1, 4)], 112)
    slat_ref[0:112] = pack([quadrant(windows, 0, q) for q in range(1, 4)], 112)
    sdiag_ref[0:48] = pack([quadrant(windows, 0, 0)], 48)
    slon_ref[112:208] = clon_ref[...]
    slat_ref[112:208] = clat_ref[...]
    sdiag_ref[48:144] = cdiag_ref[...]


def last_kernel(
    res_ref, lon_ref, lat_ref, diag_ref, leave_ref, cloc_ref, result_ref,
    tokens_ref, coarse_ref, source, coarse_source,
):
    source[0:576] = res_ref[...]
    source[576:688] = lon_ref[0:112]
    source[688:800] = lat_ref[0:112]
    source[800:848] = diag_ref[0:48]
    everything = source[...]
    for w in range(4):
        rows = pl.ds(w * WIN, WIN)
        tokens_ref[rows, :] = mm(one_hot(leave_ref[rows, :], 848), everything).astype(bf16)
    picks = one_hot(result_ref[...], 192)
    moved = []
    for half in (0, 48):
        coarse_source[0:48] = cloc_ref[half : half + 48]
        coarse_source[48:96] = lon_ref[112 + half : 160 + half]
        coarse_source[96:144] = lat_ref[112 + half : 160 + half]
        coarse_source[144:192] = diag_ref[48 + half : 96 + half]
        moved.append(mm(picks, coarse_source[...]))
    moved = jnp.concatenate(moved, axis=1)
    for z in range(2):
        for row in range(6):
            start = z * 72 + row * 12
            coarse_ref[z, row] = moved[start : start + 12].astype(bf16)


def run(kernel, outs, scratch, weight, inputs):
    shapes = [jax.ShapeDtypeStruct(shape, kind) for shape, kind in outs]
    size = sum(math.prod(s.shape) * s.dtype.itemsize for s in shapes)
    size += sum(x.size * x.dtype.itemsize for x in inputs)
    return pl.pallas_call(
        kernel,
        out_shape=shapes,
        scratch_shapes=[pltpu.VMEM(shape, kind) for shape, kind in scratch],
        compiler_params=pltpu.CompilerParams(vmem_limit_bytes=VMEM),
        cost_estimate=pl.CostEstimate(
            flops=weight * 1_000_000_000, bytes_accessed=size, transcendentals=0
        ),
    )(*inputs)


def move(value, lon_steps, lat_steps):
    lon, lat = lax.axis_size("lon"), lax.axis_size("lat")
    if lat_steps == 0:
        pairs = [(s, (s + lon_steps) % lon) for s in range(lon)]
        return lax.ppermute(value, "lon", pairs)
    if lon_steps == 0:
        pairs = [(s, (s + lat_steps) % lat) for s in range(lat)]
        return lax.ppermute(value, "lat", pairs)
    pairs = [
        (b * lat + a, (b + lon_steps) % lon * lat + (a + lat_steps) % lat)
        for b in range(lon)
        for a in range(lat)
    ]
    return lax.ppermute(value, ("lon", "lat"), pairs)


def send(pieces, steps):
    on_lon, on_lat, on_both = pieces
    return move(on_lon, steps, 0), move(on_lat, 0, steps), move(on_both, steps, steps)


def lon_total(value):
    count = lax.axis_size("lon")
    if value.shape[0] == count:
        parts = lax.all_to_all(value, "lon", 0, 0)
        total = jnp.sum(parts.astype(f32), axis=0, keepdims=True).astype(bf16)
        return lax.all_to_all(jnp.broadcast_to(total, value.shape), "lon", 0, 0)
    step = 1
    while step < count:
        other = lax.ppermute(value, "lon", [(s, s ^ step) for s in range(count)])
        value = (value.astype(f32) + other.astype(f32)).astype(bf16)
        step *= 2
    return value


def body(
    tokens, mask_ids, fine_qkv, fine_proj, fine_up, fine_down, fine_bias, reduce_weight,
    coarse_qkv, coarse_proj, coarse_up, coarse_down, coarse_bias, out_grad,
):
    lat_index = lax.axis_index("lat")
    flat = tokens.reshape(576, 192)
    column = lambda index: jnp.asarray(index).reshape(-1, 1)
    line = lambda index: jnp.asarray(index).reshape(1, -1)
    tok = ((576, 192), bf16)
    edges = [((112, 192), bf16), ((112, 192), bf16), ((48, 192), bf16)]
    wide_edges = [((208, 192), bf16), ((208, 192), bf16), ((144, 192), bf16)]
    quad = ((96, 192), bf16)
    scores = ((12 * WIN, WIN), f32)
    table_rows = ((12, 192, WIN), bf16)
    held = ((12, 2, 12, 16, WIN), bf16)

    *sent, grad_here = run(edge_kernel, wide_edges + [quad], [], 1, (flat, out_grad))
    first = send(sent, 1)
    (fine_table,) = run(
        bias_kernel, [scores], [held], 2,
        (fine_bias.transpose(1, 0, 2), line(BASE), column(ROW_SLOT)),
    )

    labels = mask_ids.reshape(2, 2, 2, 3, 2, 2, 6)
    top = jnp.zeros((2, 2, 1, 1, 1, 1), jnp.int32).at[0, 0].set(1)[None]
    labels = labels * 2 + jnp.where(lat_index == 0, top, 0)
    labels = labels.transpose(1, 4, 2, 5, 0, 3, 6).reshape(4, WIN)
    fine_mask = jnp.where(labels[:, :, None] == labels[:, None, :], 0.0, -1e30).astype(f32)
    low_half = jnp.arange(WIN) < WIN // 2
    coarse_mask = jnp.where(
        (low_half[:, None] == low_half[None, :]) | (lat_index != 0), 0.0, -1e30
    ).astype(f32)

    fine = run(
        fine_kernel,
        [tok] + edges
        + [tok] * 3
        + [((24 * WIN, WIN), bf16), tok, ((576, 1), f32), tok, ((576, 1), f32), ((576, 768), bf16)],
        [((848, 192), bf16)],
        8,
        (flat, *first, column(ARRIVE), fine_table, fine_mask, fine_qkv, fine_proj, fine_up, fine_down),
    )
    q, k, v, probs, n1, r1, n2, r2, slope = fine[4:]
    arrived = send(fine[1:4], 1)
    late_table, _ = lax.optimization_barrier((coarse_bias.transpose(1, 0, 2), fine[1]))
    (coarse_table,) = run(
        bias_kernel, [scores], [held], 2, (late_table, line(BASE), column(ROW_SLOT))
    )
    coarse = run(
        coarse_kernel,
        [quad] * 4 + edges + [((336, 192), bf16), scores],
        [((848, 192), bf16), ((12 * WIN, WIN), bf16), ((576, 192), bf16)],
        9,
        (
            fine[0], *arrived, column(MERGE), column(SPLIT), coarse_table, coarse_mask, grad_here, *first,
            reduce_weight, coarse_qkv, coarse_proj, coarse_up, coarse_down,
        ),
    )
    c00, c01, c10, c11 = coarse[:4]
    arrived = send(coarse[4:7], -1)
    (coarse_grad,) = run(
        coarse_table_kernel, [((24, 6 * ENTRIES), bf16)], [table_rows], 2,
        (coarse[8], column(BASE), line(ROW_SLOT)),
    )
    chunks = 8 if lax.axis_size("lon") == 8 else 1
    *passed, tables = run(
        fine_back_kernel,
        [((576, 192), f32)] + [tok] * 3 + [((chunks, 48 // chunks, 6 * ENTRIES), bf16)],
        [((608, 192), bf16), scores, table_rows],
        7,
        (
            *arrived, coarse[7], column(BACK), q, k, v, probs, n2, r2, slope,
            fine_proj, fine_up, fine_down, column(BASE), line(ROW_SLOT), coarse_grad,
        ),
    )
    sums = lon_total(tables)
    fine_back = run(
        qkv_back_kernel, [tok] + wide_edges, [], 2,
        (*passed, n1, r1, fine_qkv, c10, c01, c00),
    )
    arrived = send(fine_back[1:4], -1)
    d_tokens, coarse_result = run(
        last_kernel,
        [tok, ((2, 6, 12, 384), bf16)],
        [((848, 192), bf16), ((192, 192), bf16)],
        1,
        (fine_back[0], *arrived, column(LEAVE), c11, column(RESULT)),
    )
    fine_out, coarse_out = run(
        table_sum_kernel,
        [((HEADS_F, 2, 12 * ENTRIES), f32), ((HEADS_C, 1, 12 * ENTRIES), f32)],
        [], 1, (sums,),
    )
    return (
        coarse_result,
        d_tokens.reshape(tokens.shape),
        fine_out.transpose(1, 0, 2),
        coarse_out.transpose(1, 0, 2),
    )


def solution(mesh):
    grid = P(None, "lat", "lon", None)
    bands = P("lat", None, None)
    in_specs = (
        grid, P(None, "lat", "lon"), P(), P(), P(), P(), bands,
        P(), P(), P(), P(), P(), bands, grid,
    )
    out_specs = (grid, grid, bands, bands)
    return jax.shard_map(body, mesh=mesh, in_specs=in_specs, out_specs=out_specs, check_vma=False)
```

```python
import math

import jax
import jax.numpy as jnp
import numpy as np
from jax import lax
from jax.experimental import pallas as pl
from jax.experimental.pallas import tpu as pltpu
from jax.sharding import PartitionSpec as P

HEADS_F = 6
HEADS_C = 12
HEAD = 32
WIN = 144
QUAD = 36
SPAN = 23
ENTRIES = 276
LOG2E = math.log2(math.e)
VMEM = 20 * 1024 * 1024
f32 = jnp.float32
bf16 = jnp.bfloat16


def spot(z, i, j):
    quadrant = (i % 6) // 3 * 2 + (j % 12) // 6
    return quadrant * QUAD + z * 18 + i % 3 * 6 + j % 6


def fine_spot(z, i, j):
    return (i // 6 * 2 + j // 12) * WIN + spot(z, i, j)


def in_quad(z, i, j):
    return z * 18 + i % 3 * 6 + j % 6


def index_maps():
    arrive = np.zeros(576, np.int32)
    merge = np.zeros(576, np.int32)
    split = np.full(608, -1, np.int32)
    back = np.zeros(576, np.int32)
    leave = np.zeros(576, np.int32)
    for z in range(2):
        for i in range(12):
            for j in range(24):
                here = fine_spot(z, i, j)
                if i >= 3 and j >= 6:
                    arrive[here] = z * 288 + (i - 3) * 24 + j - 6
                    came = fine_spot(z, i - 3, j - 6)
                elif i >= 3:
                    came = 576 + (i - 3) // 3 * QUAD + in_quad(z, i, j)
                elif j >= 6:
                    came = 688 + (j - 6) // 6 * QUAD + in_quad(z, i, j)
                else:
                    came = 800 + in_quad(z, i, j)
                if came >= 576:
                    arrive[here] = came
                part = (i % 2 + j % 2 * 2) * WIN + spot(z, i // 2, j // 2)
                merge[part] = came
                if i >= 3 and j >= 6:
                    slot = 112 + z * 162 + (i - 3) * 18 + j - 6
                    back[fine_spot(z, i - 3, j - 6)] = slot
                elif i >= 3:
                    slot = z * 54 + (i - 3) * 6 + j
                    back[fine_spot(z, i - 3, j + 18)] = slot
                elif j >= 6:
                    slot = 448 + z * 54 + i * 18 + j - 6
                    back[fine_spot(z, i + 9, j - 6)] = slot
                else:
                    slot = 560 + z * 18 + i * 6 + j
                    back[fine_spot(z, i + 9, j + 18)] = slot
                split[slot] = part
                natural = z * 288 + i * 24 + j
                if i < 9 and j < 18:
                    leave[natural] = fine_spot(z, i + 3, j + 6)
                elif i < 9:
                    leave[natural] = 576 + i // 3 * QUAD + in_quad(z, i, j)
                elif j < 18:
                    leave[natural] = 688 + j // 6 * QUAD + in_quad(z, i, j)
                else:
                    leave[natural] = 800 + in_quad(z, i, j)
    result = np.zeros(WIN, np.int32)
    base = np.zeros(WIN, np.int32)
    row_slot = np.zeros(WIN, np.int32)
    for z in range(2):
        for i in range(6):
            for j in range(12):
                result[z * 72 + i * 12 + j] = (i // 3 * 2 + j // 6) * 48 + in_quad(z, i, j)
                here = spot(z, i, j)
                base[here] = (z * 6 + i) * SPAN + 11 - j
                row_slot[here] = j * 16 + z * 6 + i
    return arrive, merge, split, back, leave, result, base, row_slot


ARRIVE, MERGE, SPLIT, BACK, LEAVE, RESULT, BASE, ROW_SLOT = index_maps()


def one_hot(column, width):
    spots = lax.broadcasted_iota(jnp.int32, (column.shape[0], width), 1)
    return jnp.where(spots == column, 1.0, 0.0).astype(bf16)


def mm(left, right):
    return jnp.dot(left, right, preferred_element_type=f32)


def mm_nt(left, right):
    return lax.dot_general(left, right, (((1,), (1,)), ((), ())), preferred_element_type=f32)


def mm_tn(left, right):
    return lax.dot_general(left, right, (((0,), (0,)), ((), ())), preferred_element_type=f32)


def norm(values):
    centred = values - jnp.mean(values, axis=-1, keepdims=True)
    scale = lax.rsqrt(jnp.mean(centred * centred, axis=-1, keepdims=True) + 1e-5)
    return centred * scale, scale


def norm_back(grad, normed, scale):
    along = jnp.mean(grad * normed, axis=-1, keepdims=True)
    return (grad - jnp.mean(grad, axis=-1, keepdims=True) - normed * along) * scale


def gelu_pair(x):
    u = jnp.abs(x) * math.sqrt(0.5)
    t = 1.0 / (1.0 + 0.3275911 * u)
    e = jnp.exp(-u * u)
    poly = 1.421413741 + t * (-1.453152027 + t * 1.061405429)
    tail = 0.5 * (t * (0.254829592 + t * (-0.284496736 + t * poly))) * e
    below = jnp.where(x >= 0, 1.0 - tail, tail)
    return x * below, below + x * (e * (1.0 / math.sqrt(2 * math.pi)))


def groups(channels):
    return [(start, min(start + 128, channels)) for start in range(0, channels, 128)]


def head_lanes(rows, width):
    return lax.broadcasted_iota(jnp.int32, (rows, width), 1) // HEAD


def stack_heads(part):
    lanes = head_lanes(part.shape[0], part.shape[1])
    count = part.shape[1] // HEAD
    zero = jnp.zeros_like(part)
    return jnp.concatenate([jnp.where(lanes == h, part, zero) for h in range(count)], axis=0)


def pick_heads(stacked):
    width = stacked.shape[1]
    lanes = head_lanes(WIN, width)
    total = stacked[:WIN]
    for h in range(1, width // HEAD):
        total = jnp.where(lanes == h, stacked[h * WIN : (h + 1) * WIN], total)
    return total


def attend(queries, keys, values, bias_ref, bias_row, mask, probs_ref, probs_row):
    mixed = []
    for start, stop in groups(queries.shape[1]):
        count = (stop - start) // HEAD
        scores = mm_nt(stack_heads(queries[:, start:stop]), keys[:, start:stop])
        row = start // HEAD * WIN
        for h in range(count):
            here = row + h * WIN
            logits = (
                scores[h * WIN : (h + 1) * WIN] * (HEAD**-0.5 * LOG2E)
                + bias_ref[pl.ds(bias_row + here, WIN), :]
                + mask
            )
            raised = jnp.exp2(logits - jnp.max(logits, axis=-1, keepdims=True))
            probs = raised * (1.0 / jnp.sum(raised, axis=-1, keepdims=True))
            probs_ref[pl.ds(probs_row + here, WIN), :] = probs.astype(bf16)
        stacked = mm(probs_ref[pl.ds(probs_row + row, count * WIN), :], values[:, start:stop])
        mixed.append(pick_heads(stacked))
    return jnp.concatenate(mixed, axis=1)


def attend_back(queries, keys, values, mix_grad, probs_ref, probs_row, score_ref, add):
    query_grad, key_grad, value_grad = [], [], []
    for start, stop in groups(queries.shape[1]):
        count = (stop - start) // HEAD
        row = start // HEAD * WIN
        probs_all = probs_ref[pl.ds(probs_row + row, count * WIN), :]
        grads = stack_heads(mix_grad[:, start:stop])
        value_grad.append(mm_tn(probs_all, grads))
        probs_grad = mm_nt(grads, values[:, start:stop])
        pieces = []
        for h in range(count):
            probs = probs_all[h * WIN : (h + 1) * WIN].astype(f32)
            grad = probs_grad[h * WIN : (h + 1) * WIN]
            weighted = grad * probs
            score_grad = weighted - probs * jnp.sum(weighted, axis=-1, keepdims=True)
            place = pl.ds(row + h * WIN, WIN)
            if add:
                score_ref[place, :] += score_grad
            else:
                score_ref[place, :] = score_grad
            pieces.append(score_grad.astype(bf16))
        score_all = jnp.concatenate(pieces, axis=0)
        query_grad.append(pick_heads(mm(score_all, keys[:, start:stop])))
        key_grad.append(mm_tn(score_all, stack_heads(queries[:, start:stop])))
    scale = HEAD**-0.5
    return (
        jnp.concatenate(query_grad, axis=1) * scale,
        jnp.concatenate(key_grad, axis=1) * scale,
        jnp.concatenate(value_grad, axis=1),
    )


def swap_rows():
    row = lax.broadcasted_iota(jnp.int32, (192, 192), 0)
    return jnp.where(
        lax.broadcasted_iota(jnp.int32, (192, 192), 1) == row % 16 * 16 + row // 16, 1.0, 0.0
    ).astype(bf16)


def table_grad(score_ref, base_ref, slot_ref, rows_ref):
    regroup = jnp.where(
        lax.broadcasted_iota(jnp.int32, (192, WIN), 0) == slot_ref[...], 1.0, 0.0
    ).astype(bf16)
    for h in range(12):
        moved = mm(regroup, score_ref[pl.ds(h * WIN, WIN), :].astype(bf16)).astype(bf16)
        rows_ref[:, pl.ds(h * 16, 16), :] = moved.reshape(12, 16, WIN)
    total = jnp.zeros((192, ENTRIES), f32)
    for column in range(12):
        total += mm(rows_ref[column], one_hot(base_ref[...] + column, ENTRIES))
    swapped = mm(swap_rows(), total.astype(bf16))
    halves = [
        jnp.concatenate([swapped[a * 16 : a * 16 + 12] for a in range(start, start + 6)], axis=1)
        for start in (0, 6)
    ]
    return jnp.concatenate(halves, axis=0).astype(bf16)


def pack(pieces, rows):
    count = sum(piece.shape[0] for piece in pieces)
    if rows > count:
        pieces = pieces + [jnp.zeros((rows - count, pieces[0].shape[1]), f32)]
    return jnp.concatenate(pieces, axis=0).astype(bf16)


def quadrant(windows, qi, qj):
    part = (qi % 2 * 2 + qj % 2) * QUAD
    return windows[qi // 2 * 2 + qj // 2][part : part + QUAD]


def halves(values):
    return [values[:, 0:192], values[:, 192:384]]


def edge_kernel(
    tokens_hbm, grad_hbm, slon_ref, slat_ref, sdiag_ref, gloc_ref, tokens_ref, grad_ref, done
):
    copies = [
        pltpu.make_async_copy(tokens_hbm, tokens_ref, done.at[0]),
        pltpu.make_async_copy(grad_hbm, grad_ref, done.at[1]),
    ]
    for copy in copies:
        copy.start()
    for copy in copies:
        copy.wait()
    tokens = tokens_ref[...].astype(f32)
    grads = grad_ref[...].astype(f32)

    def token_quadrant(row, start):
        pieces = []
        for z in range(2):
            for i in range(row, row + 3):
                place = (z * 12 + i) * 24 + start
                pieces.append(tokens[place : place + 6])
        return jnp.concatenate(pieces, axis=0)

    def grad_quadrant(hi, hj):
        pieces = [
            grads[hi * 3 + row, hj * 6 : hj * 6 + 6, z]
            for z in range(2)
            for row in range(3)
        ]
        return pack(pieces, 48)

    slon_ref[0:112] = pack([token_quadrant(q * 3, 18) for q in range(3)], 112)
    slat_ref[0:112] = pack([token_quadrant(9, q * 6) for q in range(3)], 112)
    sdiag_ref[0:48] = pack([token_quadrant(9, 18)], 48)
    gloc_ref[0:48], gloc_ref[48:96] = halves(grad_quadrant(0, 0))
    slon_ref[112:160], slon_ref[160:208] = halves(grad_quadrant(0, 1))
    slat_ref[112:160], slat_ref[160:208] = halves(grad_quadrant(1, 0))
    sdiag_ref[48:96], sdiag_ref[96:144] = halves(grad_quadrant(1, 1))


def expand(table_ref, base_ref, slot_ref, out_ref, held):
    table = jnp.concatenate([table_ref[:, b, :] for b in range(table_ref.shape[1])], axis=0)
    filler = jnp.zeros((4, ENTRIES), f32)
    pieces = []
    for a in range(12):
        pieces += [table[:, a * ENTRIES : (a + 1) * ENTRIES], filler]
    table = jnp.concatenate(pieces, axis=0)
    high = table.astype(bf16)
    low = (table - high.astype(f32)).astype(bf16)
    swap = swap_rows()
    table = jnp.concatenate(
        [mm(swap, high).astype(bf16), mm(swap, low).astype(bf16)], axis=0
    )
    entry = lax.broadcasted_iota(jnp.int32, (ENTRIES, WIN), 0)
    for column in range(12):
        picker = jnp.where(entry == base_ref[...] + column, 1.0, 0.0).astype(bf16)
        picked = mm(table, picker).astype(bf16)
        held[:, 0, column] = picked[0:192].reshape(12, 16, WIN)
        held[:, 1, column] = picked[192:384].reshape(12, 16, WIN)
    spots = lax.broadcasted_iota(jnp.int32, (WIN, 384), 1)
    spots = jnp.where(spots >= 192, spots - 192, spots)
    twice = jnp.where(spots == slot_ref[...], 1.0, 0.0).astype(bf16)
    for h in range(12):
        out_ref[pl.ds(h * WIN, WIN), :] = mm(twice, held[h].reshape(384, WIN)) * LOG2E


def bias_kernel(table_ref, base_ref, slot_ref, out_ref, held):
    expand(table_ref, base_ref, slot_ref, out_ref, held)


def coarse_table_kernel(score_ref, base_ref, slot_ref, table_ref, rows_ref):
    table_ref[...] = table_grad(score_ref, base_ref, slot_ref, rows_ref)


def table_sum_kernel(kept_ref, other_ref, out_ref):
    total = kept_ref[...].astype(f32) + other_ref[...].astype(f32)
    total = jnp.concatenate([total[0:12], total[12:24]], axis=1)
    heads = out_ref.shape[0]
    for b in range(out_ref.shape[1]):
        out_ref[:, b, :] = total[b * heads : (b + 1) * heads]


def fine_kernel(
    tokens_ref, lon_ref, lat_ref, diag_ref, arrive_ref, bias_ref, mask_ref,
    qkv_ref, proj_ref, up_ref, down_ref,
    res_ref, slon_ref, slat_ref, sdiag_ref,
    q_ref, k_ref, v_ref, probs_ref, n1_ref, r1_ref, n2_ref, r2_ref, slope_ref,
    source,
):
    source[0:576] = tokens_ref[...]
    source[576:688] = lon_ref[0:112]
    source[688:800] = lat_ref[0:112]
    source[800:848] = diag_ref[0:48]
    everything = source[...]
    w_qkv = qkv_ref[...]
    bases = []
    for w in range(4):
        rows = pl.ds(w * WIN, WIN)
        base = mm(one_hot(arrive_ref[rows, :], 848), everything)
        normed, scale = norm(base)
        normed = normed.astype(bf16)
        n1_ref[rows, :] = normed
        r1_ref[rows, :] = scale
        q_ref[rows, :] = mm(normed, w_qkv[:, 0:192]).astype(bf16)
        k_ref[rows, :] = mm(normed, w_qkv[:, 192:384]).astype(bf16)
        v_ref[rows, :] = mm(normed, w_qkv[:, 384:576]).astype(bf16)
        bases.append(base)
    windows = []
    for w in range(4):
        rows = pl.ds(w * WIN, WIN)
        mixture = attend(
            q_ref[rows, :], k_ref[rows, :], v_ref[rows, :],
            bias_ref, w // 2 * 6 * WIN, mask_ref[w], probs_ref, w * 6 * WIN,
        ).astype(bf16)
        first = bases[w] + mm(mixture, proj_ref[...])
        renormed, scale = norm(first)
        renormed = renormed.astype(bf16)
        n2_ref[rows, :] = renormed
        r2_ref[rows, :] = scale
        active, slope = gelu_pair(mm(renormed, up_ref[...]))
        slope_ref[rows, :] = slope.astype(bf16)
        result = first + mm_nt(active.astype(bf16), down_ref[...])
        res_ref[rows, :] = result.astype(bf16)
        windows.append(result)
    slon_ref[...] = pack([quadrant(windows, q, 3) for q in range(3)], 112)
    slat_ref[...] = pack([quadrant(windows, 3, q) for q in range(3)], 112)
    sdiag_ref[...] = pack([quadrant(windows, 3, 3)], 48)


def coarse_kernel(
    res_ref, lon_ref, lat_ref, diag_ref, merge_ref, split_ref, bias_ref, mask_ref,
    gloc_ref, glon_ref, glat_ref, gdiag_ref,
    reduce_ref, qkv_ref, proj_ref, up_ref, down_ref,
    c0, c1, c2, c3, dlon_ref, dlat_ref, ddiag_ref, dloc_ref, score_ref,
    source, probs_ref, parts_ref,
):
    source[0:576] = res_ref[...]
    source[576:688] = lon_ref[...]
    source[688:800] = lat_ref[...]
    source[800:848] = diag_ref[...]
    everything = source[...]
    parts = [mm(one_hot(merge_ref[pl.ds(k * WIN, WIN), :], 848), everything) for k in range(4)]
    mean = sum(jnp.sum(part, axis=-1, keepdims=True) for part in parts) * (1.0 / 768)
    parts = [part - mean for part in parts]
    square = sum(jnp.sum(part * part, axis=-1, keepdims=True) for part in parts)
    merge_scale = lax.rsqrt(square * (1.0 / 768) + 1e-5)
    parts = [(part * merge_scale).astype(bf16) for part in parts]
    base = sum(mm(parts[k], reduce_ref[k * 192 : (k + 1) * 192]) for k in range(4))
    base = base.astype(bf16).astype(f32)
    normed, scale1 = norm(base)
    normed = normed.astype(bf16)
    queries = mm(normed, qkv_ref[:, 0:384]).astype(bf16)
    keys = mm(normed, qkv_ref[:, 384:768]).astype(bf16)
    values = mm(normed, qkv_ref[:, 768:1152]).astype(bf16)
    mixture = attend(queries, keys, values, bias_ref, 0, mask_ref[...], probs_ref, 0).astype(bf16)
    first = base + mm(mixture, proj_ref[...])
    renormed, scale2 = norm(first)
    renormed = renormed.astype(bf16)
    active, slope = gelu_pair(mm(renormed, up_ref[...]))
    result = first + mm(active.astype(bf16), down_ref[...])
    for index, out in enumerate((c0, c1, c2, c3)):
        piece = pack([result[index * QUAD : (index + 1) * QUAD]], 48)
        out[0:48], out[48:96] = halves(piece)

    pieces = []
    for ref, start in ((gdiag_ref, 48), (glat_ref, 112), (glon_ref, 112), (gloc_ref, 0)):
        both = [ref[start : start + 48], ref[start + 48 : start + 96]]
        pieces.append(jnp.concatenate([half.astype(f32)[:QUAD] for half in both], axis=1))
    grad = jnp.concatenate(pieces, axis=0)
    inner = mm_nt(grad.astype(bf16), down_ref[...]) * slope
    grad = grad + norm_back(mm_nt(inner.astype(bf16), up_ref[...]), renormed.astype(f32), scale2)
    mix_grad = mm_nt(grad.astype(bf16), proj_ref[...]).astype(bf16)
    dq, dk, dv = attend_back(queries, keys, values, mix_grad, probs_ref, 0, score_ref, False)
    normed_grad = (
        mm_nt(dq.astype(bf16), qkv_ref[:, 0:384])
        + mm_nt(dk.astype(bf16), qkv_ref[:, 384:768])
        + mm_nt(dv.astype(bf16), qkv_ref[:, 768:1152])
    )
    grad = grad + norm_back(normed_grad, normed.astype(f32), scale1)
    grad = grad.astype(bf16)
    grads = [mm_nt(grad, reduce_ref[k * 192 : (k + 1) * 192]) for k in range(4)]
    mean = sum(jnp.sum(g, axis=-1, keepdims=True) for g in grads) * (1.0 / 768)
    along = sum(
        jnp.sum(g * p.astype(f32), axis=-1, keepdims=True) for g, p in zip(grads, parts)
    ) * (1.0 / 768)
    for k in range(4):
        part = (grads[k] - mean - parts[k].astype(f32) * along) * merge_scale
        parts_ref[pl.ds(k * WIN, WIN), :] = part.astype(bf16)
    everything = parts_ref[...]
    moved = mm(one_hot(split_ref[...], 576), everything).astype(bf16)
    dlon_ref[...] = moved[0:112]
    dloc_ref[...] = moved[112:448]
    dlat_ref[...] = moved[448:560]
    ddiag_ref[...] = moved[560:608]


def band_back(band, source, back_ref, saved, weights, outs, score_ref):
    q_ref, k_ref, v_ref, probs_ref, n2_ref, r2_ref, slope_ref = saved
    proj_ref, up_ref, down_ref = weights
    grad_ref, dq_ref, dk_ref, dv_ref = outs
    everything = source[...]
    for across in range(2):
        w = band * 2 + across
        rows = pl.ds(w * WIN, WIN)
        here = pl.ds(across * WIN, WIN)
        grad = mm(one_hot(back_ref[rows, :], everything.shape[0]), everything)
        inner = mm(grad.astype(bf16), down_ref[...]) * slope_ref[rows, :].astype(f32)
        grad = grad + norm_back(
            mm_nt(inner.astype(bf16), up_ref[...]), n2_ref[rows, :].astype(f32), r2_ref[rows, :]
        )
        grad_ref[here, :] = grad
        mix_grad = mm_nt(grad.astype(bf16), proj_ref[...]).astype(bf16)
        dq, dk, dv = attend_back(
            q_ref[rows, :], k_ref[rows, :], v_ref[rows, :], mix_grad,
            probs_ref, w * 6 * WIN, score_ref, across == 1,
        )
        dq_ref[here, :] = dq.astype(bf16)
        dk_ref[here, :] = dk.astype(bf16)
        dv_ref[here, :] = dv.astype(bf16)


def first_band_kernel(dlon_ref, dloc_ref, back_ref, *refs):
    *refs, source = refs
    source[0:112] = dlon_ref[...]
    source[112:448] = dloc_ref[...]
    band_back(0, source, back_ref, refs[:7], refs[7:10], refs[10:14], refs[14])


def second_band_kernel(
    dlon_ref, dloc_ref, dlat_ref, ddiag_ref, back_ref, first_ref, base_ref, slot_ref, *refs
):
    *refs, source, score_ref, rows_ref = refs
    source[0:112] = dlon_ref[...]
    source[112:448] = dloc_ref[...]
    source[448:560] = dlat_ref[...]
    source[560:608] = ddiag_ref[...]
    half = 6 * WIN
    score_ref[pl.ds(0, half), :] = first_ref[...]
    band_back(
        1, source, back_ref, refs[:7], refs[7:10], refs[10:14], score_ref.at[pl.ds(half, half)]
    )
    refs[14][...] = table_grad(score_ref, base_ref, slot_ref, rows_ref)


def qkv_back_kernel(*refs):
    bands, refs = (refs[:4], refs[4:8]), refs[8:]
    n1_ref, r1_ref, qkv_ref, clon_ref, clat_ref, cdiag_ref = refs[:6]
    res_ref, slon_ref, slat_ref, sdiag_ref = refs[6:]
    w_qkv = qkv_ref[...]
    windows = []
    for w in range(4):
        grad_ref, dq_ref, dk_ref, dv_ref = bands[w // 2]
        rows = pl.ds(w * WIN, WIN)
        here = pl.ds(w % 2 * WIN, WIN)
        normed_grad = (
            mm_nt(dq_ref[here, :], w_qkv[:, 0:192])
            + mm_nt(dk_ref[here, :], w_qkv[:, 192:384])
            + mm_nt(dv_ref[here, :], w_qkv[:, 384:576])
        )
        result = grad_ref[here, :] + norm_back(
            normed_grad, n1_ref[rows, :].astype(f32), r1_ref[rows, :]
        )
        res_ref[rows, :] = result.astype(bf16)
        windows.append(result)
    slon_ref[0:112] = pack([quadrant(windows, q, 0) for q in range(1, 4)], 112)
    slat_ref[0:112] = pack([quadrant(windows, 0, q) for q in range(1, 4)], 112)
    sdiag_ref[0:48] = pack([quadrant(windows, 0, 0)], 48)
    slon_ref[112:208] = clon_ref[...]
    slat_ref[112:208] = clat_ref[...]
    sdiag_ref[48:144] = cdiag_ref[...]


def last_kernel(
    res_ref, lon_ref, lat_ref, diag_ref, leave_ref, cloc_ref, result_ref,
    tokens_ref, coarse_ref, source, coarse_source,
):
    source[0:576] = res_ref[...]
    source[576:688] = lon_ref[0:112]
    source[688:800] = lat_ref[0:112]
    source[800:848] = diag_ref[0:48]
    everything = source[...]
    for w in range(4):
        rows = pl.ds(w * WIN, WIN)
        tokens_ref[rows, :] = mm(one_hot(leave_ref[rows, :], 848), everything).astype(bf16)
    picks = one_hot(result_ref[...], 192)
    moved = []
    for half in (0, 48):
        coarse_source[0:48] = cloc_ref[half : half + 48]
        coarse_source[48:96] = lon_ref[112 + half : 160 + half]
        coarse_source[96:144] = lat_ref[112 + half : 160 + half]
        coarse_source[144:192] = diag_ref[48 + half : 96 + half]
        moved.append(mm(picks, coarse_source[...]))
    moved = jnp.concatenate(moved, axis=1)
    for z in range(2):
        for row in range(6):
            start = z * 72 + row * 12
            coarse_ref[z, row] = moved[start : start + 12].astype(bf16)


def run(kernel, outs, scratch, weight, inputs):
    shapes = [jax.ShapeDtypeStruct(shape, kind) for shape, kind in outs]
    size = sum(math.prod(s.shape) * s.dtype.itemsize for s in shapes)
    size += sum(x.size * x.dtype.itemsize for x in inputs)
    return pl.pallas_call(
        kernel,
        out_shape=shapes,
        scratch_shapes=[pltpu.VMEM(shape, kind) for shape, kind in scratch],
        compiler_params=pltpu.CompilerParams(vmem_limit_bytes=VMEM),
        cost_estimate=pl.CostEstimate(
            flops=weight * 1_000_000_000, bytes_accessed=size, transcendentals=0
        ),
    )(*inputs)


def move(value, lon_steps, lat_steps):
    lon, lat = lax.axis_size("lon"), lax.axis_size("lat")
    if lat_steps == 0:
        pairs = [(s, (s + lon_steps) % lon) for s in range(lon)]
        return lax.ppermute(value, "lon", pairs)
    if lon_steps == 0:
        pairs = [(s, (s + lat_steps) % lat) for s in range(lat)]
        return lax.ppermute(value, "lat", pairs)
    pairs = [
        (b * lat + a, (b + lon_steps) % lon * lat + (a + lat_steps) % lat)
        for b in range(lon)
        for a in range(lat)
    ]
    return lax.ppermute(value, ("lon", "lat"), pairs)


def send(pieces, steps):
    on_lon, on_lat, on_both = pieces
    return move(on_lon, steps, 0), move(on_lat, 0, steps), move(on_both, steps, steps)


def swap(value, step):
    count = lax.axis_size("lon")
    return lax.ppermute(value, "lon", [(s, s ^ step) for s in range(count)])


def add(mine, other):
    return (mine.astype(f32) + other.astype(f32)).astype(bf16)


def lon_steps():
    return [1 << bit for bit in range(lax.axis_size("lon").bit_length() - 1)]


def body(
    tokens, mask_ids, fine_qkv, fine_proj, fine_up, fine_down, fine_bias, reduce_weight,
    coarse_qkv, coarse_proj, coarse_up, coarse_down, coarse_bias, out_grad,
):
    lat_index = lax.axis_index("lat")
    fine_down = fine_down.T
    flat = tokens.reshape(576, 192)
    column = lambda index: jnp.asarray(index).reshape(-1, 1)
    line = lambda index: jnp.asarray(index).reshape(1, -1)
    tok = ((576, 192), bf16)
    edges = [((112, 192), bf16), ((112, 192), bf16), ((48, 192), bf16)]
    wide_edges = [((208, 192), bf16), ((208, 192), bf16), ((144, 192), bf16)]
    quad = ((96, 192), bf16)
    scores = ((12 * WIN, WIN), f32)
    table_rows = ((12, 192, WIN), bf16)
    held = ((12, 2, 12, 16, WIN), bf16)

    *sent, grad_here = pl.pallas_call(
        edge_kernel,
        in_specs=[pl.BlockSpec(memory_space=pl.ANY)] * 2,
        out_shape=[jax.ShapeDtypeStruct(*shape) for shape in wide_edges + [quad]],
        scratch_shapes=[
            pltpu.VMEM((576, 192), bf16),
            pltpu.VMEM((6, 12, 2, 384), bf16),
            pltpu.SemaphoreType.DMA((2,)),
        ],
        compiler_params=pltpu.CompilerParams(vmem_limit_bytes=56 * 1024 * 1024),
    )(flat, out_grad.transpose(1, 2, 0, 3))
    first = send(sent, 1)
    (fine_table,) = run(
        bias_kernel, [scores], [held], 2,
        (fine_bias.transpose(1, 0, 2), line(BASE), column(ROW_SLOT)),
    )

    labels = mask_ids.reshape(2, 2, 2, 3, 2, 2, 6)
    top = jnp.zeros((2, 2, 1, 1, 1, 1), jnp.int32).at[0, 0].set(1)[None]
    labels = labels * 2 + jnp.where(lat_index == 0, top, 0)
    labels = labels.transpose(1, 4, 2, 5, 0, 3, 6).reshape(4, WIN)
    fine_mask = jnp.where(labels[:, :, None] == labels[:, None, :], 0.0, -1e30).astype(f32)
    low_half = jnp.arange(WIN) < WIN // 2
    coarse_mask = jnp.where(
        (low_half[:, None] == low_half[None, :]) | (lat_index != 0), 0.0, -1e30
    ).astype(f32)

    fine = run(
        fine_kernel,
        [tok] + edges
        + [tok] * 3
        + [((24 * WIN, WIN), bf16), tok, ((576, 1), f32), tok, ((576, 1), f32), ((576, 768), bf16)],
        [((848, 192), bf16)],
        8,
        (flat, *first, column(ARRIVE), fine_table, fine_mask, fine_qkv, fine_proj, fine_up, fine_down),
    )
    q, k, v, probs, n1, r1, n2, r2, slope = fine[4:]
    arrived = send(fine[1:4], 1)
    late_table, _ = lax.optimization_barrier((coarse_bias.transpose(1, 0, 2), fine[1]))
    (coarse_table,) = run(
        bias_kernel, [scores], [held], 2, (late_table, line(BASE), column(ROW_SLOT))
    )
    coarse = run(
        coarse_kernel,
        [quad] * 4 + edges + [((336, 192), bf16), scores],
        [((848, 192), bf16), ((12 * WIN, WIN), bf16), ((576, 192), bf16)],
        9,
        (
            fine[0], *arrived, column(MERGE), column(SPLIT), coarse_table, coarse_mask, grad_here, *first,
            reduce_weight, coarse_qkv, coarse_proj, coarse_up, coarse_down,
        ),
    )
    c00, c01, c10, c11 = coarse[:4]
    arrived = send(coarse[4:7], -1)
    dlon, dlat, ddiag = arrived
    dlat, scored = lax.optimization_barrier((dlat, coarse[8]))
    (coarse_grad,) = run(
        coarse_table_kernel, [((24, 6 * ENTRIES), bf16)], [table_rows], 2,
        (scored, column(BASE), line(ROW_SLOT)),
    )
    steps = lon_steps()
    other = swap(coarse_grad, steps[-1])
    half_tok = ((288, 192), bf16)
    half_outs = [((288, 192), f32)] + [half_tok] * 3
    saved = (q, k, v, probs, n2, r2, slope, fine_proj, fine_up, fine_down)
    *first_half, first_scores = run(
        first_band_kernel,
        half_outs + [((6 * WIN, WIN), f32)],
        [((448, 192), bf16)],
        4,
        (dlon, coarse[7], column(BACK), *saved),
    )
    first_scores, other = lax.optimization_barrier((first_scores, other))
    coarse_grad = add(coarse_grad, other)
    other = swap(coarse_grad, steps[-2])
    *second_half, fine_grad = run(
        second_band_kernel,
        half_outs + [((24, 6 * ENTRIES), bf16)],
        [((608, 192), bf16), scores, table_rows],
        5,
        (
            dlon, coarse[7], dlat, ddiag, column(BACK), first_scores,
            column(BASE), line(ROW_SLOT), *saved,
        ),
    )
    second_half[0], other = lax.optimization_barrier((second_half[0], other))
    coarse_grad = add(coarse_grad, other)
    for step in reversed(steps[:-2]):
        coarse_sums = (coarse_grad, swap(coarse_grad, step))
        coarse_grad = add(*coarse_sums)
    other = swap(fine_grad, steps[0])
    fine_back = list(run(
        qkv_back_kernel, [tok] + wide_edges, [], 2,
        (*first_half, *second_half, n1, r1, fine_qkv, c10, c01, c00),
    ))
    fine_back[0], other = lax.optimization_barrier((fine_back[0], other))
    fine_grad = add(fine_grad, other)
    for step in steps[1:]:
        fine_sums = (fine_grad, swap(fine_grad, step))
        fine_grad = add(*fine_sums)
    arrived = send(fine_back[1:4], -1)
    d_tokens, coarse_result = run(
        last_kernel,
        [tok, ((2, 6, 12, 384), bf16)],
        [((848, 192), bf16), ((192, 192), bf16)],
        1,
        (fine_back[0], *arrived, column(LEAVE), c11, column(RESULT)),
    )
    (coarse_out,) = run(
        table_sum_kernel, [((HEADS_C, 1, 12 * ENTRIES), f32)], [], 1, coarse_sums
    )
    (fine_out,) = run(table_sum_kernel, [((HEADS_F, 2, 12 * ENTRIES), f32)], [], 1, fine_sums)
    return (
        coarse_result,
        d_tokens.reshape(tokens.shape),
        fine_out.transpose(1, 0, 2),
        coarse_out.transpose(1, 0, 2),
    )


def solution(mesh):
    grid = P(None, "lat", "lon", None)
    bands = P("lat", None, None)
    in_specs = (
        grid, P(None, "lat", "lon"), P(), P(), P(), P(), bands,
        P(), P(), P(), P(), P(), bands, grid,
    )
    out_specs = (grid, grid, bands, bands)
    return jax.shard_map(body, mesh=mesh, in_specs=in_specs, out_specs=out_specs, check_vma=False)
```

```python
import math

import jax
import jax.numpy as jnp
import numpy as np
from jax import lax
from jax.experimental import pallas as pl
from jax.experimental.pallas import tpu as pltpu
from jax.sharding import PartitionSpec as P

HEADS_F = 6
HEADS_C = 12
HEAD = 32
WIN = 144
QUAD = 36
SPAN = 23
ENTRIES = 276
LOG2E = math.log2(math.e)
VMEM = 20 * 1024 * 1024
f32 = jnp.float32
bf16 = jnp.bfloat16


def spot(z, i, j):
    quadrant = (i % 6) // 3 * 2 + (j % 12) // 6
    return quadrant * QUAD + z * 18 + i % 3 * 6 + j % 6


def fine_spot(z, i, j):
    return (i // 6 * 2 + j // 12) * WIN + spot(z, i, j)


def in_quad(z, i, j):
    return z * 18 + i % 3 * 6 + j % 6


def index_maps():
    arrive = np.zeros(576, np.int32)
    merge = np.zeros(576, np.int32)
    split = np.full(608, -1, np.int32)
    back = np.zeros(576, np.int32)
    leave = np.zeros(576, np.int32)
    for z in range(2):
        for i in range(12):
            for j in range(24):
                here = fine_spot(z, i, j)
                if i >= 3 and j >= 6:
                    arrive[here] = z * 288 + (i - 3) * 24 + j - 6
                    came = fine_spot(z, i - 3, j - 6)
                elif i >= 3:
                    came = 576 + (i - 3) // 3 * QUAD + in_quad(z, i, j)
                elif j >= 6:
                    came = 688 + (j - 6) // 6 * QUAD + in_quad(z, i, j)
                else:
                    came = 800 + in_quad(z, i, j)
                if came >= 576:
                    arrive[here] = came
                part = (i % 2 + j % 2 * 2) * WIN + spot(z, i // 2, j // 2)
                merge[part] = came
                if i >= 3 and j >= 6:
                    slot = 112 + z * 162 + (i - 3) * 18 + j - 6
                    back[fine_spot(z, i - 3, j - 6)] = slot
                elif i >= 3:
                    slot = z * 54 + (i - 3) * 6 + j
                    back[fine_spot(z, i - 3, j + 18)] = slot
                elif j >= 6:
                    slot = 448 + z * 54 + i * 18 + j - 6
                    back[fine_spot(z, i + 9, j - 6)] = slot
                else:
                    slot = 560 + z * 18 + i * 6 + j
                    back[fine_spot(z, i + 9, j + 18)] = slot
                split[slot] = part
                natural = z * 288 + i * 24 + j
                if i < 9 and j < 18:
                    leave[natural] = fine_spot(z, i + 3, j + 6)
                elif i < 9:
                    leave[natural] = 576 + i // 3 * QUAD + in_quad(z, i, j)
                elif j < 18:
                    leave[natural] = 688 + j // 6 * QUAD + in_quad(z, i, j)
                else:
                    leave[natural] = 800 + in_quad(z, i, j)
    result = np.zeros(WIN, np.int32)
    for z in range(2):
        for i in range(6):
            for j in range(12):
                result[z * 72 + i * 12 + j] = (i // 3 * 2 + j // 6) * 48 + in_quad(z, i, j)
    return arrive, merge, split, back, leave, result


ARRIVE, MERGE, SPLIT, BACK, LEAVE, RESULT = index_maps()


def places(shape, axis):
    t = lax.broadcasted_iota(jnp.int32, shape, axis)
    quad = (t * 57) >> 11
    t = t - quad * QUAD
    level = (t * 57) >> 10
    t = t - level * 18
    row = (t * 43) >> 8
    return level * 6 + (quad >> 1) * 3 + row, t - row * 6 + (quad & 1) * 6


def entry_base(shape, axis):
    row, column = places(shape, axis)
    return row * SPAN + 11 - column


def row_slot(shape, axis):
    row, column = places(shape, axis)
    return column * 16 + row


def one_hot(column, width):
    spots = lax.broadcasted_iota(jnp.int32, (column.shape[0], width), 1)
    return jnp.where(spots == column, 1.0, 0.0).astype(bf16)


def mm(left, right):
    return jnp.dot(left, right, preferred_element_type=f32)


def mm_nt(left, right):
    return lax.dot_general(left, right, (((1,), (1,)), ((), ())), preferred_element_type=f32)


def mm_tn(left, right):
    return lax.dot_general(left, right, (((0,), (0,)), ((), ())), preferred_element_type=f32)


def norm(values):
    centred = values - jnp.mean(values, axis=-1, keepdims=True)
    scale = lax.rsqrt(jnp.mean(centred * centred, axis=-1, keepdims=True) + 1e-5)
    return centred * scale, scale


def norm_back(grad, normed, scale):
    along = jnp.mean(grad * normed, axis=-1, keepdims=True)
    return (grad - jnp.mean(grad, axis=-1, keepdims=True) - normed * along) * scale


def gelu_pair(x):
    u = jnp.abs(x) * math.sqrt(0.5)
    t = 1.0 / (1.0 + 0.3275911 * u)
    e = jnp.exp(-u * u)
    poly = 1.421413741 + t * (-1.453152027 + t * 1.061405429)
    tail = 0.5 * (t * (0.254829592 + t * (-0.284496736 + t * poly))) * e
    below = jnp.where(x >= 0, 1.0 - tail, tail)
    return x * below, below + x * (e * (1.0 / math.sqrt(2 * math.pi)))


def groups(channels):
    return [(start, min(start + 128, channels)) for start in range(0, channels, 128)]


def head_lanes(rows, width):
    return lax.broadcasted_iota(jnp.int32, (rows, width), 1) // HEAD


def stack_heads(part):
    lanes = head_lanes(part.shape[0], part.shape[1])
    count = part.shape[1] // HEAD
    zero = jnp.zeros_like(part)
    return jnp.concatenate([jnp.where(lanes == h, part, zero) for h in range(count)], axis=0)


def pick_heads(stacked):
    width = stacked.shape[1]
    lanes = head_lanes(WIN, width)
    total = stacked[:WIN]
    for h in range(1, width // HEAD):
        total = jnp.where(lanes == h, stacked[h * WIN : (h + 1) * WIN], total)
    return total


def attend(queries, keys, values, bias_ref, bias_row, mask, probs_ref, probs_row):
    mixed = []
    for start, stop in groups(queries.shape[1]):
        count = (stop - start) // HEAD
        scores = mm_nt(stack_heads(queries[:, start:stop]), keys[:, start:stop])
        row = start // HEAD * WIN
        for h in range(count):
            here = row + h * WIN
            logits = (
                scores[h * WIN : (h + 1) * WIN] * (HEAD**-0.5 * LOG2E)
                + bias_ref[pl.ds(bias_row + here, WIN), :]
                + mask
            )
            raised = jnp.exp2(logits - jnp.max(logits, axis=-1, keepdims=True))
            probs = raised * (1.0 / jnp.sum(raised, axis=-1, keepdims=True))
            probs_ref[pl.ds(probs_row + here, WIN), :] = probs.astype(bf16)
        stacked = mm(probs_ref[pl.ds(probs_row + row, count * WIN), :], values[:, start:stop])
        mixed.append(pick_heads(stacked))
    return jnp.concatenate(mixed, axis=1)


def attend_back(queries, keys, values, mix_grad, probs_ref, probs_row, score_ref, add):
    query_grad, key_grad, value_grad = [], [], []
    for start, stop in groups(queries.shape[1]):
        count = (stop - start) // HEAD
        row = start // HEAD * WIN
        probs_all = probs_ref[pl.ds(probs_row + row, count * WIN), :]
        grads = stack_heads(mix_grad[:, start:stop])
        value_grad.append(mm_tn(probs_all, grads))
        probs_grad = mm_nt(grads, values[:, start:stop])
        pieces = []
        for h in range(count):
            probs = probs_all[h * WIN : (h + 1) * WIN].astype(f32)
            grad = probs_grad[h * WIN : (h + 1) * WIN]
            weighted = grad * probs
            score_grad = weighted - probs * jnp.sum(weighted, axis=-1, keepdims=True)
            place = pl.ds(row + h * WIN, WIN)
            if add:
                score_ref[place, :] += score_grad
            else:
                score_ref[place, :] = score_grad
            pieces.append(score_grad.astype(bf16))
        score_all = jnp.concatenate(pieces, axis=0)
        query_grad.append(pick_heads(mm(score_all, keys[:, start:stop])))
        key_grad.append(mm_tn(score_all, stack_heads(queries[:, start:stop])))
    scale = HEAD**-0.5
    return (
        jnp.concatenate(query_grad, axis=1) * scale,
        jnp.concatenate(key_grad, axis=1) * scale,
        jnp.concatenate(value_grad, axis=1),
    )


def swap_rows():
    row = lax.broadcasted_iota(jnp.int32, (192, 192), 0)
    return jnp.where(
        lax.broadcasted_iota(jnp.int32, (192, 192), 1) == row % 16 * 16 + row // 16, 1.0, 0.0
    ).astype(bf16)


def table_grad(score_ref, rows_ref):
    regroup = jnp.where(
        lax.broadcasted_iota(jnp.int32, (192, WIN), 0) == row_slot((1, WIN), 1), 1.0, 0.0
    ).astype(bf16)
    for h in range(12):
        moved = mm(regroup, score_ref[pl.ds(h * WIN, WIN), :].astype(bf16)).astype(bf16)
        rows_ref[:, pl.ds(h * 16, 16), :] = moved.reshape(12, 16, WIN)
    total = jnp.zeros((192, ENTRIES), f32)
    base = entry_base((WIN, 1), 0)
    for column in range(12):
        total += mm(rows_ref[column], one_hot(base + column, ENTRIES))
    swapped = mm(swap_rows(), total.astype(bf16))
    halves = [
        jnp.concatenate([swapped[a * 16 : a * 16 + 12] for a in range(start, start + 6)], axis=1)
        for start in (0, 6)
    ]
    return jnp.concatenate(halves, axis=0).astype(bf16)


def pack(pieces, rows):
    count = sum(piece.shape[0] for piece in pieces)
    if rows > count:
        pieces = pieces + [jnp.zeros((rows - count, pieces[0].shape[1]), f32)]
    return jnp.concatenate(pieces, axis=0).astype(bf16)


def quadrant(windows, qi, qj):
    part = (qi % 2 * 2 + qj % 2) * QUAD
    return windows[qi // 2 * 2 + qj // 2][part : part + QUAD]


def halves(values):
    return [values[:, 0:192], values[:, 192:384]]


def edge_kernel(tokens_ref, grad_ref, slon_ref, slat_ref, sdiag_ref, gloc_ref):
    tokens = tokens_ref[...].astype(f32)
    grads = grad_ref[...].astype(f32)

    def token_quadrant(row, start):
        pieces = []
        for z in range(2):
            for i in range(row, row + 3):
                place = (z * 12 + i) * 24 + start
                pieces.append(tokens[place : place + 6])
        return jnp.concatenate(pieces, axis=0)

    def grad_quadrant(hi, hj):
        pieces = [
            grads[hi * 3 + row, hj * 6 : hj * 6 + 6, z]
            for z in range(2)
            for row in range(3)
        ]
        return pack(pieces, 48)

    slon_ref[0:112] = pack([token_quadrant(q * 3, 18) for q in range(3)], 112)
    slat_ref[0:112] = pack([token_quadrant(9, q * 6) for q in range(3)], 112)
    sdiag_ref[0:48] = pack([token_quadrant(9, 18)], 48)
    gloc_ref[0:48], gloc_ref[48:96] = halves(grad_quadrant(0, 0))
    slon_ref[112:160], slon_ref[160:208] = halves(grad_quadrant(0, 1))
    slat_ref[112:160], slat_ref[160:208] = halves(grad_quadrant(1, 0))
    sdiag_ref[48:96], sdiag_ref[96:144] = halves(grad_quadrant(1, 1))


def expand(table_ref, out_ref, held):
    table = jnp.concatenate([table_ref[:, b, :] for b in range(table_ref.shape[1])], axis=0)
    filler = jnp.zeros((4, ENTRIES), f32)
    pieces = []
    for a in range(12):
        pieces += [table[:, a * ENTRIES : (a + 1) * ENTRIES], filler]
    table = jnp.concatenate(pieces, axis=0)
    high = table.astype(bf16)
    low = (table - high.astype(f32)).astype(bf16)
    swap = swap_rows()
    table = jnp.concatenate(
        [mm(swap, high).astype(bf16), mm(swap, low).astype(bf16)], axis=0
    )
    entry = lax.broadcasted_iota(jnp.int32, (ENTRIES, WIN), 0)
    base = entry_base((1, WIN), 1)
    for column in range(12):
        picker = jnp.where(entry == base + column, 1.0, 0.0).astype(bf16)
        picked = mm(table, picker).astype(bf16)
        held[:, 0, column] = picked[0:192].reshape(12, 16, WIN)
        held[:, 1, column] = picked[192:384].reshape(12, 16, WIN)
    spots = lax.broadcasted_iota(jnp.int32, (WIN, 384), 1)
    spots = jnp.where(spots >= 192, spots - 192, spots)
    twice = jnp.where(spots == row_slot((WIN, 1), 0), 1.0, 0.0).astype(bf16)
    for h in range(12):
        out_ref[pl.ds(h * WIN, WIN), :] = mm(twice, held[h].reshape(384, WIN)) * LOG2E


def bias_kernel(table_ref, out_ref, held):
    expand(table_ref, out_ref, held)


def coarse_table_kernel(score_ref, table_ref, rows_ref):
    table_ref[...] = table_grad(score_ref, rows_ref)


def table_sum_kernel(kept_ref, other_ref, out_ref):
    total = kept_ref[...].astype(f32) + other_ref[...].astype(f32)
    total = jnp.concatenate([total[0:12], total[12:24]], axis=1)
    heads = out_ref.shape[0]
    for b in range(out_ref.shape[1]):
        out_ref[:, b, :] = total[b * heads : (b + 1) * heads]


def fine_windows(numbers, refs):
    tokens_ref, lon_ref, lat_ref, diag_ref, arrive_ref, bias_ref, mask_ref = refs[:7]
    qkv_ref, proj_ref, up_ref, down_ref, res_ref = refs[7:12]
    q_ref, k_ref, v_ref, probs_ref, n1_ref, r1_ref, n2_ref, r2_ref, slope_ref = refs[12:21]
    source = refs[21]
    source[0:576] = tokens_ref[...]
    source[576:688] = lon_ref[0:112]
    source[688:800] = lat_ref[0:112]
    source[800:848] = diag_ref[0:48]
    everything = source[...]
    w_qkv = qkv_ref[...]
    bases = []
    for slot, w in enumerate(numbers):
        rows = pl.ds(slot * WIN, WIN)
        base = mm(one_hot(arrive_ref[pl.ds(w * WIN, WIN), :], 848), everything)
        normed, scale = norm(base)
        normed = normed.astype(bf16)
        n1_ref[rows, :] = normed
        r1_ref[rows, :] = scale
        q_ref[rows, :] = mm(normed, w_qkv[:, 0:192]).astype(bf16)
        k_ref[rows, :] = mm(normed, w_qkv[:, 192:384]).astype(bf16)
        v_ref[rows, :] = mm(normed, w_qkv[:, 384:576]).astype(bf16)
        bases.append(base)
    windows = {}
    for slot, w in enumerate(numbers):
        rows = pl.ds(slot * WIN, WIN)
        mixture = attend(
            q_ref[rows, :], k_ref[rows, :], v_ref[rows, :],
            bias_ref, w // 2 * 6 * WIN, mask_ref[w], probs_ref, slot * 6 * WIN,
        ).astype(bf16)
        first = bases[slot] + mm(mixture, proj_ref[...])
        renormed, scale = norm(first)
        renormed = renormed.astype(bf16)
        n2_ref[rows, :] = renormed
        r2_ref[rows, :] = scale
        active, slope = gelu_pair(mm(renormed, up_ref[...]))
        slope_ref[rows, :] = slope.astype(bf16)
        result = first + mm_nt(active.astype(bf16), down_ref[...])
        res_ref[rows, :] = result.astype(bf16)
        windows[w] = result
    return windows


def fine_edge_kernel(*refs):
    slon_ref, slat_ref, sdiag_ref = refs[11:14]
    windows = fine_windows((1, 2, 3), refs[:11] + refs[14:])
    slon_ref[...] = pack([quadrant(windows, q, 3) for q in range(3)], 112)
    slat_ref[...] = pack([quadrant(windows, 3, q) for q in range(3)], 112)
    sdiag_ref[...] = pack([quadrant(windows, 3, 3)], 48)


def fine_inner_kernel(*refs):
    fine_windows((0,), refs)


def coarse_kernel(
    inner_ref, res_ref, lon_ref, lat_ref, diag_ref, merge_ref, split_ref, bias_ref, mask_ref,
    gloc_ref, glon_ref, glat_ref, gdiag_ref,
    reduce_ref, qkv_ref, proj_ref, up_ref, down_ref,
    c0, c1, c2, c3, dlon_ref, dlat_ref, ddiag_ref, dloc_ref, score_ref,
    source, probs_ref, parts_ref,
):
    source[0:144] = inner_ref[...]
    source[144:576] = res_ref[...]
    source[576:688] = lon_ref[...]
    source[688:800] = lat_ref[...]
    source[800:848] = diag_ref[...]
    everything = source[...]
    parts = [mm(one_hot(merge_ref[pl.ds(k * WIN, WIN), :], 848), everything) for k in range(4)]
    mean = sum(jnp.sum(part, axis=-1, keepdims=True) for part in parts) * (1.0 / 768)
    parts = [part - mean for part in parts]
    square = sum(jnp.sum(part * part, axis=-1, keepdims=True) for part in parts)
    merge_scale = lax.rsqrt(square * (1.0 / 768) + 1e-5)
    parts = [(part * merge_scale).astype(bf16) for part in parts]
    base = sum(mm(parts[k], reduce_ref[k * 192 : (k + 1) * 192]) for k in range(4))
    base = base.astype(bf16).astype(f32)
    normed, scale1 = norm(base)
    normed = normed.astype(bf16)
    queries = mm(normed, qkv_ref[:, 0:384]).astype(bf16)
    keys = mm(normed, qkv_ref[:, 384:768]).astype(bf16)
    values = mm(normed, qkv_ref[:, 768:1152]).astype(bf16)
    mixture = attend(queries, keys, values, bias_ref, 0, mask_ref[...], probs_ref, 0).astype(bf16)
    first = base + mm(mixture, proj_ref[...])
    renormed, scale2 = norm(first)
    renormed = renormed.astype(bf16)
    active, slope = gelu_pair(mm(renormed, up_ref[...]))
    result = first + mm(active.astype(bf16), down_ref[...])
    for index, out in enumerate((c0, c1, c2, c3)):
        piece = pack([result[index * QUAD : (index + 1) * QUAD]], 48)
        out[0:48], out[48:96] = halves(piece)

    pieces = []
    for ref, start in ((gdiag_ref, 48), (glat_ref, 112), (glon_ref, 112), (gloc_ref, 0)):
        both = [ref[start : start + 48], ref[start + 48 : start + 96]]
        pieces.append(jnp.concatenate([half.astype(f32)[:QUAD] for half in both], axis=1))
    grad = jnp.concatenate(pieces, axis=0)
    inner = mm_nt(grad.astype(bf16), down_ref[...]) * slope
    grad = grad + norm_back(mm_nt(inner.astype(bf16), up_ref[...]), renormed.astype(f32), scale2)
    mix_grad = mm_nt(grad.astype(bf16), proj_ref[...]).astype(bf16)
    dq, dk, dv = attend_back(queries, keys, values, mix_grad, probs_ref, 0, score_ref, False)
    normed_grad = (
        mm_nt(dq.astype(bf16), qkv_ref[:, 0:384])
        + mm_nt(dk.astype(bf16), qkv_ref[:, 384:768])
        + mm_nt(dv.astype(bf16), qkv_ref[:, 768:1152])
    )
    grad = grad + norm_back(normed_grad, normed.astype(f32), scale1)
    grad = grad.astype(bf16)
    grads = [mm_nt(grad, reduce_ref[k * 192 : (k + 1) * 192]) for k in range(4)]
    mean = sum(jnp.sum(g, axis=-1, keepdims=True) for g in grads) * (1.0 / 768)
    along = sum(
        jnp.sum(g * p.astype(f32), axis=-1, keepdims=True) for g, p in zip(grads, parts)
    ) * (1.0 / 768)
    for k in range(4):
        part = (grads[k] - mean - parts[k].astype(f32) * along) * merge_scale
        parts_ref[pl.ds(k * WIN, WIN), :] = part.astype(bf16)
    everything = parts_ref[...]
    moved = mm(one_hot(split_ref[...], 576), everything).astype(bf16)
    dlon_ref[...] = moved[0:112]
    dloc_ref[...] = moved[112:448]
    dlat_ref[...] = moved[448:560]
    ddiag_ref[...] = moved[560:608]


def band_back(parts, source, back_ref, weights, outs, score_ref):
    proj_ref, up_ref, down_ref = weights
    grad_ref, dq_ref, dk_ref, dv_ref = outs
    everything = source[...]
    for across, (w, slot, saved) in enumerate(parts):
        q_ref, k_ref, v_ref, probs_ref, n2_ref, r2_ref, slope_ref = saved
        rows = pl.ds(slot * WIN, WIN)
        here = pl.ds(across * WIN, WIN)
        grad = mm(one_hot(back_ref[pl.ds(w * WIN, WIN), :], everything.shape[0]), everything)
        inner = mm(grad.astype(bf16), down_ref[...]) * slope_ref[rows, :].astype(f32)
        grad = grad + norm_back(
            mm_nt(inner.astype(bf16), up_ref[...]), n2_ref[rows, :].astype(f32), r2_ref[rows, :]
        )
        grad_ref[here, :] = grad
        mix_grad = mm_nt(grad.astype(bf16), proj_ref[...]).astype(bf16)
        dq, dk, dv = attend_back(
            q_ref[rows, :], k_ref[rows, :], v_ref[rows, :], mix_grad,
            probs_ref, slot * 6 * WIN, score_ref, across == 1,
        )
        dq_ref[here, :] = dq.astype(bf16)
        dk_ref[here, :] = dk.astype(bf16)
        dv_ref[here, :] = dv.astype(bf16)


def first_band_kernel(dlon_ref, dloc_ref, back_ref, *refs):
    *refs, source = refs
    source[0:112] = dlon_ref[...]
    source[112:448] = dloc_ref[...]
    parts = ((0, 0, refs[:7]), (1, 0, refs[7:14]))
    band_back(parts, source, back_ref, refs[14:17], refs[17:21], refs[21])


def second_band_kernel(
    dlon_ref, dloc_ref, dlat_ref, ddiag_ref, back_ref, first_ref, *refs
):
    *refs, source, score_ref, rows_ref = refs
    source[0:112] = dlon_ref[...]
    source[112:448] = dloc_ref[...]
    source[448:560] = dlat_ref[...]
    source[560:608] = ddiag_ref[...]
    half = 6 * WIN
    score_ref[pl.ds(0, half), :] = first_ref[...]
    parts = ((2, 1, refs[:7]), (3, 2, refs[:7]))
    band_back(
        parts, source, back_ref, refs[7:10], refs[10:14], score_ref.at[pl.ds(half, half)]
    )
    refs[14][...] = table_grad(score_ref, rows_ref)


def qkv_back_kernel(*refs):
    bands, refs = (refs[:4], refs[4:8]), refs[8:]
    norms = (refs[0:2], refs[2:4])
    qkv_ref, clon_ref, clat_ref, cdiag_ref = refs[4:8]
    res_ref, slon_ref, slat_ref, sdiag_ref = refs[8:]
    w_qkv = qkv_ref[...]
    windows = []
    for w in range(4):
        grad_ref, dq_ref, dk_ref, dv_ref = bands[w // 2]
        rows = pl.ds(w * WIN, WIN)
        here = pl.ds(w % 2 * WIN, WIN)
        normed_grad = (
            mm_nt(dq_ref[here, :], w_qkv[:, 0:192])
            + mm_nt(dk_ref[here, :], w_qkv[:, 192:384])
            + mm_nt(dv_ref[here, :], w_qkv[:, 384:576])
        )
        n1_ref, r1_ref = norms[min(w, 1)]
        slot = pl.ds(max(w - 1, 0) * WIN, WIN)
        result = grad_ref[here, :] + norm_back(
            normed_grad, n1_ref[slot, :].astype(f32), r1_ref[slot, :]
        )
        res_ref[rows, :] = result.astype(bf16)
        windows.append(result)
    slon_ref[0:112] = pack([quadrant(windows, q, 0) for q in range(1, 4)], 112)
    slat_ref[0:112] = pack([quadrant(windows, 0, q) for q in range(1, 4)], 112)
    sdiag_ref[0:48] = pack([quadrant(windows, 0, 0)], 48)
    slon_ref[112:208] = clon_ref[...]
    slat_ref[112:208] = clat_ref[...]
    sdiag_ref[48:144] = cdiag_ref[...]


def last_kernel(
    res_ref, lon_ref, lat_ref, diag_ref, leave_ref, cloc_ref, result_ref,
    tokens_ref, coarse_ref, source, coarse_source,
):
    source[0:576] = res_ref[...]
    source[576:688] = lon_ref[0:112]
    source[688:800] = lat_ref[0:112]
    source[800:848] = diag_ref[0:48]
    everything = source[...]
    for w in range(4):
        rows = pl.ds(w * WIN, WIN)
        tokens_ref[rows, :] = mm(one_hot(leave_ref[rows, :], 848), everything).astype(bf16)
    picks = one_hot(result_ref[...], 192)
    moved = []
    for half in (0, 48):
        coarse_source[0:48] = cloc_ref[half : half + 48]
        coarse_source[48:96] = lon_ref[112 + half : 160 + half]
        coarse_source[96:144] = lat_ref[112 + half : 160 + half]
        coarse_source[144:192] = diag_ref[48 + half : 96 + half]
        moved.append(mm(picks, coarse_source[...]))
    moved = jnp.concatenate(moved, axis=1)
    for z in range(2):
        for row in range(6):
            start = z * 72 + row * 12
            coarse_ref[z, row] = moved[start : start + 12].astype(bf16)


def run(kernel, outs, scratch, weight, inputs):
    shapes = [jax.ShapeDtypeStruct(shape, kind) for shape, kind in outs]
    size = sum(math.prod(s.shape) * s.dtype.itemsize for s in shapes)
    size += sum(x.size * x.dtype.itemsize for x in inputs)
    return pl.pallas_call(
        kernel,
        out_shape=shapes,
        scratch_shapes=[pltpu.VMEM(shape, kind) for shape, kind in scratch],
        compiler_params=pltpu.CompilerParams(vmem_limit_bytes=VMEM),
        cost_estimate=pl.CostEstimate(
            flops=weight * 1_000_000_000, bytes_accessed=size, transcendentals=0
        ),
    )(*inputs)


def move(value, lon_steps, lat_steps):
    lon, lat = lax.axis_size("lon"), lax.axis_size("lat")
    if lat_steps == 0:
        pairs = [(s, (s + lon_steps) % lon) for s in range(lon)]
        return lax.ppermute(value, "lon", pairs)
    if lon_steps == 0:
        pairs = [(s, (s + lat_steps) % lat) for s in range(lat)]
        return lax.ppermute(value, "lat", pairs)
    pairs = [
        (b * lat + a, (b + lon_steps) % lon * lat + (a + lat_steps) % lat)
        for b in range(lon)
        for a in range(lat)
    ]
    return lax.ppermute(value, ("lon", "lat"), pairs)


def send(pieces, steps):
    on_lon, on_lat, on_both = pieces
    return move(on_lon, steps, 0), move(on_lat, 0, steps), move(on_both, steps, steps)


def swap(value, step):
    count = lax.axis_size("lon")
    return lax.ppermute(value, "lon", [(s, s ^ step) for s in range(count)])


def add(mine, other):
    return (mine.astype(f32) + other.astype(f32)).astype(bf16)


def lon_steps():
    return [1 << bit for bit in range(lax.axis_size("lon").bit_length() - 1)]


def body(
    tokens, mask_ids, fine_qkv, fine_proj, fine_up, fine_down, fine_bias, reduce_weight,
    coarse_qkv, coarse_proj, coarse_up, coarse_down, coarse_bias, out_grad,
):
    lat_index = lax.axis_index("lat")
    fine_down = fine_down.T
    flat = tokens.reshape(576, 192)
    column = lambda index: jnp.asarray(index).reshape(-1, 1)
    tok = ((576, 192), bf16)
    edges = [((112, 192), bf16), ((112, 192), bf16), ((48, 192), bf16)]
    wide_edges = [((208, 192), bf16), ((208, 192), bf16), ((144, 192), bf16)]
    quad = ((96, 192), bf16)
    scores = ((12 * WIN, WIN), f32)
    table_rows = ((12, 192, WIN), bf16)
    held = ((12, 2, 12, 16, WIN), bf16)

    *sent, grad_here = run(
        edge_kernel, wide_edges + [quad], [], 1, (flat, out_grad.transpose(1, 2, 0, 3))
    )
    first = send(sent, 1)
    (fine_table,) = run(
        bias_kernel, [scores], [held], 2,
        (fine_bias.transpose(1, 0, 2),),
    )

    row = lax.broadcasted_iota(jnp.int32, mask_ids.shape, 1) + lat_index * mask_ids.shape[1]
    labels = mask_ids * 2 + jnp.where(row < 3, 1, 0)
    labels = labels.reshape(2, 2, 2, 3, 2, 2, 6)
    labels = labels.transpose(1, 4, 2, 5, 0, 3, 6).reshape(4, WIN)
    fine_mask = jnp.where(labels[:, :, None] == labels[:, None, :], 0.0, -1e30).astype(f32)
    low_half = jnp.arange(WIN) < WIN // 2
    coarse_mask = jnp.where(
        (low_half[:, None] == low_half[None, :]) | (lat_index != 0), 0.0, -1e30
    ).astype(f32)

    def saved_shapes(windows):
        rows = windows * WIN
        part = ((rows, 192), bf16)
        scale = ((rows, 1), f32)
        probs = ((6 * rows, WIN), bf16)
        return [part] * 3 + [probs, part, scale, part, scale, ((rows, 768), bf16)]

    inputs = (
        flat, *first, column(ARRIVE), fine_table, fine_mask,
        fine_qkv, fine_proj, fine_up, fine_down,
    )
    gathered = [((848, 192), bf16)]
    outer = run(
        fine_edge_kernel,
        edges + [((3 * WIN, 192), bf16)] + saved_shapes(3),
        gathered, 6, inputs,
    )
    arrived = send(outer[:3], 1)
    flat_after, _ = lax.optimization_barrier((flat, outer[3]))
    inner = run(
        fine_inner_kernel,
        [((WIN, 192), bf16)] + saved_shapes(1),
        gathered, 2, (flat_after, *inputs[1:]),
    )
    late_table, _ = lax.optimization_barrier((coarse_bias.transpose(1, 0, 2), outer[3]))
    (coarse_table,) = run(
        bias_kernel, [scores], [held], 2, (late_table,)
    )
    coarse = run(
        coarse_kernel,
        [quad] * 4 + edges + [((336, 192), bf16), scores],
        [((848, 192), bf16), ((12 * WIN, WIN), bf16), ((576, 192), bf16)],
        9,
        (
            inner[0], outer[3], *arrived, column(MERGE), column(SPLIT), coarse_table, coarse_mask, grad_here, *first,
            reduce_weight, coarse_qkv, coarse_proj, coarse_up, coarse_down,
        ),
    )
    c00, c01, c10, c11 = coarse[:4]
    arrived = send(coarse[4:7], -1)
    dlon, dlat, ddiag = arrived
    dlat, scored = lax.optimization_barrier((dlat, coarse[8]))
    (coarse_grad,) = run(
        coarse_table_kernel, [((24, 6 * ENTRIES), bf16)], [table_rows], 2,
        (scored,),
    )
    steps = lon_steps()
    other = swap(coarse_grad, steps[-1])
    half_tok = ((288, 192), bf16)
    half_outs = [((288, 192), f32)] + [half_tok] * 3
    q, k, v, probs, n1, r1, n2, r2, slope = outer[4:]
    outer_saved = (q, k, v, probs, n2, r2, slope)
    q, k, v, probs, n1_inner, r1_inner, n2, r2, slope = inner[1:]
    inner_saved = (q, k, v, probs, n2, r2, slope)
    weights = (fine_proj, fine_up, fine_down)
    *first_half, first_scores = run(
        first_band_kernel,
        half_outs + [((6 * WIN, WIN), f32)],
        [((448, 192), bf16)],
        4,
        (dlon, coarse[7], column(BACK), *inner_saved, *outer_saved, *weights),
    )
    first_scores, other = lax.optimization_barrier((first_scores, other))
    coarse_grad = add(coarse_grad, other)
    other = swap(coarse_grad, steps[-2])
    *second_half, fine_grad = run(
        second_band_kernel,
        half_outs + [((24, 6 * ENTRIES), bf16)],
        [((608, 192), bf16), scores, table_rows],
        5,
        (
            dlon, coarse[7], dlat, ddiag, column(BACK), first_scores,
            *outer_saved, *weights,
        ),
    )
    second_half[0], other = lax.optimization_barrier((second_half[0], other))
    coarse_grad = add(coarse_grad, other)
    for step in reversed(steps[:-2]):
        coarse_sums = (coarse_grad, swap(coarse_grad, step))
        coarse_grad = add(*coarse_sums)
    other = swap(fine_grad, steps[-1])
    fine_back = list(run(
        qkv_back_kernel, [tok] + wide_edges, [], 2,
        (*first_half, *second_half, n1_inner, r1_inner, n1, r1, fine_qkv, c10, c01, c00),
    ))
    alon, alat, adiag = send(fine_back[1:4], -1)
    alat, other = lax.optimization_barrier((alat, other))
    fine_grad = add(fine_grad, other)
    for step in reversed(steps[:-1]):
        fine_sums = (fine_grad, swap(fine_grad, step))
        fine_grad = add(*fine_sums)
    d_tokens, coarse_result = run(
        last_kernel,
        [tok, ((2, 6, 12, 384), bf16)],
        [((848, 192), bf16), ((192, 192), bf16)],
        1,
        (fine_back[0], alon, alat, adiag, column(LEAVE), c11, column(RESULT)),
    )
    (coarse_out,) = run(
        table_sum_kernel, [((HEADS_C, 1, 12 * ENTRIES), f32)], [], 1, coarse_sums
    )
    (fine_out,) = run(table_sum_kernel, [((HEADS_F, 2, 12 * ENTRIES), f32)], [], 1, fine_sums)
    return (
        coarse_result,
        d_tokens.reshape(tokens.shape),
        fine_out.transpose(1, 0, 2),
        coarse_out.transpose(1, 0, 2),
    )


def solution(mesh):
    grid = P(None, "lat", "lon", None)
    bands = P("lat", None, None)
    in_specs = (
        grid, P(None, "lat", "lon"), P(), P(), P(), P(), bands,
        P(), P(), P(), P(), P(), bands, grid,
    )
    out_specs = (grid, grid, bands, bands)
    return jax.shard_map(body, mesh=mesh, in_specs=in_specs, out_specs=out_specs, check_vma=False)
```

```python
import math

import jax
import jax.numpy as jnp
import numpy as np
from jax import lax
from jax.experimental import pallas as pl
from jax.experimental.pallas import tpu as pltpu
from jax.sharding import PartitionSpec as P

HEADS_F = 6
HEADS_C = 12
HEAD = 32
WIN = 144
QUAD = 36
SPAN = 23
ENTRIES = 276
LOG2E = math.log2(math.e)
VMEM = 20 * 1024 * 1024
f32 = jnp.float32
bf16 = jnp.bfloat16


def spot(z, i, j):
    quadrant = (i % 6) // 3 * 2 + (j % 12) // 6
    return quadrant * QUAD + z * 18 + i % 3 * 6 + j % 6


def fine_spot(z, i, j):
    return (i // 6 * 2 + j // 12) * WIN + spot(z, i, j)


def in_quad(z, i, j):
    return z * 18 + i % 3 * 6 + j % 6


def index_maps():
    arrive = np.zeros(576, np.int32)
    merge = np.zeros(576, np.int32)
    split = np.full(608, -1, np.int32)
    back = np.zeros(576, np.int32)
    leave = np.zeros(576, np.int32)
    for z in range(2):
        for i in range(12):
            for j in range(24):
                here = fine_spot(z, i, j)
                if i >= 3 and j >= 6:
                    arrive[here] = z * 288 + (i - 3) * 24 + j - 6
                    came = fine_spot(z, i - 3, j - 6)
                elif i >= 3:
                    came = 576 + (i - 3) // 3 * QUAD + in_quad(z, i, j)
                elif j >= 6:
                    came = 688 + (j - 6) // 6 * QUAD + in_quad(z, i, j)
                else:
                    came = 800 + in_quad(z, i, j)
                if came >= 576:
                    arrive[here] = came
                part = (i % 2 + j % 2 * 2) * WIN + spot(z, i // 2, j // 2)
                merge[part] = came
                if i >= 3 and j >= 6:
                    slot = 112 + z * 162 + (i - 3) * 18 + j - 6
                    back[fine_spot(z, i - 3, j - 6)] = slot
                elif i >= 3:
                    slot = z * 54 + (i - 3) * 6 + j
                    back[fine_spot(z, i - 3, j + 18)] = slot
                elif j >= 6:
                    slot = 448 + z * 54 + i * 18 + j - 6
                    back[fine_spot(z, i + 9, j - 6)] = slot
                else:
                    slot = 560 + z * 18 + i * 6 + j
                    back[fine_spot(z, i + 9, j + 18)] = slot
                split[slot] = part
                natural = z * 288 + i * 24 + j
                if i < 9 and j < 18:
                    leave[natural] = fine_spot(z, i + 3, j + 6)
                elif i < 9:
                    leave[natural] = 576 + i // 3 * QUAD + in_quad(z, i, j)
                elif j < 18:
                    leave[natural] = 688 + j // 6 * QUAD + in_quad(z, i, j)
                else:
                    leave[natural] = 800 + in_quad(z, i, j)
    result = np.zeros(WIN, np.int32)
    for z in range(2):
        for i in range(6):
            for j in range(12):
                result[z * 72 + i * 12 + j] = (i // 3 * 2 + j // 6) * 48 + in_quad(z, i, j)
    return arrive, merge, split, back, leave, result


ARRIVE, MERGE, SPLIT, BACK, LEAVE, RESULT = index_maps()


def places(shape, axis):
    t = lax.broadcasted_iota(jnp.int32, shape, axis)
    quad = (t * 57) >> 11
    t = t - quad * QUAD
    level = (t * 57) >> 10
    t = t - level * 18
    row = (t * 43) >> 8
    return level * 6 + (quad >> 1) * 3 + row, t - row * 6 + (quad & 1) * 6


def entry_base(shape, axis):
    row, column = places(shape, axis)
    return row * SPAN + 11 - column


def row_slot(shape, axis):
    row, column = places(shape, axis)
    return column * 16 + row


def one_hot(column, width):
    spots = lax.broadcasted_iota(jnp.int32, (column.shape[0], width), 1)
    return jnp.where(spots == column, 1.0, 0.0).astype(bf16)


def mm(left, right):
    return jnp.dot(left, right, preferred_element_type=f32)


def mm_nt(left, right):
    return lax.dot_general(left, right, (((1,), (1,)), ((), ())), preferred_element_type=f32)


def mm_tn(left, right):
    return lax.dot_general(left, right, (((0,), (0,)), ((), ())), preferred_element_type=f32)


def norm(values):
    centred = values - jnp.mean(values, axis=-1, keepdims=True)
    scale = lax.rsqrt(jnp.mean(centred * centred, axis=-1, keepdims=True) + 1e-5)
    return centred * scale, scale


def norm_back(grad, normed, scale):
    along = jnp.mean(grad * normed, axis=-1, keepdims=True)
    return (grad - jnp.mean(grad, axis=-1, keepdims=True) - normed * along) * scale


def gelu_pair(x):
    u = jnp.abs(x) * math.sqrt(0.5)
    t = 1.0 / (1.0 + 0.3275911 * u)
    e = jnp.exp(-u * u)
    poly = 1.421413741 + t * (-1.453152027 + t * 1.061405429)
    tail = 0.5 * (t * (0.254829592 + t * (-0.284496736 + t * poly))) * e
    below = jnp.where(x >= 0, 1.0 - tail, tail)
    return x * below, below + x * (e * (1.0 / math.sqrt(2 * math.pi)))


def groups(channels):
    return [(start, min(start + 128, channels)) for start in range(0, channels, 128)]


def head_lanes(rows, width):
    return lax.broadcasted_iota(jnp.int32, (rows, width), 1) // HEAD


def stack_heads(part):
    lanes = head_lanes(part.shape[0], part.shape[1])
    count = part.shape[1] // HEAD
    zero = jnp.zeros_like(part)
    return jnp.concatenate([jnp.where(lanes == h, part, zero) for h in range(count)], axis=0)


def pick_heads(stacked):
    width = stacked.shape[1]
    lanes = head_lanes(WIN, width)
    total = stacked[:WIN]
    for h in range(1, width // HEAD):
        total = jnp.where(lanes == h, stacked[h * WIN : (h + 1) * WIN], total)
    return total


def attend(queries, keys, values, bias_ref, bias_row, mask, probs_ref, probs_row):
    mixed = []
    for start, stop in groups(queries.shape[1]):
        count = (stop - start) // HEAD
        scores = mm_nt(stack_heads(queries[:, start:stop]), keys[:, start:stop])
        row = start // HEAD * WIN
        for h in range(count):
            here = row + h * WIN
            logits = (
                scores[h * WIN : (h + 1) * WIN] * (HEAD**-0.5 * LOG2E)
                + bias_ref[pl.ds(bias_row + here, WIN), :]
                + mask
            )
            raised = jnp.exp2(logits - jnp.max(logits, axis=-1, keepdims=True))
            probs = raised * (1.0 / jnp.sum(raised, axis=-1, keepdims=True))
            probs_ref[pl.ds(probs_row + here, WIN), :] = probs.astype(bf16)
        stacked = mm(probs_ref[pl.ds(probs_row + row, count * WIN), :], values[:, start:stop])
        mixed.append(pick_heads(stacked))
    return jnp.concatenate(mixed, axis=1)


def attend_back(queries, keys, values, mix_grad, probs_ref, probs_row, score_ref, add):
    query_grad, key_grad, value_grad = [], [], []
    for start, stop in groups(queries.shape[1]):
        count = (stop - start) // HEAD
        row = start // HEAD * WIN
        probs_all = probs_ref[pl.ds(probs_row + row, count * WIN), :]
        grads = stack_heads(mix_grad[:, start:stop])
        value_grad.append(mm_tn(probs_all, grads))
        probs_grad = mm_nt(grads, values[:, start:stop])
        pieces = []
        for h in range(count):
            probs = probs_all[h * WIN : (h + 1) * WIN].astype(f32)
            grad = probs_grad[h * WIN : (h + 1) * WIN]
            weighted = grad * probs
            score_grad = weighted - probs * jnp.sum(weighted, axis=-1, keepdims=True)
            place = pl.ds(row + h * WIN, WIN)
            if add:
                score_ref[place, :] += score_grad
            else:
                score_ref[place, :] = score_grad
            pieces.append(score_grad.astype(bf16))
        score_all = jnp.concatenate(pieces, axis=0)
        query_grad.append(pick_heads(mm(score_all, keys[:, start:stop])))
        key_grad.append(mm_tn(score_all, stack_heads(queries[:, start:stop])))
    scale = HEAD**-0.5
    return (
        jnp.concatenate(query_grad, axis=1) * scale,
        jnp.concatenate(key_grad, axis=1) * scale,
        jnp.concatenate(value_grad, axis=1),
    )


def swap_rows():
    row = lax.broadcasted_iota(jnp.int32, (192, 192), 0)
    return jnp.where(
        lax.broadcasted_iota(jnp.int32, (192, 192), 1) == row % 16 * 16 + row // 16, 1.0, 0.0
    ).astype(bf16)


def table_grad(score_ref, rows_ref):
    regroup = jnp.where(
        lax.broadcasted_iota(jnp.int32, (192, WIN), 0) == row_slot((1, WIN), 1), 1.0, 0.0
    ).astype(bf16)
    for h in range(12):
        moved = mm(regroup, score_ref[pl.ds(h * WIN, WIN), :].astype(bf16)).astype(bf16)
        rows_ref[:, pl.ds(h * 16, 16), :] = moved.reshape(12, 16, WIN)
    total = jnp.zeros((192, ENTRIES), f32)
    base = entry_base((WIN, 1), 0)
    for column in range(12):
        total += mm(rows_ref[column], one_hot(base + column, ENTRIES))
    swapped = mm(swap_rows(), total.astype(bf16))
    halves = [
        jnp.concatenate([swapped[a * 16 : a * 16 + 12] for a in range(start, start + 6)], axis=1)
        for start in (0, 6)
    ]
    return jnp.concatenate(halves, axis=0).astype(bf16)


def pack(pieces, rows):
    count = sum(piece.shape[0] for piece in pieces)
    if rows > count:
        pieces = pieces + [jnp.zeros((rows - count, pieces[0].shape[1]), f32)]
    return jnp.concatenate(pieces, axis=0).astype(bf16)


def dense(pieces, rows, coarse=None):
    count = sum(piece.shape[0] for piece in pieces)
    if rows > count:
        pieces = pieces + [jnp.zeros((rows - count, 192), f32)]
    tokens = jnp.concatenate(pieces, axis=0)
    half = rows // 2
    side = jnp.concatenate([tokens[0:half, 128:192], tokens[half:rows, 128:192]], axis=1)
    filler = jnp.zeros((4, 128), f32)
    out = [tokens[:, 0:128], side]
    if coarse is None:
        out += [filler, filler]
    else:
        for start in range(0, 384, 128):
            out += [coarse[:, start : start + 128], filler]
    return jnp.concatenate(out, axis=0).astype(bf16)


def tokens_of(ref, rows):
    values = ref[...].astype(f32)
    side = values[rows : rows + rows // 2]
    side = jnp.concatenate([side[:, 0:64], side[:, 64:128]], axis=0)
    return jnp.concatenate([values[0:rows], side], axis=1).astype(bf16)


def coarse_of(ref, rows):
    values = ref[...].astype(f32)
    starts = [rows + rows // 2 + 40 * part for part in range(3)]
    return jnp.concatenate([values[start : start + QUAD] for start in starts], axis=1)


def quadrant(windows, qi, qj):
    part = (qi % 2 * 2 + qj % 2) * QUAD
    return windows[qi // 2 * 2 + qj // 2][part : part + QUAD]


def edge_kernel(tokens_ref, grad_ref, slon_ref, slat_ref, sdiag_ref, gloc_ref):
    tokens = tokens_ref[...].astype(f32)
    grads = grad_ref[...].astype(f32)

    def token_quadrant(row, start):
        pieces = []
        for z in range(2):
            for i in range(row, row + 3):
                place = (z * 12 + i) * 24 + start
                pieces.append(tokens[place : place + 6])
        return jnp.concatenate(pieces, axis=0)

    def grad_quadrant(hi, hj):
        pieces = [
            grads[hi * 3 + row, hj * 6 : hj * 6 + 6, z]
            for z in range(2)
            for row in range(3)
        ]
        return jnp.concatenate(pieces, axis=0)

    slon_ref[...] = dense([token_quadrant(q * 3, 18) for q in range(3)], 112, grad_quadrant(0, 1))
    slat_ref[...] = dense([token_quadrant(9, q * 6) for q in range(3)], 112, grad_quadrant(1, 0))
    sdiag_ref[...] = dense([token_quadrant(9, 18)], 48, grad_quadrant(1, 1))
    gloc_ref[...] = pack([grad_quadrant(0, 0)], 48)


def expand(table_ref, out_ref, held):
    table = jnp.concatenate([table_ref[:, b, :] for b in range(table_ref.shape[1])], axis=0)
    filler = jnp.zeros((4, ENTRIES), f32)
    pieces = []
    for a in range(12):
        pieces += [table[:, a * ENTRIES : (a + 1) * ENTRIES], filler]
    table = jnp.concatenate(pieces, axis=0)
    high = table.astype(bf16)
    low = (table - high.astype(f32)).astype(bf16)
    swap = swap_rows()
    table = jnp.concatenate(
        [mm(swap, high).astype(bf16), mm(swap, low).astype(bf16)], axis=0
    )
    entry = lax.broadcasted_iota(jnp.int32, (ENTRIES, WIN), 0)
    base = entry_base((1, WIN), 1)
    for column in range(12):
        picker = jnp.where(entry == base + column, 1.0, 0.0).astype(bf16)
        picked = mm(table, picker).astype(bf16)
        held[:, 0, column] = picked[0:192].reshape(12, 16, WIN)
        held[:, 1, column] = picked[192:384].reshape(12, 16, WIN)
    spots = lax.broadcasted_iota(jnp.int32, (WIN, 384), 1)
    spots = jnp.where(spots >= 192, spots - 192, spots)
    twice = jnp.where(spots == row_slot((WIN, 1), 0), 1.0, 0.0).astype(bf16)
    for h in range(12):
        out_ref[pl.ds(h * WIN, WIN), :] = mm(twice, held[h].reshape(384, WIN)) * LOG2E


def bias_kernel(table_ref, out_ref, held):
    expand(table_ref, out_ref, held)


def coarse_table_kernel(score_ref, table_ref, rows_ref):
    table_ref[...] = table_grad(score_ref, rows_ref)


def table_sum_kernel(fine_kept, fine_other, coarse_kept, coarse_other, fine_ref, coarse_ref):
    for kept, other, out_ref in (
        (fine_kept, fine_other, fine_ref),
        (coarse_kept, coarse_other, coarse_ref),
    ):
        total = kept[...].astype(f32) + other[...].astype(f32)
        total = jnp.concatenate([total[0:12], total[12:24]], axis=1)
        heads = out_ref.shape[0]
        for b in range(out_ref.shape[1]):
            out_ref[:, b, :] = total[b * heads : (b + 1) * heads]


def fine_windows(numbers, refs):
    tokens_ref, lon_ref, lat_ref, diag_ref, arrive_ref, bias_ref, mask_ref = refs[:7]
    qkv_ref, proj_ref, up_ref, down_ref, res_ref = refs[7:12]
    q_ref, k_ref, v_ref, probs_ref, n1_ref, r1_ref, n2_ref, r2_ref, slope_ref = refs[12:21]
    source = refs[21]
    source[0:576] = tokens_ref[...]
    source[576:688] = tokens_of(lon_ref, 112)
    source[688:800] = tokens_of(lat_ref, 112)
    source[800:848] = tokens_of(diag_ref, 48)
    everything = source[...]
    w_qkv = qkv_ref[...]
    bases = []
    for slot, w in enumerate(numbers):
        rows = pl.ds(slot * WIN, WIN)
        base = mm(one_hot(arrive_ref[pl.ds(w * WIN, WIN), :], 848), everything)
        normed, scale = norm(base)
        normed = normed.astype(bf16)
        n1_ref[rows, :] = normed
        r1_ref[rows, :] = scale
        q_ref[rows, :] = mm(normed, w_qkv[:, 0:192]).astype(bf16)
        k_ref[rows, :] = mm(normed, w_qkv[:, 192:384]).astype(bf16)
        v_ref[rows, :] = mm(normed, w_qkv[:, 384:576]).astype(bf16)
        bases.append(base)
    windows = {}
    for slot, w in enumerate(numbers):
        rows = pl.ds(slot * WIN, WIN)
        mixture = attend(
            q_ref[rows, :], k_ref[rows, :], v_ref[rows, :],
            bias_ref, w // 2 * 6 * WIN, mask_ref[w], probs_ref, slot * 6 * WIN,
        ).astype(bf16)
        first = bases[slot] + mm(mixture, proj_ref[...])
        renormed, scale = norm(first)
        renormed = renormed.astype(bf16)
        n2_ref[rows, :] = renormed
        r2_ref[rows, :] = scale
        active, slope = gelu_pair(mm(renormed, up_ref[...]))
        slope_ref[rows, :] = slope.astype(bf16)
        result = first + mm_nt(active.astype(bf16), down_ref[...])
        res_ref[rows, :] = result.astype(bf16)
        windows[w] = result
    return windows


def fine_edge_kernel(*refs):
    slon_ref, slat_ref, sdiag_ref = refs[11:14]
    windows = fine_windows((1, 2, 3), refs[:11] + refs[14:])
    slon_ref[...] = dense([quadrant(windows, q, 3) for q in range(3)], 112)
    slat_ref[...] = dense([quadrant(windows, 3, q) for q in range(3)], 112)
    sdiag_ref[...] = dense([quadrant(windows, 3, 3)], 48)


def fine_inner_kernel(*refs):
    fine_windows((0,), refs)


def coarse_kernel(
    inner_ref, res_ref, lon_ref, lat_ref, diag_ref, merge_ref, split_ref, bias_ref, mask_ref,
    gloc_ref, glon_ref, glat_ref, gdiag_ref,
    reduce_ref, qkv_ref, proj_ref, up_ref, down_ref,
    c0, c1, c2, c3, dlon_ref, dlat_ref, ddiag_ref, dloc_ref, score_ref,
    source, probs_ref, parts_ref,
):
    source[0:144] = inner_ref[...]
    source[144:576] = res_ref[...]
    source[576:688] = tokens_of(lon_ref, 112)
    source[688:800] = tokens_of(lat_ref, 112)
    source[800:848] = tokens_of(diag_ref, 48)
    everything = source[...]
    parts = [mm(one_hot(merge_ref[pl.ds(k * WIN, WIN), :], 848), everything) for k in range(4)]
    mean = sum(jnp.sum(part, axis=-1, keepdims=True) for part in parts) * (1.0 / 768)
    parts = [part - mean for part in parts]
    square = sum(jnp.sum(part * part, axis=-1, keepdims=True) for part in parts)
    merge_scale = lax.rsqrt(square * (1.0 / 768) + 1e-5)
    parts = [(part * merge_scale).astype(bf16) for part in parts]
    base = sum(mm(parts[k], reduce_ref[k * 192 : (k + 1) * 192]) for k in range(4))
    base = base.astype(bf16).astype(f32)
    normed, scale1 = norm(base)
    normed = normed.astype(bf16)
    queries = mm(normed, qkv_ref[:, 0:384]).astype(bf16)
    keys = mm(normed, qkv_ref[:, 384:768]).astype(bf16)
    values = mm(normed, qkv_ref[:, 768:1152]).astype(bf16)
    mixture = attend(queries, keys, values, bias_ref, 0, mask_ref[...], probs_ref, 0).astype(bf16)
    first = base + mm(mixture, proj_ref[...])
    renormed, scale2 = norm(first)
    renormed = renormed.astype(bf16)
    active, slope = gelu_pair(mm(renormed, up_ref[...]))
    result = first + mm(active.astype(bf16), down_ref[...])
    for index, out in enumerate((c0, c1, c2, c3)):
        out[...] = pack([result[index * QUAD : (index + 1) * QUAD]], 48)

    grad = jnp.concatenate(
        [
            coarse_of(gdiag_ref, 48),
            coarse_of(glat_ref, 112),
            coarse_of(glon_ref, 112),
            gloc_ref[...].astype(f32)[:QUAD],
        ],
        axis=0,
    )
    inner = mm_nt(grad.astype(bf16), down_ref[...]) * slope
    grad = grad + norm_back(mm_nt(inner.astype(bf16), up_ref[...]), renormed.astype(f32), scale2)
    mix_grad = mm_nt(grad.astype(bf16), proj_ref[...]).astype(bf16)
    dq, dk, dv = attend_back(queries, keys, values, mix_grad, probs_ref, 0, score_ref, False)
    normed_grad = (
        mm_nt(dq.astype(bf16), qkv_ref[:, 0:384])
        + mm_nt(dk.astype(bf16), qkv_ref[:, 384:768])
        + mm_nt(dv.astype(bf16), qkv_ref[:, 768:1152])
    )
    grad = grad + norm_back(normed_grad, normed.astype(f32), scale1)
    grad = grad.astype(bf16)
    grads = [mm_nt(grad, reduce_ref[k * 192 : (k + 1) * 192]) for k in range(4)]
    mean = sum(jnp.sum(g, axis=-1, keepdims=True) for g in grads) * (1.0 / 768)
    along = sum(
        jnp.sum(g * p.astype(f32), axis=-1, keepdims=True) for g, p in zip(grads, parts)
    ) * (1.0 / 768)
    for k in range(4):
        part = (grads[k] - mean - parts[k].astype(f32) * along) * merge_scale
        parts_ref[pl.ds(k * WIN, WIN), :] = part.astype(bf16)
    everything = parts_ref[...]
    moved = mm(one_hot(split_ref[...], 576), everything)
    dlon_ref[...] = dense([moved[0:112]], 112)
    dloc_ref[...] = moved[112:448].astype(bf16)
    dlat_ref[...] = dense([moved[448:560]], 112)
    ddiag_ref[...] = dense([moved[560:608]], 48)


def band_back(parts, source, back_ref, weights, outs, score_ref):
    proj_ref, up_ref, down_ref = weights
    grad_ref, dq_ref, dk_ref, dv_ref = outs
    everything = source[...]
    for across, (w, slot, saved) in enumerate(parts):
        q_ref, k_ref, v_ref, probs_ref, n2_ref, r2_ref, slope_ref = saved
        rows = pl.ds(slot * WIN, WIN)
        here = pl.ds(across * WIN, WIN)
        grad = mm(one_hot(back_ref[pl.ds(w * WIN, WIN), :], everything.shape[0]), everything)
        inner = mm(grad.astype(bf16), down_ref[...]) * slope_ref[rows, :].astype(f32)
        grad = grad + norm_back(
            mm_nt(inner.astype(bf16), up_ref[...]), n2_ref[rows, :].astype(f32), r2_ref[rows, :]
        )
        grad_ref[here, :] = grad
        mix_grad = mm_nt(grad.astype(bf16), proj_ref[...]).astype(bf16)
        dq, dk, dv = attend_back(
            q_ref[rows, :], k_ref[rows, :], v_ref[rows, :], mix_grad,
            probs_ref, slot * 6 * WIN, score_ref, across == 1,
        )
        dq_ref[here, :] = dq.astype(bf16)
        dk_ref[here, :] = dk.astype(bf16)
        dv_ref[here, :] = dv.astype(bf16)


def first_band_kernel(dlon_ref, dloc_ref, back_ref, *refs):
    *refs, source = refs
    source[0:112] = tokens_of(dlon_ref, 112)
    source[112:448] = dloc_ref[...]
    parts = ((0, 0, refs[:7]), (1, 0, refs[7:14]))
    band_back(parts, source, back_ref, refs[14:17], refs[17:21], refs[21])


def second_band_kernel(
    dlon_ref, dloc_ref, dlat_ref, ddiag_ref, back_ref, first_ref, *refs
):
    *refs, source, score_ref, rows_ref = refs
    source[0:112] = tokens_of(dlon_ref, 112)
    source[112:448] = dloc_ref[...]
    source[448:560] = tokens_of(dlat_ref, 112)
    source[560:608] = tokens_of(ddiag_ref, 48)
    half = 6 * WIN
    score_ref[pl.ds(0, half), :] = first_ref[...]
    parts = ((2, 1, refs[:7]), (3, 2, refs[:7]))
    band_back(
        parts, source, back_ref, refs[7:10], refs[10:14], score_ref.at[pl.ds(half, half)]
    )
    refs[14][...] = table_grad(score_ref, rows_ref)


def qkv_back_kernel(*refs):
    bands, refs = (refs[:4], refs[4:8]), refs[8:]
    norms = (refs[0:2], refs[2:4])
    qkv_ref, clon_ref, clat_ref, cdiag_ref = refs[4:8]
    res_ref, slon_ref, slat_ref, sdiag_ref = refs[8:]
    w_qkv = qkv_ref[...]
    windows = []
    for w in range(4):
        grad_ref, dq_ref, dk_ref, dv_ref = bands[w // 2]
        rows = pl.ds(w * WIN, WIN)
        here = pl.ds(w % 2 * WIN, WIN)
        normed_grad = (
            mm_nt(dq_ref[here, :], w_qkv[:, 0:192])
            + mm_nt(dk_ref[here, :], w_qkv[:, 192:384])
            + mm_nt(dv_ref[here, :], w_qkv[:, 384:576])
        )
        n1_ref, r1_ref = norms[min(w, 1)]
        slot = pl.ds(max(w - 1, 0) * WIN, WIN)
        result = grad_ref[here, :] + norm_back(
            normed_grad, n1_ref[slot, :].astype(f32), r1_ref[slot, :]
        )
        res_ref[rows, :] = result.astype(bf16)
        windows.append(result)
    clon, clat, cdiag = [
        ref[...].astype(f32)[:QUAD] for ref in (clon_ref, clat_ref, cdiag_ref)
    ]
    slon_ref[...] = dense([quadrant(windows, q, 0) for q in range(1, 4)], 112, clon)
    slat_ref[...] = dense([quadrant(windows, 0, q) for q in range(1, 4)], 112, clat)
    sdiag_ref[...] = dense([quadrant(windows, 0, 0)], 48, cdiag)


def last_kernel(
    res_ref, lon_ref, lat_ref, diag_ref, leave_ref, cloc_ref, result_ref,
    tokens_ref, coarse_ref, source, coarse_source,
):
    source[0:576] = res_ref[...]
    source[576:688] = tokens_of(lon_ref, 112)
    source[688:800] = tokens_of(lat_ref, 112)
    source[800:848] = tokens_of(diag_ref, 48)
    everything = source[...]
    for w in range(4):
        rows = pl.ds(w * WIN, WIN)
        tokens_ref[rows, :] = mm(one_hot(leave_ref[rows, :], 848), everything).astype(bf16)
    coarse_source[0:48] = cloc_ref[...]
    coarse_source[48:96] = pack([coarse_of(lon_ref, 112)], 48)
    coarse_source[96:144] = pack([coarse_of(lat_ref, 112)], 48)
    coarse_source[144:192] = pack([coarse_of(diag_ref, 48)], 48)
    moved = mm(one_hot(result_ref[...], 192), coarse_source[...])
    for z in range(2):
        for row in range(6):
            start = z * 72 + row * 12
            coarse_ref[z, row] = moved[start : start + 12].astype(bf16)


def run(kernel, outs, scratch, weight, inputs):
    shapes = [jax.ShapeDtypeStruct(shape, kind) for shape, kind in outs]
    size = sum(math.prod(s.shape) * s.dtype.itemsize for s in shapes)
    size += sum(x.size * x.dtype.itemsize for x in inputs)
    return pl.pallas_call(
        kernel,
        out_shape=shapes,
        scratch_shapes=[pltpu.VMEM(shape, kind) for shape, kind in scratch],
        compiler_params=pltpu.CompilerParams(vmem_limit_bytes=VMEM),
        cost_estimate=pl.CostEstimate(
            flops=weight * 1_000_000_000, bytes_accessed=size, transcendentals=0
        ),
    )(*inputs)


def move(value, lon_steps, lat_steps):
    lon, lat = lax.axis_size("lon"), lax.axis_size("lat")
    if lat_steps == 0:
        pairs = [(s, (s + lon_steps) % lon) for s in range(lon)]
        return lax.ppermute(value, "lon", pairs)
    if lon_steps == 0:
        pairs = [(s, (s + lat_steps) % lat) for s in range(lat)]
        return lax.ppermute(value, "lat", pairs)
    pairs = [
        (b * lat + a, (b + lon_steps) % lon * lat + (a + lat_steps) % lat)
        for b in range(lon)
        for a in range(lat)
    ]
    return lax.ppermute(value, ("lon", "lat"), pairs)


def send(pieces, steps):
    on_lon, on_lat, on_both = pieces
    return move(on_lon, steps, 0), move(on_lat, 0, steps), move(on_both, steps, steps)


def swap(value, step):
    count = lax.axis_size("lon")
    return lax.ppermute(value, "lon", [(s, s ^ step) for s in range(count)])


def add(mine, other):
    return (mine.astype(f32) + other.astype(f32)).astype(bf16)


def lon_steps():
    return [1 << bit for bit in range(lax.axis_size("lon").bit_length() - 1)]


def body(
    tokens, mask_ids, fine_qkv, fine_proj, fine_up, fine_down, fine_bias, reduce_weight,
    coarse_qkv, coarse_proj, coarse_up, coarse_down, coarse_bias, out_grad,
):
    lat_index = lax.axis_index("lat")
    fine_down = fine_down.T
    flat = tokens.reshape(576, 192)
    column = lambda index: jnp.asarray(index).reshape(-1, 1)
    tok = ((576, 192), bf16)
    edges = [((176, 128), bf16), ((176, 128), bf16), ((80, 128), bf16)]
    wide_edges = [((288, 128), bf16), ((288, 128), bf16), ((192, 128), bf16)]
    quad = ((48, 384), bf16)
    scores = ((12 * WIN, WIN), f32)
    table_rows = ((12, 192, WIN), bf16)
    held = ((12, 2, 12, 16, WIN), bf16)

    *sent, grad_here = run(
        edge_kernel, wide_edges + [quad], [], 1, (flat, out_grad.transpose(1, 2, 0, 3))
    )
    first = send(sent, 1)
    (fine_table,) = run(
        bias_kernel, [scores], [held], 2,
        (fine_bias.transpose(1, 0, 2),),
    )

    row = lax.broadcasted_iota(jnp.int32, mask_ids.shape, 1) + lat_index * mask_ids.shape[1]
    labels = mask_ids * 2 + jnp.where(row < 3, 1, 0)
    labels = labels.reshape(2, 2, 2, 3, 2, 2, 6)
    labels = labels.transpose(1, 4, 2, 5, 0, 3, 6).reshape(4, WIN)
    fine_mask = jnp.where(labels[:, :, None] == labels[:, None, :], 0.0, -1e30).astype(f32)
    low_half = jnp.arange(WIN) < WIN // 2
    coarse_mask = jnp.where(
        (low_half[:, None] == low_half[None, :]) | (lat_index != 0), 0.0, -1e30
    ).astype(f32)

    def saved_shapes(windows):
        rows = windows * WIN
        part = ((rows, 192), bf16)
        scale = ((rows, 1), f32)
        probs = ((6 * rows, WIN), bf16)
        return [part] * 3 + [probs, part, scale, part, scale, ((rows, 768), bf16)]

    inputs = (
        flat, *first, column(ARRIVE), fine_table, fine_mask,
        fine_qkv, fine_proj, fine_up, fine_down,
    )
    gathered = [((848, 192), bf16)]
    outer = run(
        fine_edge_kernel,
        edges + [((3 * WIN, 192), bf16)] + saved_shapes(3),
        gathered, 6, inputs,
    )
    arrived = send(outer[:3], 1)
    flat_after, _ = lax.optimization_barrier((flat, outer[3]))
    inner = run(
        fine_inner_kernel,
        [((WIN, 192), bf16)] + saved_shapes(1),
        gathered, 2, (flat_after, *inputs[1:]),
    )
    late_table, _ = lax.optimization_barrier((coarse_bias.transpose(1, 0, 2), outer[3]))
    (coarse_table,) = run(
        bias_kernel, [scores], [held], 2, (late_table,)
    )
    coarse = run(
        coarse_kernel,
        [quad] * 4 + edges + [((336, 192), bf16), scores],
        [((848, 192), bf16), ((12 * WIN, WIN), bf16), ((576, 192), bf16)],
        9,
        (
            inner[0], outer[3], *arrived, column(MERGE), column(SPLIT), coarse_table, coarse_mask, grad_here, *first,
            reduce_weight, coarse_qkv, coarse_proj, coarse_up, coarse_down,
        ),
    )
    c00, c01, c10, c11 = coarse[:4]
    arrived = send(coarse[4:7], -1)
    dlon, dlat, ddiag = arrived
    dlat, scored = lax.optimization_barrier((dlat, coarse[8]))
    (coarse_grad,) = run(
        coarse_table_kernel, [((24, 6 * ENTRIES), bf16)], [table_rows], 2,
        (scored,),
    )
    steps = lon_steps()
    other = swap(coarse_grad, steps[-1])
    half_tok = ((288, 192), bf16)
    half_outs = [((288, 192), f32)] + [half_tok] * 3
    q, k, v, probs, n1, r1, n2, r2, slope = outer[4:]
    outer_saved = (q, k, v, probs, n2, r2, slope)
    q, k, v, probs, n1_inner, r1_inner, n2, r2, slope = inner[1:]
    inner_saved = (q, k, v, probs, n2, r2, slope)
    weights = (fine_proj, fine_up, fine_down)
    *first_half, first_scores = run(
        first_band_kernel,
        half_outs + [((6 * WIN, WIN), f32)],
        [((448, 192), bf16)],
        4,
        (dlon, coarse[7], column(BACK), *inner_saved, *outer_saved, *weights),
    )
    first_scores, other = lax.optimization_barrier((first_scores, other))
    coarse_grad = add(coarse_grad, other)
    other = swap(coarse_grad, steps[-2])
    *second_half, fine_grad = run(
        second_band_kernel,
        half_outs + [((24, 6 * ENTRIES), bf16)],
        [((608, 192), bf16), scores, table_rows],
        5,
        (
            dlon, coarse[7], dlat, ddiag, column(BACK), first_scores,
            *outer_saved, *weights,
        ),
    )
    second_half[0], other = lax.optimization_barrier((second_half[0], other))
    coarse_grad = add(coarse_grad, other)
    for step in reversed(steps[:-2]):
        coarse_sums = (coarse_grad, swap(coarse_grad, step))
        coarse_grad = add(*coarse_sums)
    other = swap(fine_grad, steps[-1])
    fine_back = list(run(
        qkv_back_kernel, [tok] + wide_edges, [], 2,
        (*first_half, *second_half, n1_inner, r1_inner, n1, r1, fine_qkv, c10, c01, c00),
    ))
    alon, alat, adiag = send(fine_back[1:4], -1)
    alat, other = lax.optimization_barrier((alat, other))
    fine_grad = add(fine_grad, other)
    for step in reversed(steps[:-1]):
        fine_sums = (fine_grad, swap(fine_grad, step))
        fine_grad = add(*fine_sums)
    d_tokens, coarse_result = run(
        last_kernel,
        [tok, ((2, 6, 12, 384), bf16)],
        [((848, 192), bf16), ((192, 384), bf16)],
        1,
        (fine_back[0], alon, alat, adiag, column(LEAVE), c11, column(RESULT)),
    )
    fine_out, coarse_out = run(
        table_sum_kernel,
        [((HEADS_F, 2, 12 * ENTRIES), f32), ((HEADS_C, 1, 12 * ENTRIES), f32)],
        [], 1, (*fine_sums, *coarse_sums),
    )
    return (
        coarse_result,
        d_tokens.reshape(tokens.shape),
        fine_out.transpose(1, 0, 2),
        coarse_out.transpose(1, 0, 2),
    )


def solution(mesh):
    grid = P(None, "lat", "lon", None)
    bands = P("lat", None, None)
    in_specs = (
        grid, P(None, "lat", "lon"), P(), P(), P(), P(), bands,
        P(), P(), P(), P(), P(), bands, grid,
    )
    out_specs = (grid, grid, bands, bands)
    return jax.shard_map(body, mesh=mesh, in_specs=in_specs, out_specs=out_specs, check_vma=False)
```

```python
import math

import jax
import jax.numpy as jnp
import numpy as np
from jax import lax
from jax.experimental import pallas as pl
from jax.experimental.pallas import tpu as pltpu
from jax.sharding import PartitionSpec as P

HEADS_F = 6
HEADS_C = 12
HEAD = 32
WIN = 144
QUAD = 36
SPAN = 23
ENTRIES = 276
LOG2E = math.log2(math.e)
VMEM = 20 * 1024 * 1024
f32 = jnp.float32
bf16 = jnp.bfloat16


def spot(z, i, j):
    quadrant = (i % 6) // 3 * 2 + (j % 12) // 6
    return quadrant * QUAD + z * 18 + i % 3 * 6 + j % 6


def fine_spot(z, i, j):
    return (i // 6 * 2 + j // 12) * WIN + spot(z, i, j)


def in_quad(z, i, j):
    return z * 18 + i % 3 * 6 + j % 6


def index_maps():
    arrive = np.zeros(576, np.int32)
    merge = np.zeros(576, np.int32)
    split = np.full(608, -1, np.int32)
    back = np.zeros(576, np.int32)
    leave = np.zeros(576, np.int32)
    for z in range(2):
        for i in range(12):
            for j in range(24):
                here = fine_spot(z, i, j)
                if i >= 3 and j >= 6:
                    arrive[here] = z * 288 + (i - 3) * 24 + j - 6
                    came = fine_spot(z, i - 3, j - 6)
                elif i >= 3:
                    came = 576 + (i - 3) // 3 * QUAD + in_quad(z, i, j)
                elif j >= 6:
                    came = 688 + (j - 6) // 6 * QUAD + in_quad(z, i, j)
                else:
                    came = 800 + in_quad(z, i, j)
                if came >= 576:
                    arrive[here] = came
                part = (i % 2 + j % 2 * 2) * WIN + spot(z, i // 2, j // 2)
                merge[part] = came
                if i >= 3 and j >= 6:
                    slot = 112 + z * 162 + (i - 3) * 18 + j - 6
                    back[fine_spot(z, i - 3, j - 6)] = slot
                elif i >= 3:
                    slot = z * 54 + (i - 3) * 6 + j
                    back[fine_spot(z, i - 3, j + 18)] = slot
                elif j >= 6:
                    slot = 448 + z * 54 + i * 18 + j - 6
                    back[fine_spot(z, i + 9, j - 6)] = slot
                else:
                    slot = 560 + z * 18 + i * 6 + j
                    back[fine_spot(z, i + 9, j + 18)] = slot
                split[slot] = part
                natural = z * 288 + i * 24 + j
                if i < 9 and j < 18:
                    leave[natural] = fine_spot(z, i + 3, j + 6)
                elif i < 9:
                    leave[natural] = 576 + i // 3 * QUAD + in_quad(z, i, j)
                elif j < 18:
                    leave[natural] = 688 + j // 6 * QUAD + in_quad(z, i, j)
                else:
                    leave[natural] = 800 + in_quad(z, i, j)
    result = np.zeros(WIN, np.int32)
    for z in range(2):
        for i in range(6):
            for j in range(12):
                result[z * 72 + i * 12 + j] = (i // 3 * 2 + j // 6) * 48 + in_quad(z, i, j)
    return arrive, merge, split, back, leave, result


ARRIVE, MERGE, SPLIT, BACK, LEAVE, RESULT = index_maps()


def places(shape, axis):
    t = lax.broadcasted_iota(jnp.int32, shape, axis)
    quad = (t * 57) >> 11
    t = t - quad * QUAD
    level = (t * 57) >> 10
    t = t - level * 18
    row = (t * 43) >> 8
    return level * 6 + (quad >> 1) * 3 + row, t - row * 6 + (quad & 1) * 6


def entry_base(shape, axis):
    row, column = places(shape, axis)
    return row * SPAN + 11 - column


def row_slot(shape, axis):
    row, column = places(shape, axis)
    return column * 16 + row


def one_hot(column, width):
    spots = lax.broadcasted_iota(jnp.int32, (column.shape[0], width), 1)
    return jnp.where(spots == column, 1.0, 0.0).astype(bf16)


def mm(left, right):
    return jnp.dot(left, right, preferred_element_type=f32)


def mm_nt(left, right):
    return lax.dot_general(left, right, (((1,), (1,)), ((), ())), preferred_element_type=f32)


def mm_tn(left, right):
    return lax.dot_general(left, right, (((0,), (0,)), ((), ())), preferred_element_type=f32)


def norm(values):
    centred = values - jnp.mean(values, axis=-1, keepdims=True)
    scale = lax.rsqrt(jnp.mean(centred * centred, axis=-1, keepdims=True) + 1e-5)
    return centred * scale, scale


def norm_back(grad, normed, scale):
    along = jnp.mean(grad * normed, axis=-1, keepdims=True)
    return (grad - jnp.mean(grad, axis=-1, keepdims=True) - normed * along) * scale


def gelu_pair(x):
    u = jnp.abs(x) * math.sqrt(0.5)
    t = 1.0 / (1.0 + 0.3275911 * u)
    e = jnp.exp(-u * u)
    poly = 1.421413741 + t * (-1.453152027 + t * 1.061405429)
    tail = 0.5 * (t * (0.254829592 + t * (-0.284496736 + t * poly))) * e
    below = jnp.where(x >= 0, 1.0 - tail, tail)
    return x * below, below + x * (e * (1.0 / math.sqrt(2 * math.pi)))


def groups(channels):
    return [(start, min(start + 128, channels)) for start in range(0, channels, 128)]


def head_lanes(rows, width):
    return lax.broadcasted_iota(jnp.int32, (rows, width), 1) // HEAD


def stack_heads(part):
    lanes = head_lanes(part.shape[0], part.shape[1])
    count = part.shape[1] // HEAD
    zero = jnp.zeros_like(part)
    return jnp.concatenate([jnp.where(lanes == h, part, zero) for h in range(count)], axis=0)


def pick_heads(stacked):
    width = stacked.shape[1]
    lanes = head_lanes(WIN, width)
    total = stacked[:WIN]
    for h in range(1, width // HEAD):
        total = jnp.where(lanes == h, stacked[h * WIN : (h + 1) * WIN], total)
    return total


def attend(queries, keys, values, bias_ref, bias_row, mask, probs_ref, probs_row):
    mixed = []
    for start, stop in groups(queries.shape[1]):
        count = (stop - start) // HEAD
        scores = mm_nt(stack_heads(queries[:, start:stop]), keys[:, start:stop])
        row = start // HEAD * WIN
        for h in range(count):
            here = row + h * WIN
            logits = (
                scores[h * WIN : (h + 1) * WIN] * (HEAD**-0.5 * LOG2E)
                + bias_ref[pl.ds(bias_row + here, WIN), :]
                + mask
            )
            raised = jnp.exp2(logits - jnp.max(logits, axis=-1, keepdims=True))
            probs = raised * (1.0 / jnp.sum(raised, axis=-1, keepdims=True))
            probs_ref[pl.ds(probs_row + here, WIN), :] = probs.astype(bf16)
        stacked = mm(probs_ref[pl.ds(probs_row + row, count * WIN), :], values[:, start:stop])
        mixed.append(pick_heads(stacked))
    return jnp.concatenate(mixed, axis=1)


def attend_back(queries, keys, values, mix_grad, probs_ref, probs_row, score_ref, add):
    query_grad, key_grad, value_grad = [], [], []
    for start, stop in groups(queries.shape[1]):
        count = (stop - start) // HEAD
        row = start // HEAD * WIN
        probs_all = probs_ref[pl.ds(probs_row + row, count * WIN), :]
        grads = stack_heads(mix_grad[:, start:stop])
        value_grad.append(mm_tn(probs_all, grads))
        probs_grad = mm_nt(grads, values[:, start:stop])
        pieces = []
        for h in range(count):
            probs = probs_all[h * WIN : (h + 1) * WIN].astype(f32)
            grad = probs_grad[h * WIN : (h + 1) * WIN]
            weighted = grad * probs
            score_grad = weighted - probs * jnp.sum(weighted, axis=-1, keepdims=True)
            place = pl.ds(row + h * WIN, WIN)
            if add:
                score_ref[place, :] += score_grad
            else:
                score_ref[place, :] = score_grad
            pieces.append(score_grad.astype(bf16))
        score_all = jnp.concatenate(pieces, axis=0)
        query_grad.append(pick_heads(mm(score_all, keys[:, start:stop])))
        key_grad.append(mm_tn(score_all, stack_heads(queries[:, start:stop])))
    scale = HEAD**-0.5
    return (
        jnp.concatenate(query_grad, axis=1) * scale,
        jnp.concatenate(key_grad, axis=1) * scale,
        jnp.concatenate(value_grad, axis=1),
    )


def swap_rows():
    row = lax.broadcasted_iota(jnp.int32, (192, 192), 0)
    return jnp.where(
        lax.broadcasted_iota(jnp.int32, (192, 192), 1) == row % 16 * 16 + row // 16, 1.0, 0.0
    ).astype(bf16)


def table_grad(score_ref, rows_ref):
    regroup = jnp.where(
        lax.broadcasted_iota(jnp.int32, (192, WIN), 0) == row_slot((1, WIN), 1), 1.0, 0.0
    ).astype(bf16)
    for h in range(12):
        moved = mm(regroup, score_ref[pl.ds(h * WIN, WIN), :].astype(bf16)).astype(bf16)
        rows_ref[:, pl.ds(h * 16, 16), :] = moved.reshape(12, 16, WIN)
    total = jnp.zeros((192, ENTRIES), f32)
    base = entry_base((WIN, 1), 0)
    for column in range(12):
        total += mm(rows_ref[column], one_hot(base + column, ENTRIES))
    swapped = mm(swap_rows(), total.astype(bf16))
    halves = [
        jnp.concatenate([swapped[a * 16 : a * 16 + 12] for a in range(start, start + 6)], axis=1)
        for start in (0, 6)
    ]
    return jnp.concatenate(halves, axis=0).astype(bf16)


def pack(pieces, rows):
    count = sum(piece.shape[0] for piece in pieces)
    if rows > count:
        pieces = pieces + [jnp.zeros((rows - count, pieces[0].shape[1]), f32)]
    return jnp.concatenate(pieces, axis=0).astype(bf16)


def dense(pieces, rows, coarse=None):
    count = sum(piece.shape[0] for piece in pieces)
    if rows > count:
        pieces = pieces + [jnp.zeros((rows - count, 192), f32)]
    tokens = jnp.concatenate(pieces, axis=0)
    half = rows // 2
    side = jnp.concatenate([tokens[0:half, 128:192], tokens[half:rows, 128:192]], axis=1)
    filler = jnp.zeros((4, 128), f32)
    out = [tokens[:, 0:128], side]
    if coarse is None:
        out += [filler, filler]
    else:
        for start in range(0, 384, 128):
            out += [coarse[:, start : start + 128], filler]
    return jnp.concatenate(out, axis=0).astype(bf16)


def tokens_of(ref, rows):
    values = ref[...].astype(f32)
    side = values[rows : rows + rows // 2]
    side = jnp.concatenate([side[:, 0:64], side[:, 64:128]], axis=0)
    return jnp.concatenate([values[0:rows], side], axis=1).astype(bf16)


def coarse_of(ref, rows):
    values = ref[...].astype(f32)
    starts = [rows + rows // 2 + 40 * part for part in range(3)]
    return jnp.concatenate([values[start : start + QUAD] for start in starts], axis=1)


def quadrant(windows, qi, qj):
    part = (qi % 2 * 2 + qj % 2) * QUAD
    return windows[qi // 2 * 2 + qj // 2][part : part + QUAD]


def edge_kernel(tokens_ref, slon_ref, slat_ref, sdiag_ref):
    tokens = tokens_ref[...].astype(f32)

    def token_quadrant(row, start):
        pieces = []
        for z in range(2):
            for i in range(row, row + 3):
                place = (z * 12 + i) * 24 + start
                pieces.append(tokens[place : place + 6])
        return jnp.concatenate(pieces, axis=0)

    slon_ref[...] = dense([token_quadrant(q * 3, 18) for q in range(3)], 112)
    slat_ref[...] = dense([token_quadrant(9, q * 6) for q in range(3)], 112)
    sdiag_ref[...] = dense([token_quadrant(9, 18)], 48)


def expand(table_ref, out_ref, held):
    table = jnp.concatenate([table_ref[:, b, :] for b in range(table_ref.shape[1])], axis=0)
    filler = jnp.zeros((4, ENTRIES), f32)
    pieces = []
    for a in range(12):
        pieces += [table[:, a * ENTRIES : (a + 1) * ENTRIES], filler]
    table = jnp.concatenate(pieces, axis=0)
    high = table.astype(bf16)
    low = (table - high.astype(f32)).astype(bf16)
    swap = swap_rows()
    table = jnp.concatenate(
        [mm(swap, high).astype(bf16), mm(swap, low).astype(bf16)], axis=0
    )
    entry = lax.broadcasted_iota(jnp.int32, (ENTRIES, WIN), 0)
    base = entry_base((1, WIN), 1)
    for column in range(12):
        picker = jnp.where(entry == base + column, 1.0, 0.0).astype(bf16)
        picked = mm(table, picker).astype(bf16)
        held[:, 0, column] = picked[0:192].reshape(12, 16, WIN)
        held[:, 1, column] = picked[192:384].reshape(12, 16, WIN)
    spots = lax.broadcasted_iota(jnp.int32, (WIN, 384), 1)
    spots = jnp.where(spots >= 192, spots - 192, spots)
    twice = jnp.where(spots == row_slot((WIN, 1), 0), 1.0, 0.0).astype(bf16)
    for h in range(12):
        out_ref[pl.ds(h * WIN, WIN), :] = mm(twice, held[h].reshape(384, WIN)) * LOG2E


def bias_kernel(table_ref, out_ref, held):
    expand(table_ref, out_ref, held)


def coarse_table_kernel(score_ref, table_ref, rows_ref):
    table_ref[...] = table_grad(score_ref, rows_ref)


def table_sum_kernel(fine_kept, fine_other, coarse_kept, coarse_other, fine_ref, coarse_ref):
    for kept, other, out_ref in (
        (fine_kept, fine_other, fine_ref),
        (coarse_kept, coarse_other, coarse_ref),
    ):
        total = kept[...].astype(f32) + other[...].astype(f32)
        total = jnp.concatenate([total[0:12], total[12:24]], axis=1)
        heads = out_ref.shape[0]
        for b in range(out_ref.shape[1]):
            out_ref[:, b, :] = total[b * heads : (b + 1) * heads]


def fine_windows(numbers, refs):
    tokens_ref, lon_ref, lat_ref, diag_ref, arrive_ref, bias_ref, mask_ref = refs[:7]
    qkv_ref, proj_ref, up_ref, down_ref, res_ref = refs[7:12]
    q_ref, k_ref, v_ref, probs_ref, n1_ref, r1_ref, n2_ref, r2_ref, slope_ref = refs[12:21]
    source = refs[21]
    source[0:576] = tokens_ref[...]
    source[576:688] = tokens_of(lon_ref, 112)
    source[688:800] = tokens_of(lat_ref, 112)
    source[800:848] = tokens_of(diag_ref, 48)
    everything = source[...]
    w_qkv = qkv_ref[...]
    bases = []
    for slot, w in enumerate(numbers):
        rows = pl.ds(slot * WIN, WIN)
        base = mm(one_hot(arrive_ref[pl.ds(w * WIN, WIN), :], 848), everything)
        normed, scale = norm(base)
        normed = normed.astype(bf16)
        n1_ref[rows, :] = normed
        r1_ref[rows, :] = scale
        q_ref[rows, :] = mm(normed, w_qkv[:, 0:192]).astype(bf16)
        k_ref[rows, :] = mm(normed, w_qkv[:, 192:384]).astype(bf16)
        v_ref[rows, :] = mm(normed, w_qkv[:, 384:576]).astype(bf16)
        bases.append(base)
    windows = {}
    for slot, w in enumerate(numbers):
        rows = pl.ds(slot * WIN, WIN)
        mixture = attend(
            q_ref[rows, :], k_ref[rows, :], v_ref[rows, :],
            bias_ref, w // 2 * 6 * WIN, mask_ref[w], probs_ref, slot * 6 * WIN,
        ).astype(bf16)
        first = bases[slot] + mm(mixture, proj_ref[...])
        renormed, scale = norm(first)
        renormed = renormed.astype(bf16)
        n2_ref[rows, :] = renormed
        r2_ref[rows, :] = scale
        active, slope = gelu_pair(mm(renormed, up_ref[...]))
        slope_ref[rows, :] = slope.astype(bf16)
        result = first + mm_nt(active.astype(bf16), down_ref[...])
        res_ref[rows, :] = result.astype(bf16)
        windows[w] = result
    return windows


def fine_edge_kernel(grad_ref, *refs):
    slon_ref, slat_ref, sdiag_ref, gloc_ref = refs[11:15]
    windows = fine_windows((1, 2, 3), refs[:11] + refs[15:])
    grads = grad_ref[...].astype(f32)

    def grad_quadrant(hi, hj):
        pieces = [
            grads[hi * 3 + row, hj * 6 : hj * 6 + 6, z] for z in range(2) for row in range(3)
        ]
        return jnp.concatenate(pieces, axis=0)

    slon_ref[...] = dense([quadrant(windows, q, 3) for q in range(3)], 112, grad_quadrant(0, 1))
    slat_ref[...] = dense([quadrant(windows, 3, q) for q in range(3)], 112, grad_quadrant(1, 0))
    sdiag_ref[...] = dense([quadrant(windows, 3, 3)], 48, grad_quadrant(1, 1))
    gloc_ref[...] = pack([grad_quadrant(0, 0)], 48)


def fine_inner_kernel(*refs):
    fine_windows((0,), refs)


def coarse_kernel(
    inner_ref, res_ref, lon_ref, lat_ref, diag_ref, merge_ref, split_ref, bias_ref, mask_ref,
    gloc_ref,
    reduce_ref, qkv_ref, proj_ref, up_ref, down_ref,
    c0, c1, c2, c3, dlon_ref, dlat_ref, ddiag_ref, dloc_ref, score_ref,
    source, probs_ref, parts_ref,
):
    source[0:144] = inner_ref[...]
    source[144:576] = res_ref[...]
    source[576:688] = tokens_of(lon_ref, 112)
    source[688:800] = tokens_of(lat_ref, 112)
    source[800:848] = tokens_of(diag_ref, 48)
    everything = source[...]
    parts = [mm(one_hot(merge_ref[pl.ds(k * WIN, WIN), :], 848), everything) for k in range(4)]
    mean = sum(jnp.sum(part, axis=-1, keepdims=True) for part in parts) * (1.0 / 768)
    parts = [part - mean for part in parts]
    square = sum(jnp.sum(part * part, axis=-1, keepdims=True) for part in parts)
    merge_scale = lax.rsqrt(square * (1.0 / 768) + 1e-5)
    parts = [(part * merge_scale).astype(bf16) for part in parts]
    base = sum(mm(parts[k], reduce_ref[k * 192 : (k + 1) * 192]) for k in range(4))
    base = base.astype(bf16).astype(f32)
    normed, scale1 = norm(base)
    normed = normed.astype(bf16)
    queries = mm(normed, qkv_ref[:, 0:384]).astype(bf16)
    keys = mm(normed, qkv_ref[:, 384:768]).astype(bf16)
    values = mm(normed, qkv_ref[:, 768:1152]).astype(bf16)
    mixture = attend(queries, keys, values, bias_ref, 0, mask_ref[...], probs_ref, 0).astype(bf16)
    first = base + mm(mixture, proj_ref[...])
    renormed, scale2 = norm(first)
    renormed = renormed.astype(bf16)
    active, slope = gelu_pair(mm(renormed, up_ref[...]))
    result = first + mm(active.astype(bf16), down_ref[...])
    for index, out in enumerate((c0, c1, c2, c3)):
        out[...] = pack([result[index * QUAD : (index + 1) * QUAD]], 48)

    grad = jnp.concatenate(
        [
            coarse_of(diag_ref, 48),
            coarse_of(lat_ref, 112),
            coarse_of(lon_ref, 112),
            gloc_ref[...].astype(f32)[:QUAD],
        ],
        axis=0,
    )
    inner = mm_nt(grad.astype(bf16), down_ref[...]) * slope
    grad = grad + norm_back(mm_nt(inner.astype(bf16), up_ref[...]), renormed.astype(f32), scale2)
    mix_grad = mm_nt(grad.astype(bf16), proj_ref[...]).astype(bf16)
    dq, dk, dv = attend_back(queries, keys, values, mix_grad, probs_ref, 0, score_ref, False)
    normed_grad = (
        mm_nt(dq.astype(bf16), qkv_ref[:, 0:384])
        + mm_nt(dk.astype(bf16), qkv_ref[:, 384:768])
        + mm_nt(dv.astype(bf16), qkv_ref[:, 768:1152])
    )
    grad = grad + norm_back(normed_grad, normed.astype(f32), scale1)
    grad = grad.astype(bf16)
    grads = [mm_nt(grad, reduce_ref[k * 192 : (k + 1) * 192]) for k in range(4)]
    mean = sum(jnp.sum(g, axis=-1, keepdims=True) for g in grads) * (1.0 / 768)
    along = sum(
        jnp.sum(g * p.astype(f32), axis=-1, keepdims=True) for g, p in zip(grads, parts)
    ) * (1.0 / 768)
    for k in range(4):
        part = (grads[k] - mean - parts[k].astype(f32) * along) * merge_scale
        parts_ref[pl.ds(k * WIN, WIN), :] = part.astype(bf16)
    everything = parts_ref[...]
    moved = mm(one_hot(split_ref[...], 576), everything)
    dlon_ref[...] = dense([moved[0:112]], 112)
    dloc_ref[...] = moved[112:448].astype(bf16)
    dlat_ref[...] = dense([moved[448:560]], 112)
    ddiag_ref[...] = dense([moved[560:608]], 48)


def band_back(parts, source, back_ref, weights, outs, score_ref):
    proj_ref, up_ref, down_ref = weights
    grad_ref, dq_ref, dk_ref, dv_ref = outs
    everything = source[...]
    for across, (w, slot, saved) in enumerate(parts):
        q_ref, k_ref, v_ref, probs_ref, n2_ref, r2_ref, slope_ref = saved
        rows = pl.ds(slot * WIN, WIN)
        here = pl.ds(across * WIN, WIN)
        grad = mm(one_hot(back_ref[pl.ds(w * WIN, WIN), :], everything.shape[0]), everything)
        inner = mm(grad.astype(bf16), down_ref[...]) * slope_ref[rows, :].astype(f32)
        grad = grad + norm_back(
            mm_nt(inner.astype(bf16), up_ref[...]), n2_ref[rows, :].astype(f32), r2_ref[rows, :]
        )
        grad_ref[here, :] = grad
        mix_grad = mm_nt(grad.astype(bf16), proj_ref[...]).astype(bf16)
        dq, dk, dv = attend_back(
            q_ref[rows, :], k_ref[rows, :], v_ref[rows, :], mix_grad,
            probs_ref, slot * 6 * WIN, score_ref, across == 1,
        )
        dq_ref[here, :] = dq.astype(bf16)
        dk_ref[here, :] = dk.astype(bf16)
        dv_ref[here, :] = dv.astype(bf16)


def first_band_kernel(dlon_ref, dloc_ref, back_ref, *refs):
    *refs, source = refs
    source[0:112] = tokens_of(dlon_ref, 112)
    source[112:448] = dloc_ref[...]
    parts = ((0, 0, refs[:7]), (1, 0, refs[7:14]))
    band_back(parts, source, back_ref, refs[14:17], refs[17:21], refs[21])


def second_band_kernel(
    dlon_ref, dloc_ref, dlat_ref, ddiag_ref, back_ref, first_ref, *refs
):
    *refs, source, score_ref, rows_ref = refs
    source[0:112] = tokens_of(dlon_ref, 112)
    source[112:448] = dloc_ref[...]
    source[448:560] = tokens_of(dlat_ref, 112)
    source[560:608] = tokens_of(ddiag_ref, 48)
    half = 6 * WIN
    score_ref[pl.ds(0, half), :] = first_ref[...]
    parts = ((2, 1, refs[:7]), (3, 2, refs[:7]))
    band_back(
        parts, source, back_ref, refs[7:10], refs[10:14], score_ref.at[pl.ds(half, half)]
    )
    refs[14][...] = table_grad(score_ref, rows_ref)


def qkv_back_kernel(*refs):
    bands, refs = (refs[:4], refs[4:8]), refs[8:]
    norms = (refs[0:2], refs[2:4])
    qkv_ref, clon_ref, clat_ref, cdiag_ref = refs[4:8]
    res_ref, slon_ref, slat_ref, sdiag_ref = refs[8:]
    w_qkv = qkv_ref[...]
    windows = []
    for w in range(4):
        grad_ref, dq_ref, dk_ref, dv_ref = bands[w // 2]
        rows = pl.ds(w * WIN, WIN)
        here = pl.ds(w % 2 * WIN, WIN)
        normed_grad = (
            mm_nt(dq_ref[here, :], w_qkv[:, 0:192])
            + mm_nt(dk_ref[here, :], w_qkv[:, 192:384])
            + mm_nt(dv_ref[here, :], w_qkv[:, 384:576])
        )
        n1_ref, r1_ref = norms[min(w, 1)]
        slot = pl.ds(max(w - 1, 0) * WIN, WIN)
        result = grad_ref[here, :] + norm_back(
            normed_grad, n1_ref[slot, :].astype(f32), r1_ref[slot, :]
        )
        res_ref[rows, :] = result.astype(bf16)
        windows.append(result)
    clon, clat, cdiag = [
        ref[...].astype(f32)[:QUAD] for ref in (clon_ref, clat_ref, cdiag_ref)
    ]
    slon_ref[...] = dense([quadrant(windows, q, 0) for q in range(1, 4)], 112, clon)
    slat_ref[...] = dense([quadrant(windows, 0, q) for q in range(1, 4)], 112, clat)
    sdiag_ref[...] = dense([quadrant(windows, 0, 0)], 48, cdiag)


def last_kernel(
    res_ref, lon_ref, lat_ref, diag_ref, leave_ref, cloc_ref, result_ref,
    tokens_ref, coarse_ref, source, coarse_source,
):
    source[0:576] = res_ref[...]
    source[576:688] = tokens_of(lon_ref, 112)
    source[688:800] = tokens_of(lat_ref, 112)
    source[800:848] = tokens_of(diag_ref, 48)
    everything = source[...]
    for w in range(4):
        rows = pl.ds(w * WIN, WIN)
        tokens_ref[rows, :] = mm(one_hot(leave_ref[rows, :], 848), everything).astype(bf16)
    coarse_source[0:48] = cloc_ref[...]
    coarse_source[48:96] = pack([coarse_of(lon_ref, 112)], 48)
    coarse_source[96:144] = pack([coarse_of(lat_ref, 112)], 48)
    coarse_source[144:192] = pack([coarse_of(diag_ref, 48)], 48)
    moved = mm(one_hot(result_ref[...], 192), coarse_source[...])
    for z in range(2):
        for row in range(6):
            start = z * 72 + row * 12
            coarse_ref[z, row] = moved[start : start + 12].astype(bf16)


def run(kernel, outs, scratch, weight, inputs):
    shapes = [jax.ShapeDtypeStruct(shape, kind) for shape, kind in outs]
    size = sum(math.prod(s.shape) * s.dtype.itemsize for s in shapes)
    size += sum(x.size * x.dtype.itemsize for x in inputs)
    return pl.pallas_call(
        kernel,
        out_shape=shapes,
        scratch_shapes=[pltpu.VMEM(shape, kind) for shape, kind in scratch],
        compiler_params=pltpu.CompilerParams(vmem_limit_bytes=VMEM),
        cost_estimate=pl.CostEstimate(
            flops=weight * 1_000_000_000, bytes_accessed=size, transcendentals=0
        ),
    )(*inputs)


def move(value, lon_steps, lat_steps):
    lon, lat = lax.axis_size("lon"), lax.axis_size("lat")
    if lat_steps == 0:
        pairs = [(s, (s + lon_steps) % lon) for s in range(lon)]
        return lax.ppermute(value, "lon", pairs)
    if lon_steps == 0:
        pairs = [(s, (s + lat_steps) % lat) for s in range(lat)]
        return lax.ppermute(value, "lat", pairs)
    pairs = [
        (b * lat + a, (b + lon_steps) % lon * lat + (a + lat_steps) % lat)
        for b in range(lon)
        for a in range(lat)
    ]
    return lax.ppermute(value, ("lon", "lat"), pairs)


def send(pieces, steps):
    on_lon, on_lat, on_both = pieces
    return move(on_lon, steps, 0), move(on_lat, 0, steps), move(on_both, steps, steps)


def swap(value, step):
    count = lax.axis_size("lon")
    return lax.ppermute(value, "lon", [(s, s ^ step) for s in range(count)])


def add(mine, other):
    return (mine.astype(f32) + other.astype(f32)).astype(bf16)


def lon_steps():
    return [1 << bit for bit in range(lax.axis_size("lon").bit_length() - 1)]


def body(
    tokens, mask_ids, fine_qkv, fine_proj, fine_up, fine_down, fine_bias, reduce_weight,
    coarse_qkv, coarse_proj, coarse_up, coarse_down, coarse_bias, out_grad,
):
    lat_index = lax.axis_index("lat")
    fine_down = fine_down.T
    flat = tokens.reshape(576, 192)
    column = lambda index: jnp.asarray(index).reshape(-1, 1)
    tok = ((576, 192), bf16)
    edges = [((176, 128), bf16), ((176, 128), bf16), ((80, 128), bf16)]
    wide_edges = [((288, 128), bf16), ((288, 128), bf16), ((192, 128), bf16)]
    quad = ((48, 384), bf16)
    scores = ((12 * WIN, WIN), f32)
    table_rows = ((12, 192, WIN), bf16)
    held = ((12, 2, 12, 16, WIN), bf16)

    first = send(run(edge_kernel, edges, [], 1, (flat,)), 1)
    (fine_table,) = run(
        bias_kernel, [scores], [held], 2,
        (fine_bias.transpose(1, 0, 2),),
    )

    row = lax.broadcasted_iota(jnp.int32, mask_ids.shape, 1) + lat_index * mask_ids.shape[1]
    labels = mask_ids * 2 + jnp.where(row < 3, 1, 0)
    labels = labels.reshape(2, 2, 2, 3, 2, 2, 6)
    labels = labels.transpose(1, 4, 2, 5, 0, 3, 6).reshape(4, WIN)
    fine_mask = jnp.where(labels[:, :, None] == labels[:, None, :], 0.0, -1e30).astype(f32)
    low_half = jnp.arange(WIN) < WIN // 2
    coarse_mask = jnp.where(
        (low_half[:, None] == low_half[None, :]) | (lat_index != 0), 0.0, -1e30
    ).astype(f32)

    def saved_shapes(windows):
        rows = windows * WIN
        part = ((rows, 192), bf16)
        scale = ((rows, 1), f32)
        probs = ((6 * rows, WIN), bf16)
        return [part] * 3 + [probs, part, scale, part, scale, ((rows, 768), bf16)]

    inputs = (
        flat, *first, column(ARRIVE), fine_table, fine_mask,
        fine_qkv, fine_proj, fine_up, fine_down,
    )
    gathered = [((848, 192), bf16)]
    outer = run(
        fine_edge_kernel,
        wide_edges + [quad, ((3 * WIN, 192), bf16)] + saved_shapes(3),
        gathered, 6, (out_grad.transpose(1, 2, 0, 3), *inputs),
    )
    arrived = send(outer[:3], 1)
    flat_after, _ = lax.optimization_barrier((flat, outer[4]))
    inner = run(
        fine_inner_kernel,
        [((WIN, 192), bf16)] + saved_shapes(1),
        gathered, 2, (flat_after, *inputs[1:]),
    )
    late_table, _ = lax.optimization_barrier((coarse_bias.transpose(1, 0, 2), outer[4]))
    (coarse_table,) = run(
        bias_kernel, [scores], [held], 2, (late_table,)
    )
    coarse = run(
        coarse_kernel,
        [quad] * 4 + edges + [((336, 192), bf16), scores],
        [((848, 192), bf16), ((12 * WIN, WIN), bf16), ((576, 192), bf16)],
        9,
        (
            inner[0], outer[4], *arrived, column(MERGE), column(SPLIT), coarse_table, coarse_mask, outer[3],
            reduce_weight, coarse_qkv, coarse_proj, coarse_up, coarse_down,
        ),
    )
    c00, c01, c10, c11 = coarse[:4]
    arrived = send(coarse[4:7], -1)
    dlon, dlat, ddiag = arrived
    dlat, scored = lax.optimization_barrier((dlat, coarse[8]))
    (coarse_grad,) = run(
        coarse_table_kernel, [((24, 6 * ENTRIES), bf16)], [table_rows], 2,
        (scored,),
    )
    steps = lon_steps()
    other = swap(coarse_grad, steps[0])
    half_tok = ((288, 192), bf16)
    half_outs = [((288, 192), f32)] + [half_tok] * 3
    q, k, v, probs, n1, r1, n2, r2, slope = outer[5:]
    outer_saved = (q, k, v, probs, n2, r2, slope)
    q, k, v, probs, n1_inner, r1_inner, n2, r2, slope = inner[1:]
    inner_saved = (q, k, v, probs, n2, r2, slope)
    weights = (fine_proj, fine_up, fine_down)
    *first_half, first_scores = run(
        first_band_kernel,
        half_outs + [((6 * WIN, WIN), f32)],
        [((448, 192), bf16)],
        4,
        (dlon, coarse[7], column(BACK), *inner_saved, *outer_saved, *weights),
    )
    first_scores, other = lax.optimization_barrier((first_scores, other))
    coarse_grad = add(coarse_grad, other)
    other = swap(coarse_grad, steps[-1])
    *second_half, fine_grad = run(
        second_band_kernel,
        half_outs + [((24, 6 * ENTRIES), bf16)],
        [((608, 192), bf16), scores, table_rows],
        5,
        (
            dlon, coarse[7], dlat, ddiag, column(BACK), first_scores,
            *outer_saved, *weights,
        ),
    )
    second_half[0], other = lax.optimization_barrier((second_half[0], other))
    coarse_grad = add(coarse_grad, other)
    for step in steps[1:-1]:
        coarse_sums = (coarse_grad, swap(coarse_grad, step))
        coarse_grad = add(*coarse_sums)
    other = swap(fine_grad, steps[-1])
    fine_back = list(run(
        qkv_back_kernel, [tok] + wide_edges, [], 2,
        (*first_half, *second_half, n1_inner, r1_inner, n1, r1, fine_qkv, c10, c01, c00),
    ))
    alon, alat, adiag = send(fine_back[1:4], -1)
    alat, adiag, other = lax.optimization_barrier((alat, adiag, other))
    fine_grad = add(fine_grad, other)
    for step in reversed(steps[:-1]):
        fine_sums = (fine_grad, swap(fine_grad, step))
        fine_grad = add(*fine_sums)
    d_tokens, coarse_result = run(
        last_kernel,
        [tok, ((2, 6, 12, 384), bf16)],
        [((848, 192), bf16), ((192, 384), bf16)],
        1,
        (fine_back[0], alon, alat, adiag, column(LEAVE), c11, column(RESULT)),
    )
    fine_out, coarse_out = run(
        table_sum_kernel,
        [((HEADS_F, 2, 12 * ENTRIES), f32), ((HEADS_C, 1, 12 * ENTRIES), f32)],
        [], 1, (*fine_sums, *coarse_sums),
    )
    return (
        coarse_result,
        d_tokens.reshape(tokens.shape),
        fine_out.transpose(1, 0, 2),
        coarse_out.transpose(1, 0, 2),
    )


def solution(mesh):
    grid = P(None, "lat", "lon", None)
    bands = P("lat", None, None)
    in_specs = (
        grid, P(None, "lat", "lon"), P(), P(), P(), P(), bands,
        P(), P(), P(), P(), P(), bands, grid,
    )
    out_specs = (grid, grid, bands, bands)
    return jax.shard_map(body, mesh=mesh, in_specs=in_specs, out_specs=out_specs, check_vma=False)
```

```python
import math

import jax
import jax.numpy as jnp
import numpy as np
from jax import lax
from jax.experimental import pallas as pl
from jax.experimental.pallas import tpu as pltpu
from jax.sharding import PartitionSpec as P

HEADS_F = 6
HEADS_C = 12
HEAD = 32
WIN = 144
QUAD = 36
SPAN = 23
ENTRIES = 276
LOG2E = math.log2(math.e)
VMEM = 20 * 1024 * 1024
f32 = jnp.float32
bf16 = jnp.bfloat16


def spot(z, i, j):
    quadrant = (i % 6) // 3 * 2 + (j % 12) // 6
    return quadrant * QUAD + z * 18 + i % 3 * 6 + j % 6


def fine_spot(z, i, j):
    return (i // 6 * 2 + j // 12) * WIN + spot(z, i, j)


def in_quad(z, i, j):
    return z * 18 + i % 3 * 6 + j % 6


def index_maps():
    arrive = np.zeros(576, np.int32)
    merge = np.zeros(576, np.int32)
    split = np.full(608, -1, np.int32)
    back = np.zeros(576, np.int32)
    leave = np.zeros(576, np.int32)
    for z in range(2):
        for i in range(12):
            for j in range(24):
                here = fine_spot(z, i, j)
                if i >= 3 and j >= 6:
                    arrive[here] = z * 288 + (i - 3) * 24 + j - 6
                    came = fine_spot(z, i - 3, j - 6)
                elif i >= 3:
                    came = 576 + (i - 3) // 3 * QUAD + in_quad(z, i, j)
                elif j >= 6:
                    came = 688 + (j - 6) // 6 * QUAD + in_quad(z, i, j)
                else:
                    came = 800 + in_quad(z, i, j)
                if came >= 576:
                    arrive[here] = came
                part = (i % 2 + j % 2 * 2) * WIN + spot(z, i // 2, j // 2)
                merge[part] = came
                if i >= 3 and j >= 6:
                    slot = 112 + z * 162 + (i - 3) * 18 + j - 6
                    back[fine_spot(z, i - 3, j - 6)] = slot
                elif i >= 3:
                    slot = z * 54 + (i - 3) * 6 + j
                    back[fine_spot(z, i - 3, j + 18)] = slot
                elif j >= 6:
                    slot = 448 + z * 54 + i * 18 + j - 6
                    back[fine_spot(z, i + 9, j - 6)] = slot
                else:
                    slot = 560 + z * 18 + i * 6 + j
                    back[fine_spot(z, i + 9, j + 18)] = slot
                split[slot] = part
                natural = z * 288 + i * 24 + j
                if i < 9 and j < 18:
                    leave[natural] = fine_spot(z, i + 3, j + 6)
                elif i < 9:
                    leave[natural] = 576 + i // 3 * QUAD + in_quad(z, i, j)
                elif j < 18:
                    leave[natural] = 688 + j // 6 * QUAD + in_quad(z, i, j)
                else:
                    leave[natural] = 800 + in_quad(z, i, j)
    result = np.zeros(WIN, np.int32)
    for z in range(2):
        for i in range(6):
            for j in range(12):
                result[z * 72 + i * 12 + j] = (i // 3 * 2 + j // 6) * 48 + in_quad(z, i, j)
    return arrive, merge, split, back, leave, result


ARRIVE, MERGE, SPLIT, BACK, LEAVE, RESULT = index_maps()


def places(shape, axis):
    t = lax.broadcasted_iota(jnp.int32, shape, axis)
    quad = (t * 57) >> 11
    t = t - quad * QUAD
    level = (t * 57) >> 10
    t = t - level * 18
    row = (t * 43) >> 8
    return level * 6 + (quad >> 1) * 3 + row, t - row * 6 + (quad & 1) * 6


def entry_base(shape, axis):
    row, column = places(shape, axis)
    return row * SPAN + 11 - column


def row_slot(shape, axis):
    row, column = places(shape, axis)
    return column * 16 + row


def one_hot(column, width):
    spots = lax.broadcasted_iota(jnp.int32, (column.shape[0], width), 1)
    return jnp.where(spots == column, 1.0, 0.0).astype(bf16)


def mm(left, right):
    return jnp.dot(left, right, preferred_element_type=f32)


def mm_nt(left, right):
    return lax.dot_general(left, right, (((1,), (1,)), ((), ())), preferred_element_type=f32)


def mm_tn(left, right):
    return lax.dot_general(left, right, (((0,), (0,)), ((), ())), preferred_element_type=f32)


def norm(values):
    centred = values - jnp.mean(values, axis=-1, keepdims=True)
    scale = lax.rsqrt(jnp.mean(centred * centred, axis=-1, keepdims=True) + 1e-5)
    return centred * scale, scale


def norm_back(grad, normed, scale):
    along = jnp.mean(grad * normed, axis=-1, keepdims=True)
    return (grad - jnp.mean(grad, axis=-1, keepdims=True) - normed * along) * scale


def gelu_pair(x):
    u = jnp.abs(x) * math.sqrt(0.5)
    t = 1.0 / (1.0 + 0.3275911 * u)
    e = jnp.exp(-u * u)
    poly = 1.421413741 + t * (-1.453152027 + t * 1.061405429)
    tail = 0.5 * (t * (0.254829592 + t * (-0.284496736 + t * poly))) * e
    below = jnp.where(x >= 0, 1.0 - tail, tail)
    return x * below, below + x * (e * (1.0 / math.sqrt(2 * math.pi)))


def groups(channels):
    return [(start, min(start + 128, channels)) for start in range(0, channels, 128)]


def head_lanes(rows, width):
    return lax.broadcasted_iota(jnp.int32, (rows, width), 1) // HEAD


def stack_heads(part):
    lanes = head_lanes(part.shape[0], part.shape[1])
    count = part.shape[1] // HEAD
    zero = jnp.zeros_like(part)
    return jnp.concatenate([jnp.where(lanes == h, part, zero) for h in range(count)], axis=0)


def pick_heads(stacked):
    width = stacked.shape[1]
    lanes = head_lanes(WIN, width)
    total = stacked[:WIN]
    for h in range(1, width // HEAD):
        total = jnp.where(lanes == h, stacked[h * WIN : (h + 1) * WIN], total)
    return total


def attend(queries, keys, values, bias_ref, bias_row, mask, probs_ref, probs_row):
    mixed = []
    for start, stop in groups(queries.shape[1]):
        count = (stop - start) // HEAD
        scores = mm_nt(stack_heads(queries[:, start:stop]), keys[:, start:stop])
        row = start // HEAD * WIN
        for h in range(count):
            here = row + h * WIN
            logits = (
                scores[h * WIN : (h + 1) * WIN] * (HEAD**-0.5 * LOG2E)
                + bias_ref[pl.ds(bias_row + here, WIN), :]
                + mask
            )
            raised = jnp.exp2(logits - jnp.max(logits, axis=-1, keepdims=True))
            probs = raised * (1.0 / jnp.sum(raised, axis=-1, keepdims=True))
            probs_ref[pl.ds(probs_row + here, WIN), :] = probs.astype(bf16)
        stacked = mm(probs_ref[pl.ds(probs_row + row, count * WIN), :], values[:, start:stop])
        mixed.append(pick_heads(stacked))
    return jnp.concatenate(mixed, axis=1)


def attend_back(queries, keys, values, mix_grad, probs_ref, probs_row, score_ref, add):
    query_grad, key_grad, value_grad = [], [], []
    for start, stop in groups(queries.shape[1]):
        count = (stop - start) // HEAD
        row = start // HEAD * WIN
        probs_all = probs_ref[pl.ds(probs_row + row, count * WIN), :]
        grads = stack_heads(mix_grad[:, start:stop])
        value_grad.append(mm_tn(probs_all, grads))
        probs_grad = mm_nt(grads, values[:, start:stop])
        pieces = []
        for h in range(count):
            probs = probs_all[h * WIN : (h + 1) * WIN].astype(f32)
            grad = probs_grad[h * WIN : (h + 1) * WIN]
            weighted = grad * probs
            score_grad = weighted - probs * jnp.sum(weighted, axis=-1, keepdims=True)
            place = pl.ds(row + h * WIN, WIN)
            if add:
                score_ref[place, :] += score_grad
            else:
                score_ref[place, :] = score_grad
            pieces.append(score_grad.astype(bf16))
        score_all = jnp.concatenate(pieces, axis=0)
        query_grad.append(pick_heads(mm(score_all, keys[:, start:stop])))
        key_grad.append(mm_tn(score_all, stack_heads(queries[:, start:stop])))
    scale = HEAD**-0.5
    return (
        jnp.concatenate(query_grad, axis=1) * scale,
        jnp.concatenate(key_grad, axis=1) * scale,
        jnp.concatenate(value_grad, axis=1),
    )


def swap_rows():
    row = lax.broadcasted_iota(jnp.int32, (192, 192), 0)
    return jnp.where(
        lax.broadcasted_iota(jnp.int32, (192, 192), 1) == row % 16 * 16 + row // 16, 1.0, 0.0
    ).astype(bf16)


def table_grad(score_ref, rows_ref):
    regroup = jnp.where(
        lax.broadcasted_iota(jnp.int32, (192, WIN), 0) == row_slot((1, WIN), 1), 1.0, 0.0
    ).astype(bf16)
    for h in range(12):
        moved = mm(regroup, score_ref[pl.ds(h * WIN, WIN), :].astype(bf16)).astype(bf16)
        rows_ref[:, pl.ds(h * 16, 16), :] = moved.reshape(12, 16, WIN)
    total = jnp.zeros((192, ENTRIES), f32)
    base = entry_base((WIN, 1), 0)
    for column in range(12):
        total += mm(rows_ref[column], one_hot(base + column, ENTRIES))
    swapped = mm(swap_rows(), total.astype(bf16))
    halves = [
        jnp.concatenate([swapped[a * 16 : a * 16 + 12] for a in range(start, start + 6)], axis=1)
        for start in (0, 6)
    ]
    return jnp.concatenate(halves, axis=0).astype(bf16)


def pack(pieces, rows):
    count = sum(piece.shape[0] for piece in pieces)
    if rows > count:
        pieces = pieces + [jnp.zeros((rows - count, pieces[0].shape[1]), f32)]
    return jnp.concatenate(pieces, axis=0).astype(bf16)


def dense(pieces, rows, coarse=None):
    count = sum(piece.shape[0] for piece in pieces)
    if rows > count:
        pieces = pieces + [jnp.zeros((rows - count, 192), f32)]
    tokens = jnp.concatenate(pieces, axis=0)
    half = rows // 2
    side = jnp.concatenate([tokens[0:half, 128:192], tokens[half:rows, 128:192]], axis=1)
    filler = jnp.zeros((4, 128), f32)
    out = [tokens[:, 0:128], side]
    if coarse is None:
        out += [filler, filler]
    else:
        for start in range(0, 384, 128):
            out += [coarse[:, start : start + 128], filler]
    return jnp.concatenate(out, axis=0).astype(bf16)


def tokens_of(ref, rows):
    values = ref[...].astype(f32)
    side = values[rows : rows + rows // 2]
    side = jnp.concatenate([side[:, 0:64], side[:, 64:128]], axis=0)
    return jnp.concatenate([values[0:rows], side], axis=1).astype(bf16)


def coarse_of(ref, rows):
    values = ref[...].astype(f32)
    starts = [rows + rows // 2 + 40 * part for part in range(3)]
    return jnp.concatenate([values[start : start + QUAD] for start in starts], axis=1)


def quadrant(windows, qi, qj):
    part = (qi % 2 * 2 + qj % 2) * QUAD
    return windows[qi // 2 * 2 + qj // 2][part : part + QUAD]


def edge_kernel(tokens_ref, slon_ref, slat_ref, sdiag_ref):
    tokens = tokens_ref[...].astype(f32)

    def token_quadrant(row, start):
        pieces = []
        for z in range(2):
            for i in range(row, row + 3):
                place = (z * 12 + i) * 24 + start
                pieces.append(tokens[place : place + 6])
        return jnp.concatenate(pieces, axis=0)

    slon_ref[...] = dense([token_quadrant(q * 3, 18) for q in range(3)], 112)
    slat_ref[...] = dense([token_quadrant(9, q * 6) for q in range(3)], 112)
    sdiag_ref[...] = dense([token_quadrant(9, 18)], 48)


def expand(table_ref, out_ref, held):
    table = jnp.concatenate([table_ref[:, b, :] for b in range(table_ref.shape[1])], axis=0)
    filler = jnp.zeros((4, ENTRIES), f32)
    pieces = []
    for a in range(12):
        pieces += [table[:, a * ENTRIES : (a + 1) * ENTRIES], filler]
    table = jnp.concatenate(pieces, axis=0)
    high = table.astype(bf16)
    low = (table - high.astype(f32)).astype(bf16)
    swap = swap_rows()
    table = jnp.concatenate(
        [mm(swap, high).astype(bf16), mm(swap, low).astype(bf16)], axis=0
    )
    entry = lax.broadcasted_iota(jnp.int32, (ENTRIES, WIN), 0)
    base = entry_base((1, WIN), 1)
    for column in range(12):
        picker = jnp.where(entry == base + column, 1.0, 0.0).astype(bf16)
        picked = mm(table, picker).astype(bf16)
        held[:, 0, column] = picked[0:192].reshape(12, 16, WIN)
        held[:, 1, column] = picked[192:384].reshape(12, 16, WIN)
    spots = lax.broadcasted_iota(jnp.int32, (WIN, 384), 1)
    spots = jnp.where(spots >= 192, spots - 192, spots)
    twice = jnp.where(spots == row_slot((WIN, 1), 0), 1.0, 0.0).astype(bf16)
    for h in range(12):
        out_ref[pl.ds(h * WIN, WIN), :] = mm(twice, held[h].reshape(384, WIN)) * LOG2E


def bias_kernel(table_ref, out_ref, held):
    expand(table_ref, out_ref, held)


def coarse_table_kernel(score_ref, table_ref, rows_ref):
    table_ref[...] = table_grad(score_ref, rows_ref)


def table_sum_kernel(fine_kept, fine_other, coarse_kept, coarse_other, fine_ref, coarse_ref):
    for kept, other, out_ref in (
        (fine_kept, fine_other, fine_ref),
        (coarse_kept, coarse_other, coarse_ref),
    ):
        total = kept[...].astype(f32) + other[...].astype(f32)
        total = jnp.concatenate([total[0:12], total[12:24]], axis=1)
        heads = out_ref.shape[0]
        for b in range(out_ref.shape[1]):
            out_ref[:, b, :] = total[b * heads : (b + 1) * heads]


def fine_windows(numbers, refs):
    tokens_ref, lon_ref, lat_ref, diag_ref, arrive_ref, bias_ref, mask_ref = refs[:7]
    qkv_ref, proj_ref, up_ref, down_ref, res_ref = refs[7:12]
    q_ref, k_ref, v_ref, probs_ref, n1_ref, r1_ref, n2_ref, r2_ref, slope_ref = refs[12:21]
    source = refs[21]
    source[0:576] = tokens_ref[...]
    source[576:688] = tokens_of(lon_ref, 112)
    source[688:800] = tokens_of(lat_ref, 112)
    source[800:848] = tokens_of(diag_ref, 48)
    everything = source[...]
    w_qkv = qkv_ref[...]
    bases = []
    for slot, w in enumerate(numbers):
        rows = pl.ds(slot * WIN, WIN)
        base = mm(one_hot(arrive_ref[pl.ds(w * WIN, WIN), :], 848), everything)
        normed, scale = norm(base)
        normed = normed.astype(bf16)
        n1_ref[rows, :] = normed
        r1_ref[rows, :] = scale
        q_ref[rows, :] = mm(normed, w_qkv[:, 0:192]).astype(bf16)
        k_ref[rows, :] = mm(normed, w_qkv[:, 192:384]).astype(bf16)
        v_ref[rows, :] = mm(normed, w_qkv[:, 384:576]).astype(bf16)
        bases.append(base)
    windows = {}
    for slot, w in enumerate(numbers):
        rows = pl.ds(slot * WIN, WIN)
        mixture = attend(
            q_ref[rows, :], k_ref[rows, :], v_ref[rows, :],
            bias_ref, w // 2 * 6 * WIN, mask_ref[w], probs_ref, slot * 6 * WIN,
        ).astype(bf16)
        first = bases[slot] + mm(mixture, proj_ref[...])
        renormed, scale = norm(first)
        renormed = renormed.astype(bf16)
        n2_ref[rows, :] = renormed
        r2_ref[rows, :] = scale
        active, slope = gelu_pair(mm(renormed, up_ref[...]))
        slope_ref[rows, :] = slope.astype(bf16)
        result = first + mm_nt(active.astype(bf16), down_ref[...])
        res_ref[rows, :] = result.astype(bf16)
        windows[w] = result
    return windows


def fine_edge_kernel(grad_ref, *refs):
    slon_ref, slat_ref, sdiag_ref, gloc_ref = refs[11:15]
    windows = fine_windows((1, 2, 3), refs[:11] + refs[15:])
    grads = grad_ref[...].astype(f32)

    def grad_quadrant(hi, hj):
        pieces = [
            grads[hi * 3 + row, hj * 6 : hj * 6 + 6, z] for z in range(2) for row in range(3)
        ]
        return jnp.concatenate(pieces, axis=0)

    slon_ref[...] = dense([quadrant(windows, q, 3) for q in range(3)], 112, grad_quadrant(0, 1))
    slat_ref[...] = dense([quadrant(windows, 3, q) for q in range(3)], 112, grad_quadrant(1, 0))
    sdiag_ref[...] = dense([quadrant(windows, 3, 3)], 48, grad_quadrant(1, 1))
    gloc_ref[...] = pack([grad_quadrant(0, 0)], 48)


def fine_inner_kernel(*refs):
    fine_windows((0,), refs)


def coarse_kernel(
    inner_ref, res_ref, lon_ref, lat_ref, diag_ref, merge_ref, split_ref, bias_ref, mask_ref,
    gloc_ref,
    reduce_ref, qkv_ref, proj_ref, up_ref, down_ref,
    c0, c1, c2, c3, dlon_ref, dlat_ref, ddiag_ref, dloc_ref, score_ref,
    source, probs_ref, parts_ref,
):
    source[0:144] = inner_ref[...]
    source[144:576] = res_ref[...]
    source[576:688] = tokens_of(lon_ref, 112)
    source[688:800] = tokens_of(lat_ref, 112)
    source[800:848] = tokens_of(diag_ref, 48)
    everything = source[...]
    parts = [mm(one_hot(merge_ref[pl.ds(k * WIN, WIN), :], 848), everything) for k in range(4)]
    mean = sum(jnp.sum(part, axis=-1, keepdims=True) for part in parts) * (1.0 / 768)
    parts = [part - mean for part in parts]
    square = sum(jnp.sum(part * part, axis=-1, keepdims=True) for part in parts)
    merge_scale = lax.rsqrt(square * (1.0 / 768) + 1e-5)
    parts = [(part * merge_scale).astype(bf16) for part in parts]
    base = sum(mm(parts[k], reduce_ref[k * 192 : (k + 1) * 192]) for k in range(4))
    base = base.astype(bf16).astype(f32)
    normed, scale1 = norm(base)
    normed = normed.astype(bf16)
    queries = mm(normed, qkv_ref[:, 0:384]).astype(bf16)
    keys = mm(normed, qkv_ref[:, 384:768]).astype(bf16)
    values = mm(normed, qkv_ref[:, 768:1152]).astype(bf16)
    mixture = attend(queries, keys, values, bias_ref, 0, mask_ref[...], probs_ref, 0).astype(bf16)
    first = base + mm(mixture, proj_ref[...])
    renormed, scale2 = norm(first)
    renormed = renormed.astype(bf16)
    active, slope = gelu_pair(mm(renormed, up_ref[...]))
    result = first + mm(active.astype(bf16), down_ref[...])
    for index, out in enumerate((c0, c1, c2, c3)):
        out[...] = pack([result[index * QUAD : (index + 1) * QUAD]], 48)

    grad = jnp.concatenate(
        [
            coarse_of(diag_ref, 48),
            coarse_of(lat_ref, 112),
            coarse_of(lon_ref, 112),
            gloc_ref[...].astype(f32)[:QUAD],
        ],
        axis=0,
    )
    inner = mm_nt(grad.astype(bf16), down_ref[...]) * slope
    grad = grad + norm_back(mm_nt(inner.astype(bf16), up_ref[...]), renormed.astype(f32), scale2)
    mix_grad = mm_nt(grad.astype(bf16), proj_ref[...]).astype(bf16)
    dq, dk, dv = attend_back(queries, keys, values, mix_grad, probs_ref, 0, score_ref, False)
    normed_grad = (
        mm_nt(dq.astype(bf16), qkv_ref[:, 0:384])
        + mm_nt(dk.astype(bf16), qkv_ref[:, 384:768])
        + mm_nt(dv.astype(bf16), qkv_ref[:, 768:1152])
    )
    grad = grad + norm_back(normed_grad, normed.astype(f32), scale1)
    grad = grad.astype(bf16)
    grads = [mm_nt(grad, reduce_ref[k * 192 : (k + 1) * 192]) for k in range(4)]
    mean = sum(jnp.sum(g, axis=-1, keepdims=True) for g in grads) * (1.0 / 768)
    along = sum(
        jnp.sum(g * p.astype(f32), axis=-1, keepdims=True) for g, p in zip(grads, parts)
    ) * (1.0 / 768)
    for k in range(4):
        part = (grads[k] - mean - parts[k].astype(f32) * along) * merge_scale
        parts_ref[pl.ds(k * WIN, WIN), :] = part.astype(bf16)
    everything = parts_ref[...]
    moved = mm(one_hot(split_ref[...], 576), everything)
    dlon_ref[...] = dense([moved[0:112]], 112)
    dloc_ref[...] = moved[112:448].astype(bf16)
    dlat_ref[...] = dense([moved[448:560]], 112)
    ddiag_ref[...] = dense([moved[560:608]], 48)


def band_back(parts, source, back_ref, weights, outs, score_ref):
    proj_ref, up_ref, down_ref = weights
    grad_ref, dq_ref, dk_ref, dv_ref = outs
    everything = source[...]
    for across, (w, slot, saved) in enumerate(parts):
        q_ref, k_ref, v_ref, probs_ref, n2_ref, r2_ref, slope_ref = saved
        rows = pl.ds(slot * WIN, WIN)
        here = pl.ds(across * WIN, WIN)
        grad = mm(one_hot(back_ref[pl.ds(w * WIN, WIN), :], everything.shape[0]), everything)
        inner = mm(grad.astype(bf16), down_ref[...]) * slope_ref[rows, :].astype(f32)
        grad = grad + norm_back(
            mm_nt(inner.astype(bf16), up_ref[...]), n2_ref[rows, :].astype(f32), r2_ref[rows, :]
        )
        grad_ref[here, :] = grad
        mix_grad = mm_nt(grad.astype(bf16), proj_ref[...]).astype(bf16)
        dq, dk, dv = attend_back(
            q_ref[rows, :], k_ref[rows, :], v_ref[rows, :], mix_grad,
            probs_ref, slot * 6 * WIN, score_ref, across == 1,
        )
        dq_ref[here, :] = dq.astype(bf16)
        dk_ref[here, :] = dk.astype(bf16)
        dv_ref[here, :] = dv.astype(bf16)


def first_band_kernel(dlon_ref, dloc_ref, back_ref, *refs):
    *refs, source = refs
    source[0:112] = tokens_of(dlon_ref, 112)
    source[112:448] = dloc_ref[...]
    parts = ((0, 0, refs[:7]), (1, 0, refs[7:14]))
    band_back(parts, source, back_ref, refs[14:17], refs[17:21], refs[21])


def second_band_kernel(
    dlon_ref, dloc_ref, dlat_ref, ddiag_ref, back_ref, first_ref, *refs
):
    *refs, source, score_ref, rows_ref = refs
    source[0:112] = tokens_of(dlon_ref, 112)
    source[112:448] = dloc_ref[...]
    source[448:560] = tokens_of(dlat_ref, 112)
    source[560:608] = tokens_of(ddiag_ref, 48)
    half = 6 * WIN
    score_ref[pl.ds(0, half), :] = first_ref[...]
    parts = ((2, 1, refs[:7]), (3, 2, refs[:7]))
    band_back(
        parts, source, back_ref, refs[7:10], refs[10:14], score_ref.at[pl.ds(half, half)]
    )
    refs[14][...] = table_grad(score_ref, rows_ref)


def qkv_back_kernel(*refs):
    bands, refs = (refs[:4], refs[4:8]), refs[8:]
    norms = (refs[0:2], refs[2:4])
    qkv_ref, clon_ref, clat_ref, cdiag_ref = refs[4:8]
    res_ref, slon_ref, slat_ref, sdiag_ref = refs[8:]
    w_qkv = qkv_ref[...]
    windows = []
    for w in range(4):
        grad_ref, dq_ref, dk_ref, dv_ref = bands[w // 2]
        rows = pl.ds(w * WIN, WIN)
        here = pl.ds(w % 2 * WIN, WIN)
        normed_grad = (
            mm_nt(dq_ref[here, :], w_qkv[:, 0:192])
            + mm_nt(dk_ref[here, :], w_qkv[:, 192:384])
            + mm_nt(dv_ref[here, :], w_qkv[:, 384:576])
        )
        n1_ref, r1_ref = norms[min(w, 1)]
        slot = pl.ds(max(w - 1, 0) * WIN, WIN)
        result = grad_ref[here, :] + norm_back(
            normed_grad, n1_ref[slot, :].astype(f32), r1_ref[slot, :]
        )
        res_ref[rows, :] = result.astype(bf16)
        windows.append(result)
    clon, clat, cdiag = [
        ref[...].astype(f32)[:QUAD] for ref in (clon_ref, clat_ref, cdiag_ref)
    ]
    slon_ref[...] = dense([quadrant(windows, q, 0) for q in range(1, 4)], 112, clon)
    slat_ref[...] = dense([quadrant(windows, 0, q) for q in range(1, 4)], 112, clat)
    sdiag_ref[...] = dense([quadrant(windows, 0, 0)], 48, cdiag)


def last_kernel(
    res_ref, lon_ref, lat_ref, diag_ref, leave_ref, cloc_ref, result_ref,
    tokens_ref, coarse_ref, source, coarse_source,
):
    source[0:576] = res_ref[...]
    source[576:688] = tokens_of(lon_ref, 112)
    source[688:800] = tokens_of(lat_ref, 112)
    source[800:848] = tokens_of(diag_ref, 48)
    everything = source[...]
    for w in range(4):
        rows = pl.ds(w * WIN, WIN)
        tokens_ref[rows, :] = mm(one_hot(leave_ref[rows, :], 848), everything).astype(bf16)
    coarse_source[0:48] = cloc_ref[...]
    coarse_source[48:96] = pack([coarse_of(lon_ref, 112)], 48)
    coarse_source[96:144] = pack([coarse_of(lat_ref, 112)], 48)
    coarse_source[144:192] = pack([coarse_of(diag_ref, 48)], 48)
    moved = mm(one_hot(result_ref[...], 192), coarse_source[...])
    for z in range(2):
        for row in range(6):
            start = z * 72 + row * 12
            coarse_ref[z, row] = moved[start : start + 12].astype(bf16)


def run(kernel, outs, scratch, weight, inputs):
    shapes = [jax.ShapeDtypeStruct(shape, kind) for shape, kind in outs]
    size = sum(math.prod(s.shape) * s.dtype.itemsize for s in shapes)
    size += sum(x.size * x.dtype.itemsize for x in inputs)
    return pl.pallas_call(
        kernel,
        out_shape=shapes,
        scratch_shapes=[pltpu.VMEM(shape, kind) for shape, kind in scratch],
        compiler_params=pltpu.CompilerParams(vmem_limit_bytes=VMEM),
        cost_estimate=pl.CostEstimate(
            flops=weight * 1_000_000_000, bytes_accessed=size, transcendentals=0
        ),
    )(*inputs)


def move(value, lon_steps, lat_steps):
    lon, lat = lax.axis_size("lon"), lax.axis_size("lat")
    if lat_steps == 0:
        pairs = [(s, (s + lon_steps) % lon) for s in range(lon)]
        return lax.ppermute(value, "lon", pairs)
    if lon_steps == 0:
        pairs = [(s, (s + lat_steps) % lat) for s in range(lat)]
        return lax.ppermute(value, "lat", pairs)
    pairs = [
        (b * lat + a, (b + lon_steps) % lon * lat + (a + lat_steps) % lat)
        for b in range(lon)
        for a in range(lat)
    ]
    return lax.ppermute(value, ("lon", "lat"), pairs)


def send(pieces, steps):
    on_lon, on_lat, on_both = pieces
    return move(on_lon, steps, 0), move(on_lat, 0, steps), move(on_both, steps, steps)


def swap(value, step):
    count = lax.axis_size("lon")
    return lax.ppermute(value, "lon", [(s, s ^ step) for s in range(count)])


def add(mine, other):
    return (mine.astype(f32) + other.astype(f32)).astype(bf16)


def lon_steps():
    return [1 << bit for bit in range(lax.axis_size("lon").bit_length() - 1)]


def body(
    tokens, mask_ids, fine_qkv, fine_proj, fine_up, fine_down, fine_bias, reduce_weight,
    coarse_qkv, coarse_proj, coarse_up, coarse_down, coarse_bias, out_grad,
):
    lat_index = lax.axis_index("lat")
    fine_down = fine_down.T
    flat = tokens.reshape(576, 192)
    column = lambda index: jnp.asarray(index).reshape(-1, 1)
    tok = ((576, 192), bf16)
    edges = [((176, 128), bf16), ((176, 128), bf16), ((80, 128), bf16)]
    wide_edges = [((288, 128), bf16), ((288, 128), bf16), ((192, 128), bf16)]
    quad = ((48, 384), bf16)
    scores = ((12 * WIN, WIN), f32)
    table_rows = ((12, 192, WIN), bf16)
    held = ((12, 2, 12, 16, WIN), bf16)

    first = send(run(edge_kernel, edges, [], 1, (flat,)), 1)
    (fine_table,) = run(
        bias_kernel, [scores], [held], 2,
        (fine_bias.transpose(1, 0, 2),),
    )

    row = lax.broadcasted_iota(jnp.int32, mask_ids.shape, 1) + lat_index * mask_ids.shape[1]
    labels = mask_ids * 2 + jnp.where(row < 3, 1, 0)
    labels = labels.reshape(2, 2, 2, 3, 2, 2, 6)
    labels = labels.transpose(1, 4, 2, 5, 0, 3, 6).reshape(4, WIN)
    fine_mask = jnp.where(labels[:, :, None] == labels[:, None, :], 0.0, -1e30).astype(f32)
    low_half = jnp.arange(WIN) < WIN // 2
    coarse_mask = jnp.where(
        (low_half[:, None] == low_half[None, :]) | (lat_index != 0), 0.0, -1e30
    ).astype(f32)

    def saved_shapes(windows):
        rows = windows * WIN
        part = ((rows, 192), bf16)
        scale = ((rows, 1), f32)
        probs = ((6 * rows, WIN), bf16)
        return [part] * 3 + [probs, part, scale, part, scale, ((rows, 768), bf16)]

    inputs = (
        flat, *first, column(ARRIVE), fine_table, fine_mask,
        fine_qkv, fine_proj, fine_up, fine_down,
    )
    gathered = [((848, 192), bf16)]
    outer = run(
        fine_edge_kernel,
        wide_edges + [quad, ((3 * WIN, 192), bf16)] + saved_shapes(3),
        gathered, 6, (out_grad.transpose(1, 2, 0, 3), *inputs),
    )
    arrived = send(outer[:3], 1)
    flat_after, _ = lax.optimization_barrier((flat, outer[4]))
    inner = run(
        fine_inner_kernel,
        [((WIN, 192), bf16)] + saved_shapes(1),
        gathered, 2, (flat_after, *inputs[1:]),
    )
    late_table, _ = lax.optimization_barrier((coarse_bias.transpose(1, 0, 2), outer[4]))
    (coarse_table,) = run(
        bias_kernel, [scores], [held], 2, (late_table,)
    )
    coarse = run(
        coarse_kernel,
        [quad] * 4 + edges + [((336, 192), bf16), scores],
        [((848, 192), bf16), ((12 * WIN, WIN), bf16), ((576, 192), bf16)],
        9,
        (
            inner[0], outer[4], *arrived, column(MERGE), column(SPLIT), coarse_table, coarse_mask, outer[3],
            reduce_weight, coarse_qkv, coarse_proj, coarse_up, coarse_down,
        ),
    )
    c00, c01, c10, c11 = coarse[:4]
    arrived = send(coarse[4:7], -1)
    dlon, dlat, ddiag = arrived
    dlat, scored = lax.optimization_barrier((dlat, coarse[8]))
    (coarse_grad,) = run(
        coarse_table_kernel, [((24, 6 * ENTRIES), bf16)], [table_rows], 2,
        (scored,),
    )
    steps = lon_steps()
    other = swap(coarse_grad, steps[1])
    half_tok = ((288, 192), bf16)
    half_outs = [((288, 192), f32)] + [half_tok] * 3
    q, k, v, probs, n1, r1, n2, r2, slope = outer[5:]
    outer_saved = (q, k, v, probs, n2, r2, slope)
    q, k, v, probs, n1_inner, r1_inner, n2, r2, slope = inner[1:]
    inner_saved = (q, k, v, probs, n2, r2, slope)
    weights = (fine_proj, fine_up, fine_down)
    *first_half, first_scores = run(
        first_band_kernel,
        half_outs + [((6 * WIN, WIN), f32)],
        [((448, 192), bf16)],
        4,
        (dlon, coarse[7], column(BACK), *inner_saved, *outer_saved, *weights),
    )
    first_scores, other = lax.optimization_barrier((first_scores, other))
    coarse_grad = add(coarse_grad, other)
    other = swap(coarse_grad, steps[-1])
    *second_half, fine_grad = run(
        second_band_kernel,
        half_outs + [((24, 6 * ENTRIES), bf16)],
        [((608, 192), bf16), scores, table_rows],
        5,
        (
            dlon, coarse[7], dlat, ddiag, column(BACK), first_scores,
            *outer_saved, *weights,
        ),
    )
    second_half[0], other = lax.optimization_barrier((second_half[0], other))
    coarse_grad = add(coarse_grad, other)
    for step in (*steps[2:-1], steps[0]):
        coarse_sums = (coarse_grad, swap(coarse_grad, step))
        coarse_grad = add(*coarse_sums)
    other = swap(fine_grad, steps[0])
    fine_back = list(run(
        qkv_back_kernel, [tok] + wide_edges, [], 2,
        (*first_half, *second_half, n1_inner, r1_inner, n1, r1, fine_qkv, c10, c01, c00),
    ))
    alon, alat, adiag = send(fine_back[1:4], -1)
    alat, adiag, other = lax.optimization_barrier((alat, adiag, other))
    fine_grad = add(fine_grad, other)
    for step in steps[1:]:
        fine_sums = (fine_grad, swap(fine_grad, step))
        fine_grad = add(*fine_sums)
    d_tokens, coarse_result = run(
        last_kernel,
        [tok, ((2, 6, 12, 384), bf16)],
        [((848, 192), bf16), ((192, 384), bf16)],
        1,
        (fine_back[0], alon, alat, adiag, column(LEAVE), c11, column(RESULT)),
    )
    fine_out, coarse_out = run(
        table_sum_kernel,
        [((HEADS_F, 2, 12 * ENTRIES), f32), ((HEADS_C, 1, 12 * ENTRIES), f32)],
        [], 1, (*fine_sums, *coarse_sums),
    )
    return (
        coarse_result,
        d_tokens.reshape(tokens.shape),
        fine_out.transpose(1, 0, 2),
        coarse_out.transpose(1, 0, 2),
    )


def solution(mesh):
    grid = P(None, "lat", "lon", None)
    bands = P("lat", None, None)
    in_specs = (
        grid, P(None, "lat", "lon"), P(), P(), P(), P(), bands,
        P(), P(), P(), P(), P(), bands, grid,
    )
    out_specs = (grid, grid, bands, bands)
    return jax.shard_map(body, mesh=mesh, in_specs=in_specs, out_specs=out_specs, check_vma=False)
```

```python
import math

import jax
import jax.numpy as jnp
import numpy as np
from jax import lax
from jax.experimental import pallas as pl
from jax.experimental.pallas import tpu as pltpu
from jax.sharding import PartitionSpec as P

HEADS_F = 6
HEADS_C = 12
HEAD = 32
WIN = 144
QUAD = 36
SPAN = 23
ENTRIES = 276
LOG2E = math.log2(math.e)
VMEM = 20 * 1024 * 1024
f32 = jnp.float32
bf16 = jnp.bfloat16


def spot(z, i, j):
    quadrant = (i % 6) // 3 * 2 + (j % 12) // 6
    return quadrant * QUAD + z * 18 + i % 3 * 6 + j % 6


def fine_spot(z, i, j):
    return (i // 6 * 2 + j // 12) * WIN + spot(z, i, j)


def in_quad(z, i, j):
    return z * 18 + i % 3 * 6 + j % 6


def index_maps():
    arrive = np.zeros(576, np.int32)
    merge = np.zeros(576, np.int32)
    split = np.full(608, -1, np.int32)
    back = np.zeros(576, np.int32)
    leave = np.zeros(576, np.int32)
    for z in range(2):
        for i in range(12):
            for j in range(24):
                here = fine_spot(z, i, j)
                if i >= 3 and j >= 6:
                    arrive[here] = z * 288 + (i - 3) * 24 + j - 6
                    came = fine_spot(z, i - 3, j - 6)
                elif i >= 3:
                    came = 576 + (i - 3) // 3 * QUAD + in_quad(z, i, j)
                elif j >= 6:
                    came = 688 + (j - 6) // 6 * QUAD + in_quad(z, i, j)
                else:
                    came = 800 + in_quad(z, i, j)
                if came >= 576:
                    arrive[here] = came
                part = (i % 2 + j % 2 * 2) * WIN + spot(z, i // 2, j // 2)
                merge[part] = came
                if i >= 3 and j >= 6:
                    slot = 112 + z * 162 + (i - 3) * 18 + j - 6
                    back[fine_spot(z, i - 3, j - 6)] = slot
                elif i >= 3:
                    slot = z * 54 + (i - 3) * 6 + j
                    back[fine_spot(z, i - 3, j + 18)] = slot
                elif j >= 6:
                    slot = 448 + z * 54 + i * 18 + j - 6
                    back[fine_spot(z, i + 9, j - 6)] = slot
                else:
                    slot = 560 + z * 18 + i * 6 + j
                    back[fine_spot(z, i + 9, j + 18)] = slot
                split[slot] = part
                natural = z * 288 + i * 24 + j
                if i < 9 and j < 18:
                    leave[natural] = fine_spot(z, i + 3, j + 6)
                elif i < 9:
                    leave[natural] = 576 + i // 3 * QUAD + in_quad(z, i, j)
                elif j < 18:
                    leave[natural] = 688 + j // 6 * QUAD + in_quad(z, i, j)
                else:
                    leave[natural] = 800 + in_quad(z, i, j)
    result = np.zeros(WIN, np.int32)
    for z in range(2):
        for i in range(6):
            for j in range(12):
                result[z * 72 + i * 12 + j] = (i // 3 * 2 + j // 6) * 48 + in_quad(z, i, j)
    return arrive, merge, split, back, leave, result


ARRIVE, MERGE, SPLIT, BACK, LEAVE, RESULT = index_maps()


def places(shape, axis):
    t = lax.broadcasted_iota(jnp.int32, shape, axis)
    quad = (t * 57) >> 11
    t = t - quad * QUAD
    level = (t * 57) >> 10
    t = t - level * 18
    row = (t * 43) >> 8
    return level * 6 + (quad >> 1) * 3 + row, t - row * 6 + (quad & 1) * 6


def entry_base(shape, axis):
    row, column = places(shape, axis)
    return row * SPAN + 11 - column


def row_slot(shape, axis):
    row, column = places(shape, axis)
    return column * 16 + row


def one_hot(column, width):
    spots = lax.broadcasted_iota(jnp.int32, (column.shape[0], width), 1)
    return jnp.where(spots == column, 1.0, 0.0).astype(bf16)


def mm(left, right):
    return jnp.dot(left, right, preferred_element_type=f32)


def mm_nt(left, right):
    return lax.dot_general(left, right, (((1,), (1,)), ((), ())), preferred_element_type=f32)


def mm_tn(left, right):
    return lax.dot_general(left, right, (((0,), (0,)), ((), ())), preferred_element_type=f32)


def norm(values):
    centred = values - jnp.mean(values, axis=-1, keepdims=True)
    scale = lax.rsqrt(jnp.mean(centred * centred, axis=-1, keepdims=True) + 1e-5)
    return centred * scale, scale


def norm_back(grad, normed, scale):
    along = jnp.mean(grad * normed, axis=-1, keepdims=True)
    return (grad - jnp.mean(grad, axis=-1, keepdims=True) - normed * along) * scale


def gelu_pair(x):
    u = jnp.abs(x) * math.sqrt(0.5)
    t = 1.0 / (1.0 + 0.3275911 * u)
    e = jnp.exp(-u * u)
    poly = 1.421413741 + t * (-1.453152027 + t * 1.061405429)
    tail = 0.5 * (t * (0.254829592 + t * (-0.284496736 + t * poly))) * e
    below = jnp.where(x >= 0, 1.0 - tail, tail)
    return x * below, below + x * (e * (1.0 / math.sqrt(2 * math.pi)))


def groups(channels):
    return [(start, min(start + 128, channels)) for start in range(0, channels, 128)]


def head_lanes(rows, width):
    return lax.broadcasted_iota(jnp.int32, (rows, width), 1) // HEAD


def stack_heads(part):
    lanes = head_lanes(part.shape[0], part.shape[1])
    count = part.shape[1] // HEAD
    zero = jnp.zeros_like(part)
    return jnp.concatenate([jnp.where(lanes == h, part, zero) for h in range(count)], axis=0)


def pick_heads(stacked):
    width = stacked.shape[1]
    lanes = head_lanes(WIN, width)
    total = stacked[:WIN]
    for h in range(1, width // HEAD):
        total = jnp.where(lanes == h, stacked[h * WIN : (h + 1) * WIN], total)
    return total


def attend(queries, keys, values, bias_ref, bias_row, mask, probs_ref, probs_row):
    mixed = []
    for start, stop in groups(queries.shape[1]):
        count = (stop - start) // HEAD
        scores = mm_nt(stack_heads(queries[:, start:stop]), keys[:, start:stop])
        row = start // HEAD * WIN
        for h in range(count):
            here = row + h * WIN
            logits = (
                scores[h * WIN : (h + 1) * WIN] * (HEAD**-0.5 * LOG2E)
                + bias_ref[pl.ds(bias_row + here, WIN), :]
                + mask
            )
            raised = jnp.exp2(logits - jnp.max(logits, axis=-1, keepdims=True))
            probs = raised * (1.0 / jnp.sum(raised, axis=-1, keepdims=True))
            probs_ref[pl.ds(probs_row + here, WIN), :] = probs.astype(bf16)
        stacked = mm(probs_ref[pl.ds(probs_row + row, count * WIN), :], values[:, start:stop])
        mixed.append(pick_heads(stacked))
    return jnp.concatenate(mixed, axis=1)


def attend_back(queries, keys, values, mix_grad, probs_ref, probs_row, score_ref, add):
    query_grad, key_grad, value_grad = [], [], []
    for start, stop in groups(queries.shape[1]):
        count = (stop - start) // HEAD
        row = start // HEAD * WIN
        probs_all = probs_ref[pl.ds(probs_row + row, count * WIN), :]
        grads = stack_heads(mix_grad[:, start:stop])
        value_grad.append(mm_tn(probs_all, grads))
        probs_grad = mm_nt(grads, values[:, start:stop])
        pieces = []
        for h in range(count):
            probs = probs_all[h * WIN : (h + 1) * WIN].astype(f32)
            grad = probs_grad[h * WIN : (h + 1) * WIN]
            weighted = grad * probs
            score_grad = weighted - probs * jnp.sum(weighted, axis=-1, keepdims=True)
            place = pl.ds(row + h * WIN, WIN)
            if add:
                score_ref[place, :] += score_grad
            else:
                score_ref[place, :] = score_grad
            pieces.append(score_grad.astype(bf16))
        score_all = jnp.concatenate(pieces, axis=0)
        query_grad.append(pick_heads(mm(score_all, keys[:, start:stop])))
        key_grad.append(mm_tn(score_all, stack_heads(queries[:, start:stop])))
    scale = HEAD**-0.5
    return (
        jnp.concatenate(query_grad, axis=1) * scale,
        jnp.concatenate(key_grad, axis=1) * scale,
        jnp.concatenate(value_grad, axis=1),
    )


def swap_rows():
    row = lax.broadcasted_iota(jnp.int32, (192, 192), 0)
    return jnp.where(
        lax.broadcasted_iota(jnp.int32, (192, 192), 1) == row % 16 * 16 + row // 16, 1.0, 0.0
    ).astype(bf16)


def table_grad(score_ref, rows_ref):
    regroup = jnp.where(
        lax.broadcasted_iota(jnp.int32, (192, WIN), 0) == row_slot((1, WIN), 1), 1.0, 0.0
    ).astype(bf16)
    for h in range(12):
        moved = mm(regroup, score_ref[pl.ds(h * WIN, WIN), :].astype(bf16)).astype(bf16)
        rows_ref[:, pl.ds(h * 16, 16), :] = moved.reshape(12, 16, WIN)
    total = jnp.zeros((192, ENTRIES), f32)
    base = entry_base((WIN, 1), 0)
    for column in range(12):
        total += mm(rows_ref[column], one_hot(base + column, ENTRIES))
    swapped = mm(swap_rows(), total.astype(bf16))
    halves = [
        jnp.concatenate([swapped[a * 16 : a * 16 + 12] for a in range(start, start + 6)], axis=1)
        for start in (0, 6)
    ]
    return jnp.concatenate(halves, axis=0).astype(bf16)


def pack(pieces, rows):
    count = sum(piece.shape[0] for piece in pieces)
    if rows > count:
        pieces = pieces + [jnp.zeros((rows - count, pieces[0].shape[1]), f32)]
    return jnp.concatenate(pieces, axis=0).astype(bf16)


def dense(pieces, rows, coarse=None):
    count = sum(piece.shape[0] for piece in pieces)
    if rows > count:
        pieces = pieces + [jnp.zeros((rows - count, 192), f32)]
    tokens = jnp.concatenate(pieces, axis=0)
    half = rows // 2
    side = jnp.concatenate([tokens[0:half, 128:192], tokens[half:rows, 128:192]], axis=1)
    filler = jnp.zeros((4, 128), f32)
    out = [tokens[:, 0:128], side]
    if coarse is None:
        out += [filler, filler]
    else:
        for start in range(0, 384, 128):
            out += [coarse[:, start : start + 128], filler]
    return jnp.concatenate(out, axis=0).astype(bf16)


def tokens_of(ref, rows):
    values = ref[...].astype(f32)
    side = values[rows : rows + rows // 2]
    side = jnp.concatenate([side[:, 0:64], side[:, 64:128]], axis=0)
    return jnp.concatenate([values[0:rows], side], axis=1).astype(bf16)


def coarse_of(ref, rows):
    values = ref[...].astype(f32)
    starts = [rows + rows // 2 + 40 * part for part in range(3)]
    return jnp.concatenate([values[start : start + QUAD] for start in starts], axis=1)


def quadrant(windows, qi, qj):
    part = (qi % 2 * 2 + qj % 2) * QUAD
    return windows[qi // 2 * 2 + qj // 2][part : part + QUAD]


def edge_kernel(tokens_ref, slon_ref, slat_ref, sdiag_ref):
    tokens = tokens_ref[...].astype(f32)

    def token_quadrant(row, start):
        pieces = []
        for z in range(2):
            for i in range(row, row + 3):
                place = (z * 12 + i) * 24 + start
                pieces.append(tokens[place : place + 6])
        return jnp.concatenate(pieces, axis=0)

    slon_ref[...] = dense([token_quadrant(q * 3, 18) for q in range(3)], 112)
    slat_ref[...] = dense([token_quadrant(9, q * 6) for q in range(3)], 112)
    sdiag_ref[...] = dense([token_quadrant(9, 18)], 48)


def expand(table_ref, out_ref, held):
    table = jnp.concatenate([table_ref[:, b, :] for b in range(table_ref.shape[1])], axis=0)
    filler = jnp.zeros((4, ENTRIES), f32)
    pieces = []
    for a in range(12):
        pieces += [table[:, a * ENTRIES : (a + 1) * ENTRIES], filler]
    table = jnp.concatenate(pieces, axis=0)
    high = table.astype(bf16)
    low = (table - high.astype(f32)).astype(bf16)
    swap = swap_rows()
    table = jnp.concatenate(
        [mm(swap, high).astype(bf16), mm(swap, low).astype(bf16)], axis=0
    )
    entry = lax.broadcasted_iota(jnp.int32, (ENTRIES, WIN), 0)
    base = entry_base((1, WIN), 1)
    for column in range(12):
        picker = jnp.where(entry == base + column, 1.0, 0.0).astype(bf16)
        picked = mm(table, picker).astype(bf16)
        held[:, 0, column] = picked[0:192].reshape(12, 16, WIN)
        held[:, 1, column] = picked[192:384].reshape(12, 16, WIN)
    spots = lax.broadcasted_iota(jnp.int32, (WIN, 384), 1)
    spots = jnp.where(spots >= 192, spots - 192, spots)
    twice = jnp.where(spots == row_slot((WIN, 1), 0), 1.0, 0.0).astype(bf16)
    for h in range(12):
        out_ref[pl.ds(h * WIN, WIN), :] = mm(twice, held[h].reshape(384, WIN)) * LOG2E


def bias_kernel(table_ref, out_ref, held):
    expand(table_ref, out_ref, held)


def coarse_table_kernel(score_ref, table_ref, rows_ref):
    table_ref[...] = table_grad(score_ref, rows_ref)


def table_sum_kernel(fine_kept, fine_other, coarse_kept, coarse_other, fine_ref, coarse_ref):
    for kept, other, out_ref in (
        (fine_kept, fine_other, fine_ref),
        (coarse_kept, coarse_other, coarse_ref),
    ):
        total = kept[...].astype(f32) + other[...].astype(f32)
        total = jnp.concatenate([total[0:12], total[12:24]], axis=1)
        heads = out_ref.shape[0]
        for b in range(out_ref.shape[1]):
            out_ref[:, b, :] = total[b * heads : (b + 1) * heads]


def fine_windows(numbers, refs):
    tokens_ref, lon_ref, lat_ref, diag_ref, arrive_ref, bias_ref, mask_ref = refs[:7]
    qkv_ref, proj_ref, up_ref, down_ref, res_ref = refs[7:12]
    q_ref, k_ref, v_ref, probs_ref, n1_ref, r1_ref, n2_ref, r2_ref, slope_ref = refs[12:21]
    source = refs[21]
    source[0:576] = tokens_ref[...]
    source[576:688] = tokens_of(lon_ref, 112)
    source[688:800] = tokens_of(lat_ref, 112)
    source[800:848] = tokens_of(diag_ref, 48)
    everything = source[...]
    w_qkv = qkv_ref[...]
    bases = []
    for slot, w in enumerate(numbers):
        rows = pl.ds(slot * WIN, WIN)
        base = mm(one_hot(arrive_ref[pl.ds(w * WIN, WIN), :], 848), everything)
        normed, scale = norm(base)
        normed = normed.astype(bf16)
        n1_ref[rows, :] = normed
        r1_ref[rows, :] = scale
        q_ref[rows, :] = mm(normed, w_qkv[:, 0:192]).astype(bf16)
        k_ref[rows, :] = mm(normed, w_qkv[:, 192:384]).astype(bf16)
        v_ref[rows, :] = mm(normed, w_qkv[:, 384:576]).astype(bf16)
        bases.append(base)
    windows = {}
    for slot, w in enumerate(numbers):
        rows = pl.ds(slot * WIN, WIN)
        mixture = attend(
            q_ref[rows, :], k_ref[rows, :], v_ref[rows, :],
            bias_ref, w // 2 * 6 * WIN, mask_ref[w], probs_ref, slot * 6 * WIN,
        ).astype(bf16)
        first = bases[slot] + mm(mixture, proj_ref[...])
        renormed, scale = norm(first)
        renormed = renormed.astype(bf16)
        n2_ref[rows, :] = renormed
        r2_ref[rows, :] = scale
        active, slope = gelu_pair(mm(renormed, up_ref[...]))
        slope_ref[rows, :] = slope.astype(bf16)
        result = first + mm_nt(active.astype(bf16), down_ref[...])
        res_ref[rows, :] = result.astype(bf16)
        windows[w] = result
    return windows


def fine_edge_kernel(grad_ref, *refs):
    slon_ref, slat_ref, sdiag_ref, gloc_ref = refs[11:15]
    windows = fine_windows((1, 2, 3), refs[:11] + refs[15:])
    grads = grad_ref[...].astype(f32)

    def grad_quadrant(hi, hj):
        pieces = [
            grads[hi * 3 + row, hj * 6 : hj * 6 + 6, z] for z in range(2) for row in range(3)
        ]
        return jnp.concatenate(pieces, axis=0)

    slon_ref[...] = dense([quadrant(windows, q, 3) for q in range(3)], 112, grad_quadrant(0, 1))
    slat_ref[...] = dense([quadrant(windows, 3, q) for q in range(3)], 112, grad_quadrant(1, 0))
    sdiag_ref[...] = dense([quadrant(windows, 3, 3)], 48, grad_quadrant(1, 1))
    gloc_ref[...] = pack([grad_quadrant(0, 0)], 48)


def fine_inner_kernel(*refs):
    fine_windows((0,), refs)


def coarse_kernel(
    inner_ref, res_ref, lon_ref, lat_ref, diag_ref, merge_ref, split_ref, bias_ref, mask_ref,
    gloc_ref,
    reduce_ref, qkv_ref, proj_ref, up_ref, down_ref,
    c0, c1, c2, c3, dlon_ref, dlat_ref, ddiag_ref, dloc_ref, score_ref,
    source, probs_ref, parts_ref,
):
    source[0:144] = inner_ref[...]
    source[144:576] = res_ref[...]
    source[576:688] = tokens_of(lon_ref, 112)
    source[688:800] = tokens_of(lat_ref, 112)
    source[800:848] = tokens_of(diag_ref, 48)
    everything = source[...]
    parts = [mm(one_hot(merge_ref[pl.ds(k * WIN, WIN), :], 848), everything) for k in range(4)]
    mean = sum(jnp.sum(part, axis=-1, keepdims=True) for part in parts) * (1.0 / 768)
    parts = [part - mean for part in parts]
    square = sum(jnp.sum(part * part, axis=-1, keepdims=True) for part in parts)
    merge_scale = lax.rsqrt(square * (1.0 / 768) + 1e-5)
    parts = [(part * merge_scale).astype(bf16) for part in parts]
    base = sum(mm(parts[k], reduce_ref[k * 192 : (k + 1) * 192]) for k in range(4))
    base = base.astype(bf16).astype(f32)
    normed, scale1 = norm(base)
    normed = normed.astype(bf16)
    queries = mm(normed, qkv_ref[:, 0:384]).astype(bf16)
    keys = mm(normed, qkv_ref[:, 384:768]).astype(bf16)
    values = mm(normed, qkv_ref[:, 768:1152]).astype(bf16)
    mixture = attend(queries, keys, values, bias_ref, 0, mask_ref[...], probs_ref, 0).astype(bf16)
    first = base + mm(mixture, proj_ref[...])
    renormed, scale2 = norm(first)
    renormed = renormed.astype(bf16)
    active, slope = gelu_pair(mm(renormed, up_ref[...]))
    result = first + mm(active.astype(bf16), down_ref[...])
    for index, out in enumerate((c0, c1, c2, c3)):
        out[...] = pack([result[index * QUAD : (index + 1) * QUAD]], 48)

    grad = jnp.concatenate(
        [
            coarse_of(diag_ref, 48),
            coarse_of(lat_ref, 112),
            coarse_of(lon_ref, 112),
            gloc_ref[...].astype(f32)[:QUAD],
        ],
        axis=0,
    )
    inner = mm_nt(grad.astype(bf16), down_ref[...]) * slope
    grad = grad + norm_back(mm_nt(inner.astype(bf16), up_ref[...]), renormed.astype(f32), scale2)
    mix_grad = mm_nt(grad.astype(bf16), proj_ref[...]).astype(bf16)
    dq, dk, dv = attend_back(queries, keys, values, mix_grad, probs_ref, 0, score_ref, False)
    normed_grad = (
        mm_nt(dq.astype(bf16), qkv_ref[:, 0:384])
        + mm_nt(dk.astype(bf16), qkv_ref[:, 384:768])
        + mm_nt(dv.astype(bf16), qkv_ref[:, 768:1152])
    )
    grad = grad + norm_back(normed_grad, normed.astype(f32), scale1)
    grad = grad.astype(bf16)
    grads = [mm_nt(grad, reduce_ref[k * 192 : (k + 1) * 192]) for k in range(4)]
    mean = sum(jnp.sum(g, axis=-1, keepdims=True) for g in grads) * (1.0 / 768)
    along = sum(
        jnp.sum(g * p.astype(f32), axis=-1, keepdims=True) for g, p in zip(grads, parts)
    ) * (1.0 / 768)
    for k in range(4):
        part = (grads[k] - mean - parts[k].astype(f32) * along) * merge_scale
        parts_ref[pl.ds(k * WIN, WIN), :] = part.astype(bf16)
    everything = parts_ref[...]
    moved = mm(one_hot(split_ref[...], 576), everything)
    dlon_ref[...] = dense([moved[0:112]], 112)
    dloc_ref[...] = moved[112:448].astype(bf16)
    dlat_ref[...] = dense([moved[448:560]], 112)
    ddiag_ref[...] = dense([moved[560:608]], 48)


def band_back(parts, source, back_ref, weights, outs, score_ref):
    proj_ref, up_ref, down_ref = weights
    grad_ref, dq_ref, dk_ref, dv_ref = outs
    everything = source[...]
    for across, (w, slot, saved) in enumerate(parts):
        q_ref, k_ref, v_ref, probs_ref, n2_ref, r2_ref, slope_ref = saved
        rows = pl.ds(slot * WIN, WIN)
        here = pl.ds(across * WIN, WIN)
        grad = mm(one_hot(back_ref[pl.ds(w * WIN, WIN), :], everything.shape[0]), everything)
        inner = mm(grad.astype(bf16), down_ref[...]) * slope_ref[rows, :].astype(f32)
        grad = grad + norm_back(
            mm_nt(inner.astype(bf16), up_ref[...]), n2_ref[rows, :].astype(f32), r2_ref[rows, :]
        )
        grad_ref[here, :] = grad
        mix_grad = mm_nt(grad.astype(bf16), proj_ref[...]).astype(bf16)
        dq, dk, dv = attend_back(
            q_ref[rows, :], k_ref[rows, :], v_ref[rows, :], mix_grad,
            probs_ref, slot * 6 * WIN, score_ref, across == 1,
        )
        dq_ref[here, :] = dq.astype(bf16)
        dk_ref[here, :] = dk.astype(bf16)
        dv_ref[here, :] = dv.astype(bf16)


def first_band_kernel(dlon_ref, dloc_ref, back_ref, *refs):
    *refs, source = refs
    source[0:112] = tokens_of(dlon_ref, 112)
    source[112:448] = dloc_ref[...]
    parts = ((0, 0, refs[:7]), (1, 0, refs[7:14]))
    band_back(parts, source, back_ref, refs[14:17], refs[17:21], refs[21])


def second_band_kernel(
    dlon_ref, dloc_ref, dlat_ref, ddiag_ref, back_ref, first_ref, *refs
):
    *refs, source, score_ref, rows_ref = refs
    source[0:112] = tokens_of(dlon_ref, 112)
    source[112:448] = dloc_ref[...]
    source[448:560] = tokens_of(dlat_ref, 112)
    source[560:608] = tokens_of(ddiag_ref, 48)
    half = 6 * WIN
    score_ref[pl.ds(0, half), :] = first_ref[...]
    parts = ((2, 1, refs[:7]), (3, 2, refs[:7]))
    band_back(
        parts, source, back_ref, refs[7:10], refs[10:14], score_ref.at[pl.ds(half, half)]
    )
    refs[14][...] = table_grad(score_ref, rows_ref)


def qkv_back_kernel(*refs):
    bands, refs = (refs[:4], refs[4:8]), refs[8:]
    norms = (refs[0:2], refs[2:4])
    qkv_ref, clon_ref, clat_ref, cdiag_ref = refs[4:8]
    res_ref, slon_ref, slat_ref, sdiag_ref = refs[8:]
    w_qkv = qkv_ref[...]
    windows = []
    for w in range(4):
        grad_ref, dq_ref, dk_ref, dv_ref = bands[w // 2]
        rows = pl.ds(w * WIN, WIN)
        here = pl.ds(w % 2 * WIN, WIN)
        normed_grad = (
            mm_nt(dq_ref[here, :], w_qkv[:, 0:192])
            + mm_nt(dk_ref[here, :], w_qkv[:, 192:384])
            + mm_nt(dv_ref[here, :], w_qkv[:, 384:576])
        )
        n1_ref, r1_ref = norms[min(w, 1)]
        slot = pl.ds(max(w - 1, 0) * WIN, WIN)
        result = grad_ref[here, :] + norm_back(
            normed_grad, n1_ref[slot, :].astype(f32), r1_ref[slot, :]
        )
        res_ref[rows, :] = result.astype(bf16)
        windows.append(result)
    clon, clat, cdiag = [
        ref[...].astype(f32)[:QUAD] for ref in (clon_ref, clat_ref, cdiag_ref)
    ]
    slon_ref[...] = dense([quadrant(windows, q, 0) for q in range(1, 4)], 112, clon)
    slat_ref[...] = dense([quadrant(windows, 0, q) for q in range(1, 4)], 112, clat)
    sdiag_ref[...] = dense([quadrant(windows, 0, 0)], 48, cdiag)


def last_kernel(
    res_ref, lon_ref, lat_ref, diag_ref, leave_ref, cloc_ref, result_ref,
    tokens_ref, coarse_ref, source, coarse_source,
):
    source[0:576] = res_ref[...]
    source[576:688] = tokens_of(lon_ref, 112)
    source[688:800] = tokens_of(lat_ref, 112)
    source[800:848] = tokens_of(diag_ref, 48)
    everything = source[...]
    for w in range(4):
        rows = pl.ds(w * WIN, WIN)
        tokens_ref[rows, :] = mm(one_hot(leave_ref[rows, :], 848), everything).astype(bf16)
    coarse_source[0:48] = cloc_ref[...]
    coarse_source[48:96] = pack([coarse_of(lon_ref, 112)], 48)
    coarse_source[96:144] = pack([coarse_of(lat_ref, 112)], 48)
    coarse_source[144:192] = pack([coarse_of(diag_ref, 48)], 48)
    moved = mm(one_hot(result_ref[...], 192), coarse_source[...])
    for z in range(2):
        for row in range(6):
            start = z * 72 + row * 12
            coarse_ref[z, row] = moved[start : start + 12].astype(bf16)


def run(kernel, outs, scratch, weight, inputs):
    shapes = [jax.ShapeDtypeStruct(shape, kind) for shape, kind in outs]
    size = sum(math.prod(s.shape) * s.dtype.itemsize for s in shapes)
    size += sum(x.size * x.dtype.itemsize for x in inputs)
    return pl.pallas_call(
        kernel,
        out_shape=shapes,
        scratch_shapes=[pltpu.VMEM(shape, kind) for shape, kind in scratch],
        compiler_params=pltpu.CompilerParams(vmem_limit_bytes=VMEM),
        cost_estimate=pl.CostEstimate(
            flops=weight * 1_000_000_000, bytes_accessed=size, transcendentals=0
        ),
    )(*inputs)


def move(value, lon_steps, lat_steps):
    lon, lat = lax.axis_size("lon"), lax.axis_size("lat")
    if lat_steps == 0:
        pairs = [(s, (s + lon_steps) % lon) for s in range(lon)]
        return lax.ppermute(value, "lon", pairs)
    if lon_steps == 0:
        pairs = [(s, (s + lat_steps) % lat) for s in range(lat)]
        return lax.ppermute(value, "lat", pairs)
    pairs = [
        (b * lat + a, (b + lon_steps) % lon * lat + (a + lat_steps) % lat)
        for b in range(lon)
        for a in range(lat)
    ]
    return lax.ppermute(value, ("lon", "lat"), pairs)


def send(pieces, steps):
    on_lon, on_lat, on_both = pieces
    return move(on_lon, steps, 0), move(on_lat, 0, steps), move(on_both, steps, steps)


def swap(value, step):
    count = lax.axis_size("lon")
    return lax.ppermute(value, "lon", [(s, s ^ step) for s in range(count)])


def add(mine, other):
    return (mine.astype(f32) + other.astype(f32)).astype(bf16)


def lon_steps():
    return [1 << bit for bit in range(lax.axis_size("lon").bit_length() - 1)]


def body(
    tokens, mask_ids, fine_qkv, fine_proj, fine_up, fine_down, fine_bias, reduce_weight,
    coarse_qkv, coarse_proj, coarse_up, coarse_down, coarse_bias, out_grad,
):
    lat_index = lax.axis_index("lat")
    fine_down = fine_down.T
    flat = tokens.reshape(576, 192)
    column = lambda index: jnp.asarray(index).reshape(-1, 1)
    tok = ((576, 192), bf16)
    edges = [((176, 128), bf16), ((176, 128), bf16), ((80, 128), bf16)]
    wide_edges = [((288, 128), bf16), ((288, 128), bf16), ((192, 128), bf16)]
    quad = ((48, 384), bf16)
    scores = ((12 * WIN, WIN), f32)
    table_rows = ((12, 192, WIN), bf16)
    held = ((12, 2, 12, 16, WIN), bf16)

    first = send(run(edge_kernel, edges, [], 1, (flat,)), 1)
    (fine_table,) = run(
        bias_kernel, [scores], [held], 2,
        (fine_bias.transpose(1, 0, 2),),
    )

    row = lax.broadcasted_iota(jnp.int32, mask_ids.shape, 1) + lat_index * mask_ids.shape[1]
    labels = mask_ids * 2 + jnp.where(row < 3, 1, 0)
    labels = labels.reshape(2, 2, 2, 3, 2, 2, 6)
    labels = labels.transpose(1, 4, 2, 5, 0, 3, 6).reshape(4, WIN)
    fine_mask = jnp.where(labels[:, :, None] == labels[:, None, :], 0.0, -1e30).astype(f32)
    low_half = jnp.arange(WIN) < WIN // 2
    coarse_mask = jnp.where(
        (low_half[:, None] == low_half[None, :]) | (lat_index != 0), 0.0, -1e30
    ).astype(f32)

    def saved_shapes(windows):
        rows = windows * WIN
        part = ((rows, 192), bf16)
        scale = ((rows, 1), f32)
        probs = ((6 * rows, WIN), bf16)
        return [part] * 3 + [probs, part, scale, part, scale, ((rows, 768), bf16)]

    inputs = (
        flat, *first, column(ARRIVE), fine_table, fine_mask,
        fine_qkv, fine_proj, fine_up, fine_down,
    )
    gathered = [((848, 192), bf16)]
    outer = run(
        fine_edge_kernel,
        wide_edges + [quad, ((3 * WIN, 192), bf16)] + saved_shapes(3),
        gathered, 6, (out_grad.transpose(1, 2, 0, 3), *inputs),
    )
    arrived = send(outer[:3], 1)
    flat_after, _ = lax.optimization_barrier((flat, outer[4]))
    inner = run(
        fine_inner_kernel,
        [((WIN, 192), bf16)] + saved_shapes(1),
        gathered, 2, (flat_after, *inputs[1:]),
    )
    late_table, _ = lax.optimization_barrier((coarse_bias.transpose(1, 0, 2), outer[4]))
    (coarse_table,) = run(
        bias_kernel, [scores], [held], 2, (late_table,)
    )
    coarse = run(
        coarse_kernel,
        [quad] * 4 + edges + [((336, 192), bf16), scores],
        [((848, 192), bf16), ((12 * WIN, WIN), bf16), ((576, 192), bf16)],
        9,
        (
            inner[0], outer[4], *arrived, column(MERGE), column(SPLIT), coarse_table, coarse_mask, outer[3],
            reduce_weight, coarse_qkv, coarse_proj, coarse_up, coarse_down,
        ),
    )
    c00, c01, c10, c11 = coarse[:4]
    arrived = send(coarse[4:7], -1)
    dlon, dlat, ddiag = arrived
    dlat, scored = lax.optimization_barrier((dlat, coarse[8]))
    (coarse_grad,) = run(
        coarse_table_kernel, [((24, 6 * ENTRIES), bf16)], [table_rows], 2,
        (scored,),
    )
    steps = lon_steps()
    other = swap(coarse_grad, steps[1])
    half_tok = ((288, 192), bf16)
    half_outs = [((288, 192), f32)] + [half_tok] * 3
    q, k, v, probs, n1, r1, n2, r2, slope = outer[5:]
    outer_saved = (q, k, v, probs, n2, r2, slope)
    q, k, v, probs, n1_inner, r1_inner, n2, r2, slope = inner[1:]
    inner_saved = (q, k, v, probs, n2, r2, slope)
    weights = (fine_proj, fine_up, fine_down)
    *first_half, first_scores = run(
        first_band_kernel,
        half_outs + [((6 * WIN, WIN), f32)],
        [((448, 192), bf16)],
        4,
        (dlon, coarse[7], column(BACK), *inner_saved, *outer_saved, *weights),
    )
    first_scores, other = lax.optimization_barrier((first_scores, other))
    coarse_grad = add(coarse_grad, other)
    other = swap(coarse_grad, steps[-1])
    *second_half, fine_grad = run(
        second_band_kernel,
        half_outs + [((24, 6 * ENTRIES), bf16)],
        [((608, 192), bf16), scores, table_rows],
        5,
        (
            dlon, coarse[7], dlat, ddiag, column(BACK), first_scores,
            *outer_saved, *weights,
        ),
    )
    second_half[0], other = lax.optimization_barrier((second_half[0], other))
    coarse_grad = add(coarse_grad, other)
    for step in (*steps[2:-1], steps[0]):
        coarse_sums = (coarse_grad, swap(coarse_grad, step))
        coarse_grad = add(*coarse_sums)
    other = swap(fine_grad, steps[0])
    fine_back = list(run(
        qkv_back_kernel, [tok] + wide_edges, [], 2,
        (*first_half, *second_half, n1_inner, r1_inner, n1, r1, fine_qkv, c10, c01, c00),
    ))
    alon, alat, adiag = send(fine_back[1:4], -1)
    alat, other = lax.optimization_barrier((alat, other))
    fine_grad = add(fine_grad, other)
    for step in steps[1:]:
        fine_sums = (fine_grad, swap(fine_grad, step))
        fine_grad = add(*fine_sums)
    d_tokens, coarse_result = run(
        last_kernel,
        [tok, ((2, 6, 12, 384), bf16)],
        [((848, 192), bf16), ((192, 384), bf16)],
        1,
        (fine_back[0], alon, alat, adiag, column(LEAVE), c11, column(RESULT)),
    )
    fine_out, coarse_out = run(
        table_sum_kernel,
        [((HEADS_F, 2, 12 * ENTRIES), f32), ((HEADS_C, 1, 12 * ENTRIES), f32)],
        [], 1, (*fine_sums, *coarse_sums),
    )
    return (
        coarse_result,
        d_tokens.reshape(tokens.shape),
        fine_out.transpose(1, 0, 2),
        coarse_out.transpose(1, 0, 2),
    )


def solution(mesh):
    grid = P(None, "lat", "lon", None)
    bands = P("lat", None, None)
    in_specs = (
        grid, P(None, "lat", "lon"), P(), P(), P(), P(), bands,
        P(), P(), P(), P(), P(), bands, grid,
    )
    out_specs = (grid, grid, bands, bands)
    return jax.shard_map(body, mesh=mesh, in_specs=in_specs, out_specs=out_specs, check_vma=False)
```

```python
import math

import jax
import jax.numpy as jnp
import numpy as np
from jax import lax
from jax.experimental import pallas as pl
from jax.experimental.pallas import tpu as pltpu
from jax.sharding import PartitionSpec as P

HEADS_F = 6
HEADS_C = 12
HEAD = 32
WIN = 144
QUAD = 36
SPAN = 23
ENTRIES = 276
LOG2E = math.log2(math.e)
VMEM = 20 * 1024 * 1024
f32 = jnp.float32
bf16 = jnp.bfloat16


def spot(z, i, j):
    quadrant = (i % 6) // 3 * 2 + (j % 12) // 6
    return quadrant * QUAD + z * 18 + i % 3 * 6 + j % 6


def fine_spot(z, i, j):
    return (i // 6 * 2 + j // 12) * WIN + spot(z, i, j)


def in_quad(z, i, j):
    return z * 18 + i % 3 * 6 + j % 6


def index_maps():
    arrive = np.zeros(576, np.int32)
    merge = np.zeros(576, np.int32)
    split = np.full(608, -1, np.int32)
    back = np.zeros(576, np.int32)
    leave = np.zeros(576, np.int32)
    for z in range(2):
        for i in range(12):
            for j in range(24):
                here = fine_spot(z, i, j)
                if i >= 3 and j >= 6:
                    arrive[here] = z * 288 + (i - 3) * 24 + j - 6
                    came = fine_spot(z, i - 3, j - 6)
                elif i >= 3:
                    came = 576 + (i - 3) // 3 * QUAD + in_quad(z, i, j)
                elif j >= 6:
                    came = 688 + (j - 6) // 6 * QUAD + in_quad(z, i, j)
                else:
                    came = 800 + in_quad(z, i, j)
                if came >= 576:
                    arrive[here] = came
                part = (i % 2 + j % 2 * 2) * WIN + spot(z, i // 2, j // 2)
                merge[part] = came
                if i >= 3 and j >= 6:
                    slot = 112 + z * 162 + (i - 3) * 18 + j - 6
                    back[fine_spot(z, i - 3, j - 6)] = slot
                elif i >= 3:
                    slot = z * 54 + (i - 3) * 6 + j
                    back[fine_spot(z, i - 3, j + 18)] = slot
                elif j >= 6:
                    slot = 448 + z * 54 + i * 18 + j - 6
                    back[fine_spot(z, i + 9, j - 6)] = slot
                else:
                    slot = 560 + z * 18 + i * 6 + j
                    back[fine_spot(z, i + 9, j + 18)] = slot
                split[slot] = part
                natural = z * 288 + i * 24 + j
                if i < 9 and j < 18:
                    leave[natural] = fine_spot(z, i + 3, j + 6)
                elif i < 9:
                    leave[natural] = 576 + i // 3 * QUAD + in_quad(z, i, j)
                elif j < 18:
                    leave[natural] = 688 + j // 6 * QUAD + in_quad(z, i, j)
                else:
                    leave[natural] = 800 + in_quad(z, i, j)
    result = np.zeros(WIN, np.int32)
    for z in range(2):
        for i in range(6):
            for j in range(12):
                result[z * 72 + i * 12 + j] = (i // 3 * 2 + j // 6) * 48 + in_quad(z, i, j)
    return arrive, merge, split, back, leave, result


ARRIVE, MERGE, SPLIT, BACK, LEAVE, RESULT = index_maps()


def places(shape, axis):
    t = lax.broadcasted_iota(jnp.int32, shape, axis)
    quad = (t * 57) >> 11
    t = t - quad * QUAD
    level = (t * 57) >> 10
    t = t - level * 18
    row = (t * 43) >> 8
    return level * 6 + (quad >> 1) * 3 + row, t - row * 6 + (quad & 1) * 6


def entry_base(shape, axis):
    row, column = places(shape, axis)
    return row * SPAN + 11 - column


def row_slot(shape, axis):
    row, column = places(shape, axis)
    return column * 16 + row


def one_hot(column, width):
    spots = lax.broadcasted_iota(jnp.int32, (column.shape[0], width), 1)
    return jnp.where(spots == column, 1.0, 0.0).astype(bf16)


def mm(left, right):
    return jnp.dot(left, right, preferred_element_type=f32)


def mm_nt(left, right):
    return lax.dot_general(left, right, (((1,), (1,)), ((), ())), preferred_element_type=f32)


def mm_tn(left, right):
    return lax.dot_general(left, right, (((0,), (0,)), ((), ())), preferred_element_type=f32)


def norm(values):
    centred = values - jnp.mean(values, axis=-1, keepdims=True)
    scale = lax.rsqrt(jnp.mean(centred * centred, axis=-1, keepdims=True) + 1e-5)
    return centred * scale, scale


def norm_back(grad, normed, scale):
    along = jnp.mean(grad * normed, axis=-1, keepdims=True)
    return (grad - jnp.mean(grad, axis=-1, keepdims=True) - normed * along) * scale


def gelu_pair(x):
    u = jnp.abs(x) * math.sqrt(0.5)
    t = 1.0 / (1.0 + 0.3275911 * u)
    e = jnp.exp(-u * u)
    poly = 1.421413741 + t * (-1.453152027 + t * 1.061405429)
    tail = 0.5 * (t * (0.254829592 + t * (-0.284496736 + t * poly))) * e
    below = jnp.where(x >= 0, 1.0 - tail, tail)
    return x * below, below + x * (e * (1.0 / math.sqrt(2 * math.pi)))


def groups(channels):
    return [(start, min(start + 128, channels)) for start in range(0, channels, 128)]


def head_lanes(rows, width):
    return lax.broadcasted_iota(jnp.int32, (rows, width), 1) // HEAD


def stack_heads(part):
    lanes = head_lanes(part.shape[0], part.shape[1])
    count = part.shape[1] // HEAD
    zero = jnp.zeros_like(part)
    return jnp.concatenate([jnp.where(lanes == h, part, zero) for h in range(count)], axis=0)


def pick_heads(stacked):
    width = stacked.shape[1]
    lanes = head_lanes(WIN, width)
    total = stacked[:WIN]
    for h in range(1, width // HEAD):
        total = jnp.where(lanes == h, stacked[h * WIN : (h + 1) * WIN], total)
    return total


def attend(queries, keys, values, bias_ref, bias_row, mask, probs_ref, probs_row):
    mixed = []
    for start, stop in groups(queries.shape[1]):
        count = (stop - start) // HEAD
        scores = mm_nt(stack_heads(queries[:, start:stop]), keys[:, start:stop])
        row = start // HEAD * WIN
        for h in range(count):
            here = row + h * WIN
            logits = (
                scores[h * WIN : (h + 1) * WIN] * (HEAD**-0.5 * LOG2E)
                + bias_ref[pl.ds(bias_row + here, WIN), :]
                + mask
            )
            raised = jnp.exp2(logits - jnp.max(logits, axis=-1, keepdims=True))
            probs = raised * (1.0 / jnp.sum(raised, axis=-1, keepdims=True))
            probs_ref[pl.ds(probs_row + here, WIN), :] = probs.astype(bf16)
        stacked = mm(probs_ref[pl.ds(probs_row + row, count * WIN), :], values[:, start:stop])
        mixed.append(pick_heads(stacked))
    return jnp.concatenate(mixed, axis=1)


def attend_back(queries, keys, values, mix_grad, probs_ref, probs_row, score_ref, add):
    query_grad, key_grad, value_grad = [], [], []
    for start, stop in groups(queries.shape[1]):
        count = (stop - start) // HEAD
        row = start // HEAD * WIN
        probs_all = probs_ref[pl.ds(probs_row + row, count * WIN), :]
        grads = stack_heads(mix_grad[:, start:stop])
        value_grad.append(mm_tn(probs_all, grads))
        probs_grad = mm_nt(grads, values[:, start:stop])
        pieces = []
        for h in range(count):
            probs = probs_all[h * WIN : (h + 1) * WIN].astype(f32)
            grad = probs_grad[h * WIN : (h + 1) * WIN]
            weighted = grad * probs
            score_grad = weighted - probs * jnp.sum(weighted, axis=-1, keepdims=True)
            place = pl.ds(row + h * WIN, WIN)
            if add:
                score_ref[place, :] += score_grad
            else:
                score_ref[place, :] = score_grad
            pieces.append(score_grad.astype(bf16))
        score_all = jnp.concatenate(pieces, axis=0)
        query_grad.append(pick_heads(mm(score_all, keys[:, start:stop])))
        key_grad.append(mm_tn(score_all, stack_heads(queries[:, start:stop])))
    scale = HEAD**-0.5
    return (
        jnp.concatenate(query_grad, axis=1) * scale,
        jnp.concatenate(key_grad, axis=1) * scale,
        jnp.concatenate(value_grad, axis=1),
    )


def swap_rows():
    row = lax.broadcasted_iota(jnp.int32, (192, 192), 0)
    return jnp.where(
        lax.broadcasted_iota(jnp.int32, (192, 192), 1) == row % 16 * 16 + row // 16, 1.0, 0.0
    ).astype(bf16)


def table_grad(score_ref, rows_ref):
    regroup = jnp.where(
        lax.broadcasted_iota(jnp.int32, (192, WIN), 0) == row_slot((1, WIN), 1), 1.0, 0.0
    ).astype(bf16)
    for h in range(12):
        moved = mm(regroup, score_ref[pl.ds(h * WIN, WIN), :].astype(bf16)).astype(bf16)
        rows_ref[:, pl.ds(h * 16, 16), :] = moved.reshape(12, 16, WIN)
    total = jnp.zeros((192, ENTRIES), f32)
    base = entry_base((WIN, 1), 0)
    for column in range(12):
        total += mm(rows_ref[column], one_hot(base + column, ENTRIES))
    swapped = mm(swap_rows(), total.astype(bf16))
    halves = [
        jnp.concatenate([swapped[a * 16 : a * 16 + 12] for a in range(start, start + 6)], axis=1)
        for start in (0, 6)
    ]
    return jnp.concatenate(halves, axis=0).astype(bf16)


def pack(pieces, rows):
    count = sum(piece.shape[0] for piece in pieces)
    if rows > count:
        pieces = pieces + [jnp.zeros((rows - count, pieces[0].shape[1]), f32)]
    return jnp.concatenate(pieces, axis=0).astype(bf16)


def dense(pieces, rows, coarse=None):
    count = sum(piece.shape[0] for piece in pieces)
    if rows > count:
        pieces = pieces + [jnp.zeros((rows - count, 192), f32)]
    tokens = jnp.concatenate(pieces, axis=0)
    half = rows // 2
    side = jnp.concatenate([tokens[0:half, 128:192], tokens[half:rows, 128:192]], axis=1)
    filler = jnp.zeros((4, 128), f32)
    out = [tokens[:, 0:128], side]
    if coarse is None:
        out += [filler, filler]
    else:
        for start in range(0, 384, 128):
            out += [coarse[:, start : start + 128], filler]
    return jnp.concatenate(out, axis=0).astype(bf16)


def tokens_of(ref, rows):
    values = ref[...].astype(f32)
    side = values[rows : rows + rows // 2]
    side = jnp.concatenate([side[:, 0:64], side[:, 64:128]], axis=0)
    return jnp.concatenate([values[0:rows], side], axis=1).astype(bf16)


def coarse_of(ref, rows):
    values = ref[...].astype(f32)
    starts = [rows + rows // 2 + 40 * part for part in range(3)]
    return jnp.concatenate([values[start : start + QUAD] for start in starts], axis=1)


def quadrant(windows, qi, qj):
    part = (qi % 2 * 2 + qj % 2) * QUAD
    return windows[qi // 2 * 2 + qj // 2][part : part + QUAD]


def edge_kernel(tokens_ref, slon_ref, slat_ref, sdiag_ref):
    tokens = tokens_ref[...].astype(f32)

    def token_quadrant(row, start):
        pieces = []
        for z in range(2):
            for i in range(row, row + 3):
                place = (z * 12 + i) * 24 + start
                pieces.append(tokens[place : place + 6])
        return jnp.concatenate(pieces, axis=0)

    slon_ref[...] = dense([token_quadrant(q * 3, 18) for q in range(3)], 112)
    slat_ref[...] = dense([token_quadrant(9, q * 6) for q in range(3)], 112)
    sdiag_ref[...] = dense([token_quadrant(9, 18)], 48)


def expand(table_ref, out_ref, held):
    table = jnp.concatenate([table_ref[:, b, :] for b in range(table_ref.shape[1])], axis=0)
    filler = jnp.zeros((4, ENTRIES), f32)
    pieces = []
    for a in range(12):
        pieces += [table[:, a * ENTRIES : (a + 1) * ENTRIES], filler]
    table = jnp.concatenate(pieces, axis=0)
    high = table.astype(bf16)
    low = (table - high.astype(f32)).astype(bf16)
    swap = swap_rows()
    table = jnp.concatenate(
        [mm(swap, high).astype(bf16), mm(swap, low).astype(bf16)], axis=0
    )
    entry = lax.broadcasted_iota(jnp.int32, (ENTRIES, WIN), 0)
    base = entry_base((1, WIN), 1)
    for column in range(12):
        picker = jnp.where(entry == base + column, 1.0, 0.0).astype(bf16)
        picked = mm(table, picker).astype(bf16)
        held[:, 0, column] = picked[0:192].reshape(12, 16, WIN)
        held[:, 1, column] = picked[192:384].reshape(12, 16, WIN)
    spots = lax.broadcasted_iota(jnp.int32, (WIN, 384), 1)
    spots = jnp.where(spots >= 192, spots - 192, spots)
    twice = jnp.where(spots == row_slot((WIN, 1), 0), 1.0, 0.0).astype(bf16)
    for h in range(12):
        out_ref[pl.ds(h * WIN, WIN), :] = mm(twice, held[h].reshape(384, WIN)) * LOG2E


def bias_kernel(table_ref, out_ref, held):
    expand(table_ref, out_ref, held)


def coarse_table_kernel(score_ref, table_ref, rows_ref):
    table_ref[...] = table_grad(score_ref, rows_ref)


def table_sum_kernel(fine_kept, fine_other, coarse_kept, coarse_other, fine_ref, coarse_ref):
    for kept, other, out_ref in (
        (fine_kept, fine_other, fine_ref),
        (coarse_kept, coarse_other, coarse_ref),
    ):
        total = kept[...].astype(f32) + other[...].astype(f32)
        total = jnp.concatenate([total[0:12], total[12:24]], axis=1)
        heads = out_ref.shape[0]
        for b in range(out_ref.shape[1]):
            out_ref[:, b, :] = total[b * heads : (b + 1) * heads]


def fine_windows(numbers, refs):
    tokens_ref, lon_ref, lat_ref, diag_ref, arrive_ref, bias_ref, mask_ref = refs[:7]
    qkv_ref, proj_ref, up_ref, down_ref, res_ref = refs[7:12]
    q_ref, k_ref, v_ref, probs_ref, n1_ref, r1_ref, n2_ref, r2_ref, slope_ref = refs[12:21]
    source = refs[21]
    source[0:576] = tokens_ref[...]
    source[576:688] = tokens_of(lon_ref, 112)
    source[688:800] = tokens_of(lat_ref, 112)
    source[800:848] = tokens_of(diag_ref, 48)
    everything = source[...]
    w_qkv = qkv_ref[...]
    bases = []
    for slot, w in enumerate(numbers):
        rows = pl.ds(slot * WIN, WIN)
        base = mm(one_hot(arrive_ref[pl.ds(w * WIN, WIN), :], 848), everything)
        normed, scale = norm(base)
        normed = normed.astype(bf16)
        n1_ref[rows, :] = normed
        r1_ref[rows, :] = scale
        q_ref[rows, :] = mm(normed, w_qkv[:, 0:192]).astype(bf16)
        k_ref[rows, :] = mm(normed, w_qkv[:, 192:384]).astype(bf16)
        v_ref[rows, :] = mm(normed, w_qkv[:, 384:576]).astype(bf16)
        bases.append(base)
    windows = {}
    for slot, w in enumerate(numbers):
        rows = pl.ds(slot * WIN, WIN)
        mixture = attend(
            q_ref[rows, :], k_ref[rows, :], v_ref[rows, :],
            bias_ref, w // 2 * 6 * WIN, mask_ref[w], probs_ref, slot * 6 * WIN,
        ).astype(bf16)
        first = bases[slot] + mm(mixture, proj_ref[...])
        renormed, scale = norm(first)
        renormed = renormed.astype(bf16)
        n2_ref[rows, :] = renormed
        r2_ref[rows, :] = scale
        active, slope = gelu_pair(mm(renormed, up_ref[...]))
        slope_ref[rows, :] = slope.astype(bf16)
        result = first + mm_nt(active.astype(bf16), down_ref[...])
        res_ref[rows, :] = result.astype(bf16)
        windows[w] = result
    return windows


def fine_edge_kernel(grad_ref, *refs):
    slon_ref, slat_ref, sdiag_ref, gloc_ref = refs[11:15]
    windows = fine_windows((1, 2, 3), refs[:11] + refs[15:])
    grads = grad_ref[...].astype(f32)

    def grad_quadrant(hi, hj):
        pieces = [
            grads[hi * 3 + row, hj * 6 : hj * 6 + 6, z] for z in range(2) for row in range(3)
        ]
        return jnp.concatenate(pieces, axis=0)

    slon_ref[...] = dense([quadrant(windows, q, 3) for q in range(3)], 112, grad_quadrant(0, 1))
    slat_ref[...] = dense([quadrant(windows, 3, q) for q in range(3)], 112, grad_quadrant(1, 0))
    sdiag_ref[...] = dense([quadrant(windows, 3, 3)], 48, grad_quadrant(1, 1))
    gloc_ref[...] = pack([grad_quadrant(0, 0)], 48)


def fine_inner_kernel(*refs):
    fine_windows((0,), refs)


def coarse_kernel(
    inner_ref, res_ref, lon_ref, lat_ref, diag_ref, merge_ref, split_ref, bias_ref, mask_ref,
    gloc_ref,
    reduce_ref, qkv_ref, proj_ref, up_ref, down_ref,
    c0, c1, c2, c3, dlon_ref, dlat_ref, ddiag_ref, dloc_ref, score_ref,
    source, probs_ref, parts_ref,
):
    source[0:144] = inner_ref[...]
    source[144:576] = res_ref[...]
    source[576:688] = tokens_of(lon_ref, 112)
    source[688:800] = tokens_of(lat_ref, 112)
    source[800:848] = tokens_of(diag_ref, 48)
    everything = source[...]
    parts = [mm(one_hot(merge_ref[pl.ds(k * WIN, WIN), :], 848), everything) for k in range(4)]
    mean = sum(jnp.sum(part, axis=-1, keepdims=True) for part in parts) * (1.0 / 768)
    parts = [part - mean for part in parts]
    square = sum(jnp.sum(part * part, axis=-1, keepdims=True) for part in parts)
    merge_scale = lax.rsqrt(square * (1.0 / 768) + 1e-5)
    parts = [(part * merge_scale).astype(bf16) for part in parts]
    base = sum(mm(parts[k], reduce_ref[k * 192 : (k + 1) * 192]) for k in range(4))
    base = base.astype(bf16).astype(f32)
    normed, scale1 = norm(base)
    normed = normed.astype(bf16)
    queries = mm(normed, qkv_ref[:, 0:384]).astype(bf16)
    keys = mm(normed, qkv_ref[:, 384:768]).astype(bf16)
    values = mm(normed, qkv_ref[:, 768:1152]).astype(bf16)
    mixture = attend(queries, keys, values, bias_ref, 0, mask_ref[...], probs_ref, 0).astype(bf16)
    first = base + mm(mixture, proj_ref[...])
    renormed, scale2 = norm(first)
    renormed = renormed.astype(bf16)
    active, slope = gelu_pair(mm(renormed, up_ref[...]))
    result = first + mm(active.astype(bf16), down_ref[...])
    for index, out in enumerate((c0, c1, c2, c3)):
        out[...] = pack([result[index * QUAD : (index + 1) * QUAD]], 48)

    grad = jnp.concatenate(
        [
            coarse_of(diag_ref, 48),
            coarse_of(lat_ref, 112),
            coarse_of(lon_ref, 112),
            gloc_ref[...].astype(f32)[:QUAD],
        ],
        axis=0,
    )
    inner = mm_nt(grad.astype(bf16), down_ref[...]) * slope
    grad = grad + norm_back(mm_nt(inner.astype(bf16), up_ref[...]), renormed.astype(f32), scale2)
    mix_grad = mm_nt(grad.astype(bf16), proj_ref[...]).astype(bf16)
    dq, dk, dv = attend_back(queries, keys, values, mix_grad, probs_ref, 0, score_ref, False)
    normed_grad = (
        mm_nt(dq.astype(bf16), qkv_ref[:, 0:384])
        + mm_nt(dk.astype(bf16), qkv_ref[:, 384:768])
        + mm_nt(dv.astype(bf16), qkv_ref[:, 768:1152])
    )
    grad = grad + norm_back(normed_grad, normed.astype(f32), scale1)
    grad = grad.astype(bf16)
    grads = [mm_nt(grad, reduce_ref[k * 192 : (k + 1) * 192]) for k in range(4)]
    mean = sum(jnp.sum(g, axis=-1, keepdims=True) for g in grads) * (1.0 / 768)
    along = sum(
        jnp.sum(g * p.astype(f32), axis=-1, keepdims=True) for g, p in zip(grads, parts)
    ) * (1.0 / 768)
    for k in range(4):
        part = (grads[k] - mean - parts[k].astype(f32) * along) * merge_scale
        parts_ref[pl.ds(k * WIN, WIN), :] = part.astype(bf16)
    everything = parts_ref[...]
    moved = mm(one_hot(split_ref[...], 576), everything)
    dlon_ref[...] = dense([moved[0:112]], 112)
    dloc_ref[...] = moved[112:448].astype(bf16)
    dlat_ref[...] = dense([moved[448:560]], 112)
    ddiag_ref[...] = dense([moved[560:608]], 48)


def band_back(parts, source, back_ref, weights, outs, score_ref):
    proj_ref, up_ref, down_ref = weights
    grad_ref, dq_ref, dk_ref, dv_ref = outs
    everything = source[...]
    for across, (w, slot, saved) in enumerate(parts):
        q_ref, k_ref, v_ref, probs_ref, n2_ref, r2_ref, slope_ref = saved
        rows = pl.ds(slot * WIN, WIN)
        here = pl.ds(across * WIN, WIN)
        grad = mm(one_hot(back_ref[pl.ds(w * WIN, WIN), :], everything.shape[0]), everything)
        inner = mm(grad.astype(bf16), down_ref[...]) * slope_ref[rows, :].astype(f32)
        grad = grad + norm_back(
            mm_nt(inner.astype(bf16), up_ref[...]), n2_ref[rows, :].astype(f32), r2_ref[rows, :]
        )
        grad_ref[here, :] = grad
        mix_grad = mm_nt(grad.astype(bf16), proj_ref[...]).astype(bf16)
        dq, dk, dv = attend_back(
            q_ref[rows, :], k_ref[rows, :], v_ref[rows, :], mix_grad,
            probs_ref, slot * 6 * WIN, score_ref, across == 1,
        )
        dq_ref[here, :] = dq.astype(bf16)
        dk_ref[here, :] = dk.astype(bf16)
        dv_ref[here, :] = dv.astype(bf16)


def first_band_kernel(dlon_ref, dloc_ref, back_ref, *refs):
    *refs, source = refs
    source[0:112] = tokens_of(dlon_ref, 112)
    source[112:448] = dloc_ref[...]
    parts = ((0, 0, refs[:7]), (1, 0, refs[7:14]))
    band_back(parts, source, back_ref, refs[14:17], refs[17:21], refs[21])


def second_band_kernel(
    dlon_ref, dloc_ref, dlat_ref, ddiag_ref, back_ref, first_ref, *refs
):
    *refs, source, score_ref, rows_ref = refs
    source[0:112] = tokens_of(dlon_ref, 112)
    source[112:448] = dloc_ref[...]
    source[448:560] = tokens_of(dlat_ref, 112)
    source[560:608] = tokens_of(ddiag_ref, 48)
    half = 6 * WIN
    score_ref[pl.ds(0, half), :] = first_ref[...]
    parts = ((2, 1, refs[:7]), (3, 2, refs[:7]))
    band_back(
        parts, source, back_ref, refs[7:10], refs[10:14], score_ref.at[pl.ds(half, half)]
    )
    refs[14][...] = table_grad(score_ref, rows_ref)


def qkv_back_kernel(*refs):
    bands, refs = (refs[:4], refs[4:8]), refs[8:]
    norms = (refs[0:2], refs[2:4])
    qkv_ref, clon_ref, clat_ref, cdiag_ref = refs[4:8]
    res_ref, slon_ref, slat_ref, sdiag_ref = refs[8:]
    w_qkv = qkv_ref[...]
    windows = []
    for w in range(4):
        grad_ref, dq_ref, dk_ref, dv_ref = bands[w // 2]
        rows = pl.ds(w * WIN, WIN)
        here = pl.ds(w % 2 * WIN, WIN)
        normed_grad = (
            mm_nt(dq_ref[here, :], w_qkv[:, 0:192])
            + mm_nt(dk_ref[here, :], w_qkv[:, 192:384])
            + mm_nt(dv_ref[here, :], w_qkv[:, 384:576])
        )
        n1_ref, r1_ref = norms[min(w, 1)]
        slot = pl.ds(max(w - 1, 0) * WIN, WIN)
        result = grad_ref[here, :] + norm_back(
            normed_grad, n1_ref[slot, :].astype(f32), r1_ref[slot, :]
        )
        res_ref[rows, :] = result.astype(bf16)
        windows.append(result)
    clon, clat, cdiag = [
        ref[...].astype(f32)[:QUAD] for ref in (clon_ref, clat_ref, cdiag_ref)
    ]
    slon_ref[...] = dense([quadrant(windows, q, 0) for q in range(1, 4)], 112, clon)
    slat_ref[...] = dense([quadrant(windows, 0, q) for q in range(1, 4)], 112, clat)
    sdiag_ref[...] = dense([quadrant(windows, 0, 0)], 48, cdiag)


def last_kernel(
    res_ref, lon_ref, lat_ref, diag_ref, leave_ref, cloc_ref, result_ref,
    tokens_ref, coarse_ref, source, coarse_source,
):
    source[0:576] = res_ref[...]
    source[576:688] = tokens_of(lon_ref, 112)
    source[688:800] = tokens_of(lat_ref, 112)
    source[800:848] = tokens_of(diag_ref, 48)
    everything = source[...]
    for w in range(4):
        rows = pl.ds(w * WIN, WIN)
        tokens_ref[rows, :] = mm(one_hot(leave_ref[rows, :], 848), everything).astype(bf16)
    coarse_source[0:48] = cloc_ref[...]
    coarse_source[48:96] = pack([coarse_of(lon_ref, 112)], 48)
    coarse_source[96:144] = pack([coarse_of(lat_ref, 112)], 48)
    coarse_source[144:192] = pack([coarse_of(diag_ref, 48)], 48)
    moved = mm(one_hot(result_ref[...], 192), coarse_source[...])
    for z in range(2):
        for row in range(6):
            start = z * 72 + row * 12
            coarse_ref[z, row] = moved[start : start + 12].astype(bf16)


def run(kernel, outs, scratch, weight, inputs):
    shapes = [jax.ShapeDtypeStruct(shape, kind) for shape, kind in outs]
    size = sum(math.prod(s.shape) * s.dtype.itemsize for s in shapes)
    size += sum(x.size * x.dtype.itemsize for x in inputs)
    return pl.pallas_call(
        kernel,
        out_shape=shapes,
        scratch_shapes=[pltpu.VMEM(shape, kind) for shape, kind in scratch],
        compiler_params=pltpu.CompilerParams(vmem_limit_bytes=VMEM),
        cost_estimate=pl.CostEstimate(
            flops=weight * 1_000_000_000, bytes_accessed=size, transcendentals=0
        ),
    )(*inputs)


def move(value, lon_steps, lat_steps):
    lon, lat = lax.axis_size("lon"), lax.axis_size("lat")
    if lat_steps == 0:
        pairs = [(s, (s + lon_steps) % lon) for s in range(lon)]
        return lax.ppermute(value, "lon", pairs)
    if lon_steps == 0:
        pairs = [(s, (s + lat_steps) % lat) for s in range(lat)]
        return lax.ppermute(value, "lat", pairs)
    pairs = [
        (b * lat + a, (b + lon_steps) % lon * lat + (a + lat_steps) % lat)
        for b in range(lon)
        for a in range(lat)
    ]
    return lax.ppermute(value, ("lon", "lat"), pairs)


def send(pieces, steps):
    on_lon, on_lat, on_both = pieces
    return move(on_lon, steps, 0), move(on_lat, 0, steps), move(on_both, steps, steps)


def swap(value, step):
    count = lax.axis_size("lon")
    return lax.ppermute(value, "lon", [(s, s ^ step) for s in range(count)])


def add(mine, other):
    return (mine.astype(f32) + other.astype(f32)).astype(bf16)


def lon_steps():
    return [1 << bit for bit in range(lax.axis_size("lon").bit_length() - 1)]


def body(
    tokens, mask_ids, fine_qkv, fine_proj, fine_up, fine_down, fine_bias, reduce_weight,
    coarse_qkv, coarse_proj, coarse_up, coarse_down, coarse_bias, out_grad,
):
    lat_index = lax.axis_index("lat")
    fine_down = fine_down.T
    flat = tokens.reshape(576, 192)
    column = lambda index: jnp.asarray(index).reshape(-1, 1)
    tok = ((576, 192), bf16)
    edges = [((176, 128), bf16), ((176, 128), bf16), ((80, 128), bf16)]
    wide_edges = [((288, 128), bf16), ((288, 128), bf16), ((192, 128), bf16)]
    quad = ((48, 384), bf16)
    scores = ((12 * WIN, WIN), f32)
    table_rows = ((12, 192, WIN), bf16)
    held = ((12, 2, 12, 16, WIN), bf16)

    first = send(run(edge_kernel, edges, [], 1, (flat,)), 1)
    (fine_table,) = run(
        bias_kernel, [scores], [held], 2,
        (fine_bias.transpose(1, 0, 2),),
    )

    row = lax.broadcasted_iota(jnp.int32, mask_ids.shape, 1) + lat_index * mask_ids.shape[1]
    labels = mask_ids * 2 + jnp.where(row < 3, 1, 0)
    labels = labels.reshape(2, 2, 2, 3, 2, 2, 6)
    labels = labels.transpose(1, 4, 2, 5, 0, 3, 6).reshape(4, WIN)
    fine_mask = jnp.where(labels[:, :, None] == labels[:, None, :], 0.0, -1e30).astype(f32)
    low_half = jnp.arange(WIN) < WIN // 2
    coarse_mask = jnp.where(
        (low_half[:, None] == low_half[None, :]) | (lat_index != 0), 0.0, -1e30
    ).astype(f32)

    def saved_shapes(windows):
        rows = windows * WIN
        part = ((rows, 192), bf16)
        scale = ((rows, 1), f32)
        probs = ((6 * rows, WIN), bf16)
        return [part] * 3 + [probs, part, scale, part, scale, ((rows, 768), bf16)]

    inputs = (
        flat, *first, column(ARRIVE), fine_table, fine_mask,
        fine_qkv, fine_proj, fine_up, fine_down,
    )
    gathered = [((848, 192), bf16)]
    outer = run(
        fine_edge_kernel,
        wide_edges + [quad, ((3 * WIN, 192), bf16)] + saved_shapes(3),
        gathered, 6, (out_grad.transpose(1, 2, 0, 3), *inputs),
    )
    arrived = send(outer[:3], 1)
    flat_after, _ = lax.optimization_barrier((flat, outer[4]))
    inner = run(
        fine_inner_kernel,
        [((WIN, 192), bf16)] + saved_shapes(1),
        gathered, 2, (flat_after, *inputs[1:]),
    )
    late_table, _ = lax.optimization_barrier((coarse_bias.transpose(1, 0, 2), outer[4]))
    (coarse_table,) = run(
        bias_kernel, [scores], [held], 2, (late_table,)
    )
    coarse = run(
        coarse_kernel,
        [quad] * 4 + edges + [((336, 192), bf16), scores],
        [((848, 192), bf16), ((12 * WIN, WIN), bf16), ((576, 192), bf16)],
        9,
        (
            inner[0], outer[4], *arrived, column(MERGE), column(SPLIT), coarse_table, coarse_mask, outer[3],
            reduce_weight, coarse_qkv, coarse_proj, coarse_up, coarse_down,
        ),
    )
    c00, c01, c10, c11 = coarse[:4]
    arrived = send(coarse[4:7], -1)
    dlon, dlat, ddiag = arrived
    dlat, scored = lax.optimization_barrier((dlat, coarse[8]))
    (coarse_grad,) = run(
        coarse_table_kernel, [((24, 6 * ENTRIES), bf16)], [table_rows], 2,
        (scored,),
    )
    steps = lon_steps()
    other = swap(coarse_grad, steps[1])
    half_tok = ((288, 192), bf16)
    half_outs = [((288, 192), f32)] + [half_tok] * 3
    q, k, v, probs, n1, r1, n2, r2, slope = outer[5:]
    outer_saved = (q, k, v, probs, n2, r2, slope)
    q, k, v, probs, n1_inner, r1_inner, n2, r2, slope = inner[1:]
    inner_saved = (q, k, v, probs, n2, r2, slope)
    weights = (fine_proj, fine_up, fine_down)
    *first_half, first_scores = run(
        first_band_kernel,
        half_outs + [((6 * WIN, WIN), f32)],
        [((448, 192), bf16)],
        4,
        (dlon, coarse[7], column(BACK), *inner_saved, *outer_saved, *weights),
    )
    first_scores, other = lax.optimization_barrier((first_scores, other))
    coarse_grad = add(coarse_grad, other)
    other = swap(coarse_grad, steps[-1])
    *second_half, fine_grad = run(
        second_band_kernel,
        half_outs + [((24, 6 * ENTRIES), bf16)],
        [((608, 192), bf16), scores, table_rows],
        5,
        (
            dlon, coarse[7], dlat, ddiag, column(BACK), first_scores,
            *outer_saved, *weights,
        ),
    )
    second_half[0], other = lax.optimization_barrier((second_half[0], other))
    coarse_grad = add(coarse_grad, other)
    other = swap(fine_grad, steps[0])
    fine_back = list(run(
        qkv_back_kernel, [tok] + wide_edges, [], 2,
        (*first_half, *second_half, n1_inner, r1_inner, n1, r1, fine_qkv, c10, c01, c00),
    ))
    alon, alat, adiag = send(fine_back[1:4], -1)
    alat, other = lax.optimization_barrier((alat, other))
    fine_grad = add(fine_grad, other)
    for step in steps[1:]:
        fine_sums = (fine_grad, swap(fine_grad, step))
        fine_grad = add(*fine_sums)
    coarse_grad, ready = lax.optimization_barrier((coarse_grad, fine_sums[0]))
    fine_sums = (ready, fine_sums[1])
    for step in (*steps[2:-1], steps[0]):
        coarse_sums = (coarse_grad, swap(coarse_grad, step))
        coarse_grad = add(*coarse_sums)
    d_tokens, coarse_result = run(
        last_kernel,
        [tok, ((2, 6, 12, 384), bf16)],
        [((848, 192), bf16), ((192, 384), bf16)],
        1,
        (fine_back[0], alon, alat, adiag, column(LEAVE), c11, column(RESULT)),
    )
    fine_out, coarse_out = run(
        table_sum_kernel,
        [((HEADS_F, 2, 12 * ENTRIES), f32), ((HEADS_C, 1, 12 * ENTRIES), f32)],
        [], 1, (*fine_sums, *coarse_sums),
    )
    return (
        coarse_result,
        d_tokens.reshape(tokens.shape),
        fine_out.transpose(1, 0, 2),
        coarse_out.transpose(1, 0, 2),
    )


def solution(mesh):
    grid = P(None, "lat", "lon", None)
    bands = P("lat", None, None)
    in_specs = (
        grid, P(None, "lat", "lon"), P(), P(), P(), P(), bands,
        P(), P(), P(), P(), P(), bands, grid,
    )
    out_specs = (grid, grid, bands, bands)
    return jax.shard_map(body, mesh=mesh, in_specs=in_specs, out_specs=out_specs, check_vma=False)
```
